32 devices in a mesh: section: 2 (over core), dp: 16 (over z, y, x).
Axes of the slice: x: 2, y: 2, z: 4, core: 2. Of those that a mesh axis runs over, the one named last changes fastest.
Arguments:
- images: bfloat16 [256, 2, 147, 128], P('dp'), may hold values from -6 to 6
- proprio: bfloat16 [256, 2, 16, 64], P('dp'), may hold values from -6 to 6
- view_mask: int32 [256, 3], P('dp'), may hold values from 0 to 1, as said below
- embodiment: int32 [256], P('dp'), may hold values from 0 to 3
- ctx_steps: int32 [256], P('dp'), may hold values from 1 to 2
- queries: bfloat16 [4, 16, 128], replicated, may hold values from -5 to 5
- key_weight: bfloat16 [4, 128, 128], replicated, may hold values from -0.5 to 0.5
- value_weight: bfloat16 [4, 128, 128], replicated, may hold values from -0.5 to 0.5
- stem_proj: bfloat16 [128, 128], replicated, may hold values from -1.5 to 1.5
- prop_lift: bfloat16 [4, 64, 128], replicated, may hold values from -0.75 to 0.75
- prop_mix: bfloat16 [4, 128, 128], replicated, may hold values from -0.5 to 0.5
- attn_gain: bfloat16 [128], replicated, may hold values from 0.5 to 1.5
- attn_bias: bfloat16 [128], replicated, may hold values from -2 to 2
- query_key_value_weight: bfloat16 [128, 384], replicated, may hold values from -0.5 to 0.5
- attention_output_weight: bfloat16 [128, 128], replicated, may hold values from -1.5 to 1.5
- mlp_gain: bfloat16 [128], replicated, may hold values from 0.5 to 1.5
- mlp_bias: bfloat16 [128], replicated, may hold values from -2 to 2
- up_weight: bfloat16 [128, 512], replicated, may hold values from -0.5 to 0.5
- up_bias: bfloat16 [512], replicated, may hold values from -2 to 2
- down_weight: bfloat16 [512, 128], replicated, may hold values from -0.25 to 0.25
- down_bias: bfloat16 [128], replicated, may hold values from -2 to 2
- out_grad: bfloat16 [256, 64, 128], P('dp'), may hold values from -6 to 6
Outputs:
- block_out: bfloat16 [256, 64, 128], P('dp', 'section')
- image_grad: bfloat16 [256, 2, 147, 128], P('dp', 'section')
- proprio_grad: bfloat16 [256, 2, 16, 64], P('dp', 'section')
- queries_grad: float32 [4, 16, 128], replicated
- keyw_grad: float32 [4, 128, 128], replicated
- valuew_grad: float32 [4, 128, 128], replicated
- stem_grad: float32 [128, 128], replicated
- lift_grad: float32 [4, 64, 128], replicated
- mixer_grad: float32 [4, 128, 128], replicated
- again_grad: float32 [128], replicated
- abias_grad: float32 [128], replicated
- qkvw_grad: float32 [128, 384], replicated
- aproj_grad: float32 [128, 128], replicated
- mgain_grad: float32 [128], replicated
- mbias_grad: float32 [128], replicated
- upw_grad: float32 [128, 512], replicated
- upb_grad: float32 [512], replicated
- downw_grad: float32 [512, 128], replicated
- downb_grad: float32 [128], replicated
The draws below stay inside these ranges and needn't reach their ends.
Inputs may be any that keep to these rules, and one draw needn't show every extreme that they name: `view_mask`: every sample has one to 3 of its views present.
All inputs are finite; a program needn't handle non-finite values.
Results may differ from the reference program's by a relative error of at most 0.02.
Values may be sent and summed in bfloat16 or wider, within the bound.
No kernel may reach another device: no remote copies, remote signals or barrier semaphores. Data moves between devices by JAX's collectives and lax.ppermute only.
A program may use at most 128 MiB of HBM per device.

```python
import math
import jax
import jax.numpy as jnp
from jax import lax

D = 128
HEADS = 8
HDIM = 16
FFW = 512
QRY = 16
PTOK = 16
PDIM = 64
VIEWS = 3
PATCH = 49
STEPS = 2
EMB = 4
SAMPLES = 256
KEYS = 147
STEP_TOK = 32
CTX = 64


def draw_view_mask(key, part):
    key = jax.random.fold_in(key, 11)
    pattern = jax.random.randint(key, (SAMPLES,), 1, 2 ** VIEWS)
    powers = 2 ** jnp.arange(VIEWS)
    return (pattern[:, None] // powers[None, :] % 2).astype(jnp.int32)


def set_ends(values, key, least, top_value):
    spot = [jax.random.randint(jax.random.fold_in(key, axis), (), 0, length) for axis, length in enumerate(values.shape)]
    widest = values.shape.index(max(values.shape))
    beside = spot[:widest] + [(spot[widest] + 1) % values.shape[widest]] + spot[widest + 1:]
    return values.at[tuple(spot)].set(least).at[tuple(beside)].set(top_value)


def level_of(stream_key, dims, shards, least, top_value):
    level = 1.0
    for axis_at, parts in shards:
        steps = jax.random.uniform(jax.random.fold_in(jax.random.fold_in(stream_key, 6), axis_at), (parts,), jnp.float32, least / len(shards), top_value / len(shards))
        level = level * jnp.repeat(jnp.exp(steps), dims[axis_at] // parts).reshape((-1,) + (1,) * (len(dims) - 1 - axis_at))
    return level


def scatter_about(rng, dims, deviation, bound, shards=(), held_as=jnp.bfloat16):
    entries = jax.random.normal(rng, dims, jnp.float32) * deviation
    if len(shards) > 0:
        entries = level_of(rng, dims, shards, -0.22, 0.18) * entries
    return jnp.clip(entries, min=-bound, max=bound).astype(held_as)


def setup_inputs(seed: int = 0) -> dict:
    key_of = jax.random.split(jax.random.key(seed), 23)
    return {
        "images": scatter_about(key_of[0], (SAMPLES, STEPS, KEYS, D), 1.0, 6.0, ((0, 16),)),
        "proprio": scatter_about(key_of[1], (SAMPLES, STEPS, PTOK, PDIM), 1.0, 6.0, ((0, 16),)),
        "view_mask": draw_view_mask(jax.random.fold_in(key_of[22], 71), 0),
        "embodiment": set_ends(jax.random.randint(key_of[3], (SAMPLES,), 0, EMB), jax.random.fold_in(key_of[3], 1), 0, EMB - 1).astype(jnp.int32),
        "ctx_steps": set_ends(jax.random.randint(key_of[4], (SAMPLES,), 1, STEPS + 1), jax.random.fold_in(key_of[4], 1), 1, STEPS).astype(jnp.int32),
        "queries": scatter_about(key_of[5], (EMB, QRY, D), 1.0, 5.0),
        "key_weight": scatter_about(key_of[6], (EMB, D, D), D ** -0.5, 0.5),
        "value_weight": scatter_about(key_of[7], (EMB, D, D), D ** -0.5, 0.5),
        "stem_proj": scatter_about(key_of[8], (D, D), HDIM ** -0.5, 1.5),
        "prop_lift": scatter_about(key_of[9], (EMB, PDIM, D), PDIM ** -0.5, 0.75),
        "prop_mix": scatter_about(key_of[10], (EMB, D, D), D ** -0.5, 0.5),
        "attn_gain": jnp.clip(1.0 + 0.1 * jax.random.normal(key_of[11], (D,), jnp.float32), 0.5, 1.5).astype(jnp.bfloat16),
        "attn_bias": scatter_about(key_of[12], (D,), 0.3, 2.0),
        "query_key_value_weight": scatter_about(key_of[13], (D, 3 * D), D ** -0.5, 0.5),
        "attention_output_weight": scatter_about(key_of[14], (D, D), HDIM ** -0.5, 1.5),
        "mlp_gain": jnp.clip(1.0 + 0.1 * jax.random.normal(key_of[15], (D,), jnp.float32), 0.5, 1.5).astype(jnp.bfloat16),
        "mlp_bias": scatter_about(key_of[16], (D,), 0.3, 2.0),
        "up_weight": scatter_about(key_of[17], (D, FFW), D ** -0.5, 0.5),
        "up_bias": scatter_about(key_of[18], (FFW,), 0.3, 2.0),
        "down_weight": scatter_about(key_of[19], (FFW, D), FFW ** -0.5, 0.25),
        "down_bias": scatter_about(key_of[20], (D,), 0.3, 2.0),
        "out_grad": scatter_about(key_of[21], (SAMPLES, CTX, D), 1.0, 6.0, ((0, 16),)),
    }


@jax.custom_vjp
def low(v):
    return lax.optimization_barrier(v.astype(jnp.bfloat16)).astype(jnp.float32)

@jax.custom_vjp
def low_back(v):
    return v

def low_keep(v):
    return (low(v), None)

def low_pass(kept, grad):
    return (grad,)

def back_keep(v):
    return (v, None)

def back_low(kept, grad):
    return (low(grad),)
low.defvjp(low_keep, low_pass)
low_back.defvjp(back_keep, back_low)

def matrix_product(form, left, right):
    return jnp.einsum(form, left, right, precision=lax.Precision.HIGHEST)

def both_reduced(values):
    return low_back(low(values))

def layer_norm(values, gain_row, bias_row):
    center = values - lax.optimization_barrier(jnp.mean(values, axis=-1, keepdims=True))
    spread = lax.optimization_barrier(jnp.mean(center * center, axis=-1, keepdims=True))
    return center * lax.rsqrt(spread + 1e-05) * gain_row + bias_row

def masked_softmax(scores, keep):
    scores = jnp.where(keep, scores, -1e+30)
    highest = lax.optimization_barrier(jnp.max(scores, axis=-1, keepdims=True))
    expo = jnp.exp(scores - highest)
    return expo / lax.optimization_barrier(jnp.sum(expo, axis=-1, keepdims=True))

def gelu_exact(values):
    return jax.nn.gelu(values, approximate=False)

def forward(images, proprio, view_mask, embodiment, ctx_steps, params):
    queries, key_weight, value_weight, stem_proj, prop_lift, prop_mix, attn_gain, attn_bias, query_key_value_weight, attention_output_weight, mlp_gain, mlp_bias, up_weight, up_bias, down_weight, down_bias = params
    samples = images.shape[0]
    scale = 1.0 / math.sqrt(HDIM)
    stem_keys = both_reduced(matrix_product('stkd,sde->stke', images, key_weight[embodiment]))
    stem_values = both_reduced(matrix_product('stkd,sde->stke', images, value_weight[embodiment]))
    query_heads = queries[embodiment].reshape(samples, QRY, HEADS, HDIM)
    key_heads = stem_keys.reshape(samples, STEPS, KEYS, HEADS, HDIM)
    value_heads = stem_values.reshape(samples, STEPS, KEYS, HEADS, HDIM)
    stem_raw = low_back(matrix_product('sqhc,stkhc->sthqk', query_heads, key_heads)) * scale
    view_keep = (jnp.repeat(view_mask, PATCH, axis=1) > 0)[:, None, None, None, :]
    stem_prob = both_reduced(masked_softmax(stem_raw, view_keep))
    stem_att = both_reduced(matrix_product('sthqk,stkhc->stqhc', stem_prob, value_heads).reshape(samples, STEPS, QRY, D))
    image_tok = matrix_product('stqd,de->stqe', stem_att, stem_proj)
    lifted = low_back(matrix_product('stjp,spd->stjd', proprio, prop_lift[embodiment]))
    prop_act = both_reduced(gelu_exact(lifted))
    prop_tok = matrix_product('stjd,sde->stje', prop_act, prop_mix[embodiment])
    token_rows = both_reduced(jnp.concatenate([image_tok, prop_tok], axis=2).reshape(samples, CTX, D))
    live = jnp.arange(CTX)[None, :] // STEP_TOK < ctx_steps[:, None]
    normalized_tokens = both_reduced(layer_norm(token_rows, attn_gain, attn_bias))
    query_key_value_full = both_reduced(matrix_product('zqj,jt->zqt', normalized_tokens, query_key_value_weight))
    trunk_q = query_key_value_full[..., :D].reshape(samples, CTX, HEADS, HDIM)
    trunk_k = query_key_value_full[..., D:2 * D].reshape(samples, CTX, HEADS, HDIM)
    trunk_v = query_key_value_full[..., 2 * D:].reshape(samples, CTX, HEADS, HDIM)
    trunk_raw = low_back(matrix_product('sqhc,skhc->shqk', trunk_q, trunk_k)) * scale
    trunk_prob = both_reduced(masked_softmax(trunk_raw, live[:, None, None, :]))
    trunk_attention = both_reduced(matrix_product('shqk,skhc->sqhc', trunk_prob, trunk_v).reshape(samples, CTX, D))
    middle_activation = token_rows + low_back(matrix_product('zqj,jt->zqt', trunk_attention, attention_output_weight))
    normed2 = both_reduced(layer_norm(middle_activation, mlp_gain, mlp_bias))
    up_pre = low_back(matrix_product('snd,df->snf', normed2, up_weight) + up_bias)
    up_act = both_reduced(gelu_exact(up_pre))
    result = middle_activation + matrix_product('snf,fd->snd', up_act, down_weight) + down_bias
    return result * live[..., None].astype(result.dtype)

def reference(images, proprio, view_mask, embodiment, ctx_steps, queries, key_weight, value_weight, stem_proj, prop_lift, prop_mix, attn_gain, attn_bias, query_key_value_weight, attention_output_weight, mlp_gain, mlp_bias, up_weight, up_bias, down_weight, down_bias, out_grad):
    params = tuple((weight_arr.astype(jnp.float32) for weight_arr in (queries, key_weight, value_weight, stem_proj, prop_lift, prop_mix, attn_gain, attn_bias, query_key_value_weight, attention_output_weight, mlp_gain, mlp_bias, up_weight, up_bias, down_weight, down_bias)))
    group = min(64, SAMPLES)
    count = SAMPLES // group

    def split(array):
        return array.reshape((count, group) + array.shape[1:])

    def one_group(totals, pieces):
        image_part, prop_part, mask_part, embod_part, steps_part, grad_part = pieces

        def run(image_float, prop_float, weights):
            return forward(image_float, prop_float, mask_part, embod_part, steps_part, weights)
        result, pullback = jax.vjp(run, image_part.astype(jnp.float32), prop_part.astype(jnp.float32), params)
        image_d, prop_d, weight_d = pullback(grad_part.astype(jnp.float32))
        totals = jax.tree.map(jnp.add, totals, weight_d)
        return (totals, (result.astype(jnp.bfloat16), image_d.astype(jnp.bfloat16), prop_d.astype(jnp.bfloat16)))
    zeros = jax.tree.map(jnp.zeros_like, params)
    totals, outputs = lax.scan(one_group, zeros, (split(images), split(proprio), split(view_mask), split(embodiment), split(ctx_steps), split(out_grad)))
    block_out = outputs[0].reshape((SAMPLES,) + outputs[0].shape[2:])
    image_grad = outputs[1].reshape((SAMPLES,) + outputs[1].shape[2:])
    proprio_grad = outputs[2].reshape((SAMPLES,) + outputs[2].shape[2:])
    return (block_out, image_grad, proprio_grad, totals[0], totals[1], totals[2], totals[3], totals[4], totals[5], totals[6], totals[7], totals[8], totals[9], totals[10], totals[11], totals[12], totals[13], totals[14], totals[15])
```

```python
import functools
import math

import jax
import jax.numpy as jnp
from jax import lax
from jax.experimental import pallas as pl
from jax.experimental.pallas import tpu as pltpu
from jax.sharding import PartitionSpec as P

HEADS = 8
F32 = jnp.float32
BF16 = jnp.bfloat16
CORES = 2
PIECES = 4
EPS = 1e-05
INV_SQRT2 = 1.0 / math.sqrt(2.0)
INV_SQRT2PI = 1.0 / math.sqrt(2.0 * math.pi)
ANY = pl.BlockSpec(memory_space=pl.ANY)
VMEM = pl.BlockSpec(memory_space=pltpu.VMEM)
SMEM = pl.BlockSpec(memory_space=pltpu.SMEM)


def mm(left, right):
    return lax.dot_general(left, right, (((1,), (0,)), ((), ())), preferred_element_type=F32)


def mm_bt(left, right):
    return lax.dot_general(left, right, (((1,), (1,)), ((), ())), preferred_element_type=F32)


def mm_at(left, right):
    return lax.dot_general(left, right, (((0,), (0,)), ((), ())), preferred_element_type=F32)


def layout(width, ffw, emb, queries, feats):
    counts = (
        ("keyw", emb * width),
        ("valuew", emb * width),
        ("mixer", emb * width),
        ("stem", width),
        ("lift", emb * feats),
        ("queries", emb * queries),
        ("qkv", 3 * width),
        ("aproj", width),
        ("up", ffw),
        ("down", ffw),
        ("vectors", 16),
    )
    table, first = {}, 0
    for name, rows in counts:
        table[name] = (first, rows)
        first += rows
    step = CORES * PIECES * 16
    return table, (first + step - 1) // step * step


def cuts(first, rows, piece):
    done = 0
    while done < rows:
        at = first + done
        count = min(rows - done, piece - at % piece)
        yield at // piece, at % piece, done, count
        done += count


def head_mask(rows, per_head, width):
    row = lax.broadcasted_iota(jnp.int32, (rows, width), 0) // per_head
    col = lax.broadcasted_iota(jnp.int32, (rows, width), 1) // (width // HEADS)
    return (row == col).astype(F32)


def spread(rows, mask):
    return jnp.concatenate([rows] * HEADS, axis=0) * mask


def fold(full, mask):
    per = full.shape[0] // HEADS
    return jnp.sum((full * mask).reshape(HEADS, per, full.shape[1]), axis=0)


def gelu_parts(values):
    cdf = 0.5 * (1.0 + lax.erf(values * INV_SQRT2))
    pdf = INV_SQRT2PI * jnp.exp(-0.5 * values * values)
    return values * cdf, cdf + values * pdf


def softmax_rows(scores, bias):
    scores = scores + bias
    expo = jnp.exp(scores - jnp.max(scores, axis=0, keepdims=True))
    return expo / jnp.sum(expo, axis=0, keepdims=True)


def softmax_rows_grad(probs, grad):
    terms = probs * grad
    return terms - probs * jnp.sum(terms, axis=0, keepdims=True)


def norm_parts(values):
    center = values - jnp.mean(values, axis=-1, keepdims=True)
    rstd = lax.rsqrt(jnp.mean(center * center, axis=-1, keepdims=True) + EPS)
    return center * rstd, rstd


def norm_grad(grad, gain, hat, rstd):
    scaled = grad * gain
    first = jnp.mean(scaled, axis=-1, keepdims=True)
    second = jnp.mean(scaled * hat, axis=-1, keepdims=True)
    return rstd * (scaled - first - hat * second)


def compute_kernel(
    dims,
    emb_ref,
    steps_ref,
    views_ref,
    images,
    proprio,
    out_grad,
    queries,
    key_w,
    value_w,
    stem_proj,
    lift_w,
    mix_w,
    again,
    abias,
    qkv_w,
    aproj,
    mgain,
    mbias,
    up_w,
    up_b,
    down_w,
    down_b,
    keep,
    send,
    block_out,
    block_send,
    image_out,
    image_send,
    prop_out,
    prop_send,
    x_s,
    p_s,
    g_s,
    qs_s,
    a_s,
    tok_s,
    xt_s,
    prob_s,
    probb_s,
    ut_s,
    satt_s,
    act_s,
    dact_s,
    hat1_s,
    rstd1_s,
    norm1_s,
    qkv_s,
    tprob_s,
    att_s,
    hat2_s,
    rstd2_s,
    norm2_s,
    up_s,
    dup_s,
    glow_s,
    gpre_s,
    gn2_s,
    gmid_s,
    gatt_s,
    gqkv_s,
    gn1_s,
    gtok_s,
    gsatt_s,
    blk_s,
    img_s,
    prp_s,
    macc_s,
    vacc_s,
    mixacc_s,
    liftacc_s,
    pack_s,
    in_sem,
    out_sem,
):
    n, steps, keys, width, qry, ptok, emb, ffw, table, views = dims
    half_tok = qry + ptok
    ctx = steps * half_tok
    rows = n * ctx
    scale = 1.0 / math.sqrt(width // HEADS)
    piece = pack_s.shape[2]
    sec = lax.axis_index("section")
    base = sec * n

    def put(name, row, value):
        first = table[name][0] + row
        for at, lo, done, count in cuts(first, value.shape[0], piece):
            pack_s[at // PIECES, at % PIECES, lo : lo + count] = value[done : done + count].astype(BF16)

    loads = [pltpu.make_async_copy(proprio.at[pl.ds(base, n)], p_s, in_sem.at[n])]
    loads += [pltpu.make_async_copy(images.at[base + s], x_s.at[s], in_sem.at[s]) for s in range(n)]
    loads += [pltpu.make_async_copy(out_grad.at[pl.ds(base, n)], g_s, in_sem.at[n + 1])]
    for copy in loads:
        copy.start()

    smask = head_mask(HEADS * qry, qry, width)
    smask_low = smask.astype(BF16)
    tmask = head_mask(HEADS * ctx, ctx, width)
    tmask_low = tmask.astype(BF16)
    for e in range(emb):
        qs = spread(queries[e], smask_low)
        qs_s[e] = qs
        a_s[e] = (mm_bt(key_w[e], qs) * scale).astype(BF16)
        macc_s[e] = jnp.zeros((width, width), F32)
        vacc_s[e] = jnp.zeros((width, width), F32)
        mixacc_s[e] = jnp.zeros((width, width), F32)
        liftacc_s[e] = jnp.zeros(liftacc_s.shape[1:], F32)

    loads[0].wait()
    for s in range(n):
        e = emb_ref[base + s]
        lifted = mm(p_s[s].reshape(steps * ptok, -1), lift_w[e])
        act, dact = gelu_parts(lifted)
        act_low = act.astype(BF16)
        act_s[s] = act_low
        dact_s[s] = dact
        tok_s[s, :, qry:] = mm(act_low, mix_w[e]).astype(BF16).reshape(steps, ptok, width)

    view_of = lax.broadcasted_iota(jnp.int32, (keys, width), 0) // (keys // views)
    for s in range(n):
        e = emb_ref[base + s]
        bias = jnp.zeros((keys, width), F32)
        for v in range(views):
            lost = jnp.where(views_ref[base + s, v] > 0, 0.0, -1e30).astype(F32)
            bias = jnp.where(view_of == v, lost, bias)
        loads[1 + s].wait()
        for t in range(steps):
            x = x_s[s, t]
            xt_s[s, t] = x.T
            prob = softmax_rows(mm(x, a_s[e]), bias)
            prob_s[s, t] = prob
            prob_low = prob.astype(BF16)
            probb_s[s, t] = prob_low
            ut = mm(xt_s[s, t], prob_low).astype(BF16)
            ut_s[s, t] = ut
            satt_s[s, t] = fold(mm_at(ut, value_w[e]), smask).astype(BF16)
    image_tok = mm(satt_s[...].reshape(n * steps * qry, width), stem_proj[...])
    tok_s[:, :, :qry] = image_tok.astype(BF16).reshape(n, steps, qry, width)

    chunk = CORES * ctx
    spans = [pl.ds(i * chunk, chunk) for i in range(rows // chunk)]
    again_row = again[...].astype(F32).reshape(1, width)
    abias_row = abias[...].astype(F32).reshape(1, width)
    mgain_row = mgain[...].astype(F32).reshape(1, width)
    mbias_row = mbias[...].astype(F32).reshape(1, width)
    upb_row = up_b[...].astype(F32).reshape(1, ffw)
    downb_row = down_b[...].astype(F32).reshape(1, width)

    def tokens_of(i):
        return tok_s[CORES * i : CORES * (i + 1)].reshape(chunk, width).astype(F32)

    for i, span in enumerate(spans):
        hat, rstd = norm_parts(tokens_of(i))
        hat1_s[span] = hat
        rstd1_s[span] = jnp.broadcast_to(rstd, hat.shape)
        norm1 = (hat * again_row + abias_row).astype(BF16)
        norm1_s[span] = norm1
        qkv_s[span] = mm(norm1, qkv_w[...]).astype(BF16)

    key_step = lax.broadcasted_iota(jnp.int32, (ctx, 1), 0) // half_tok
    for s in range(n):
        mine = pl.ds(s * ctx, ctx)
        query, key, value = (qkv_s[mine, width * j : width * (j + 1)] for j in range(3))
        dead = jnp.where(key_step < steps_ref[base + s], 0.0, -1e30).astype(F32)
        prob = softmax_rows(mm_bt(key, spread(query, tmask_low)) * scale, dead)
        tprob_s[s] = prob
        att_s[mine] = fold(mm_at(prob.astype(BF16), value), tmask).astype(BF16)

    loads[n + 1].wait()
    row_step = lax.broadcasted_iota(jnp.int32, (ctx, 1), 0) // half_tok
    mgain_sum = jnp.zeros((1, width), F32)
    mbias_sum = jnp.zeros((1, width), F32)
    downb_sum = jnp.zeros((1, width), F32)
    upb_sum = jnp.zeros((1, ffw), F32)
    for i, span in enumerate(spans):
        middle = tokens_of(i) + mm(att_s[span], aproj[...])
        hat, rstd = norm_parts(middle)
        hat2_s[span] = hat
        rstd2_s[span] = jnp.broadcast_to(rstd, hat.shape)
        norm2 = (hat * mgain_row + mbias_row).astype(BF16)
        norm2_s[span] = norm2
        act, dact = gelu_parts(mm(norm2, up_w[...]) + upb_row)
        act_low = act.astype(BF16)
        up_s[span] = act_low
        live = jnp.concatenate(
            [
                jnp.where(row_step < steps_ref[base + CORES * i + j], 1.0, 0.0).astype(F32)
                for j in range(CORES)
            ],
            axis=0,
        )
        result = (middle + mm(act_low, down_w[...]) + downb_row) * live
        blk_s[CORES * i : CORES * (i + 1)] = result.astype(BF16).reshape(CORES, steps, half_tok, width)
        grad = g_s[CORES * i : CORES * (i + 1)].reshape(chunk, width).astype(F32) * live
        grad_low = grad.astype(BF16)
        glow_s[span] = grad_low
        downb_sum += jnp.sum(grad, axis=0, keepdims=True)
        grad_up = mm_bt(grad_low, down_w[...]).astype(BF16).astype(F32)
        grad_pre = (grad_up * dact).astype(BF16)
        gpre_s[span] = grad_pre
        upb_sum += jnp.sum(grad_pre.astype(F32), axis=0, keepdims=True)
        grad_norm2 = mm_bt(grad_pre, up_w[...]).astype(BF16).astype(F32)
        mgain_sum += jnp.sum(grad_norm2 * hat, axis=0, keepdims=True)
        mbias_sum += jnp.sum(grad_norm2, axis=0, keepdims=True)
        grad_mid = norm_grad(grad_norm2, mgain_row, hat, rstd) + grad
        gn2_s[span] = grad_mid
        grad_mid_low = grad_mid.astype(BF16)
        gmid_s[span] = grad_mid_low
        gatt_s[span] = mm_bt(grad_mid_low, aproj[...]).astype(BF16)
    put("aproj", 0, mm_at(att_s[...], gmid_s[...]))
    put("down", 0, mm_at(up_s[...], glow_s[...]))
    for j in range(ffw // width):
        cols = slice(width * j, width * (j + 1))
        put("up", width * j, mm_at(norm2_s[...], gpre_s[:, cols]))

    for s in range(n):
        mine = pl.ds(s * ctx, ctx)
        query, key, value = (qkv_s[mine, width * j : width * (j + 1)] for j in range(3))
        query_spread = spread(query, tmask_low)
        grad_spread = spread(gatt_s[mine], tmask_low)
        prob = tprob_s[s]
        grad_prob = mm_bt(value, grad_spread).astype(BF16).astype(F32)
        grad_raw = (softmax_rows_grad(prob, grad_prob) * scale).astype(BF16)
        grad_query = fold(mm_at(grad_raw, key), tmask)
        gqkv_s[mine, :width] = grad_query.astype(BF16)
        gqkv_s[mine, width : 2 * width] = mm(grad_raw, query_spread).astype(BF16)
        gqkv_s[mine, 2 * width :] = mm(prob.astype(BF16), grad_spread).astype(BF16)
    again_sum = jnp.zeros((1, width), F32)
    abias_sum = jnp.zeros((1, width), F32)
    for i, span in enumerate(spans):
        grad_norm1 = mm_bt(gqkv_s[span], qkv_w[...]).astype(BF16).astype(F32)
        hat = hat1_s[span]
        again_sum += jnp.sum(grad_norm1 * hat, axis=0, keepdims=True)
        abias_sum += jnp.sum(grad_norm1, axis=0, keepdims=True)
        grad_tok = norm_grad(grad_norm1, again_row, hat, rstd1_s[span]) + gn2_s[span]
        gtok_s[CORES * i : CORES * (i + 1)] = grad_tok.astype(BF16).reshape(CORES, steps, half_tok, width)
    for j in range(3):
        cols = slice(width * j, width * (j + 1))
        put("qkv", width * j, mm_at(norm1_s[...], gqkv_s[:, cols]))
    vectors = [again_sum, abias_sum, mgain_sum, mbias_sum, downb_sum]
    vectors += [upb_sum[:, width * j : width * (j + 1)] for j in range(ffw // width)]
    vectors += [jnp.zeros((16 - len(vectors), width), F32)]
    put("vectors", 0, jnp.concatenate(vectors, axis=0))

    for s in range(n):
        e = emb_ref[base + s]
        grad_prop = gtok_s[s, :, qry:].reshape(steps * ptok, width)
        mixacc_s[e] += mm_at(act_s[s], grad_prop)
        grad_act = mm_bt(grad_prop, mix_w[e]).astype(BF16).astype(F32)
        grad_lift = (grad_act * dact_s[s]).astype(BF16)
        liftacc_s[e] += mm_at(p_s[s].reshape(steps * ptok, -1), grad_lift)
        prp_s[s] = mm_bt(grad_lift, lift_w[e]).astype(BF16).reshape(steps, ptok, -1)

    grad_img = gtok_s[:, :, :qry].reshape(n * steps * qry, width)
    put("stem", 0, mm_at(satt_s[...].reshape(n * steps * qry, width), grad_img))
    gsatt_s[...] = mm_bt(grad_img, stem_proj[...]).astype(BF16).reshape(n, steps, qry, width)
    for s in range(n):
        e = emb_ref[base + s]
        for t in range(steps):
            grad_spread = spread(gsatt_s[s, t], smask_low)
            back = mm_bt(value_w[e], grad_spread).astype(BF16)
            prob = prob_s[s, t]
            grad_prob = mm(x_s[s, t], back).astype(BF16).astype(F32)
            grad_raw = softmax_rows_grad(prob, grad_prob).astype(BF16)
            macc_s[e] += mm(xt_s[s, t], grad_raw)
            vacc_s[e] += mm(ut_s[s, t], grad_spread)
            image = mm_bt(grad_raw, a_s[e]) + mm_bt(probb_s[s, t], back)
            img_s[s, t] = image.astype(BF16)
    for e in range(emb):
        moment = (macc_s[e] * scale).astype(BF16)
        put("keyw", width * e, mm(moment, qs_s[e]))
        put("queries", qry * e, fold(mm_at(moment, key_w[e]), smask))
        put("valuew", width * e, vacc_s[e])
        put("mixer", width * e, mixacc_s[e])
        put("lift", liftacc_s.shape[1] * e, liftacc_s[e])
    used = max(first + count for first, count in table.values())
    for at, lo, _, count in cuts(used, 2 * PIECES * piece - used, piece):
        pack_s[at // PIECES, at % PIECES, lo : lo + count] = jnp.zeros((count, width), BF16)

    other = 1 - sec
    mine = pl.ds(base, n)
    stores = (
        (pack_s.at[sec], keep),
        (pack_s.at[other], send),
        (blk_s.at[:, sec], block_out.at[mine]),
        (blk_s.at[:, other], block_send),
        (img_s.at[:, sec], image_out.at[mine, 0]),
        (img_s.at[:, other], image_send),
        (prp_s.at[:, sec], prop_out.at[mine, 0]),
        (prp_s.at[:, other], prop_send),
    )
    stores = [pltpu.make_async_copy(a, b, out_sem.at[i]) for i, (a, b) in enumerate(stores)]
    for copy in stores:
        copy.start()
    for copy in stores:
        copy.wait()


def compute(args, table, total):
    images, proprio, view_mask, embodiment, ctx_steps = args[:5]
    weights, out_grad = args[5:21], args[21]
    samples, steps, keys, width = images.shape
    ptok, feats = proprio.shape[2:]
    emb, qry = weights[0].shape[:2]
    ffw = weights[12].shape[1]
    n = samples // CORES
    half_tok = qry + ptok
    ctx = steps * half_tok
    rows = n * ctx
    piece = total // (CORES * PIECES)
    dims = (n, steps, keys, width, qry, ptok, emb, ffw, table, view_mask.shape[1])

    def low(*shape):
        return pltpu.VMEM(shape, BF16)

    def full(*shape):
        return pltpu.VMEM(shape, F32)

    scratch = [
        low(n, steps, keys, width),
        low(n, steps, ptok, feats),
        low(n, ctx, width),
        low(emb, HEADS * qry, width),
        low(emb, width, HEADS * qry),
        low(n, steps, half_tok, width),
        low(n, steps, width, keys),
        full(n, steps, keys, HEADS * qry),
        low(n, steps, keys, HEADS * qry),
        low(n, steps, width, HEADS * qry),
        low(n, steps, qry, width),
        low(n, steps * ptok, width),
        full(n, steps * ptok, width),
        full(rows, width),
        full(rows, width),
        low(rows, width),
        low(rows, 3 * width),
        full(n, ctx, HEADS * ctx),
        low(rows, width),
        full(rows, width),
        full(rows, width),
        low(rows, width),
        low(rows, ffw),
        full(rows, ffw),
        low(rows, width),
        low(rows, ffw),
        full(rows, width),
        low(rows, width),
        low(rows, width),
        low(rows, 3 * width),
        full(rows, width),
        low(n, steps, half_tok, width),
        low(n, steps, qry, width),
        low(n, steps, half_tok, width),
        low(n, steps, keys, width),
        low(n, steps, ptok, feats),
        full(emb, width, HEADS * qry),
        full(emb, width, width),
        full(emb, width, width),
        full(emb, feats, width),
        low(CORES, PIECES, piece, width),
        pltpu.SemaphoreType.DMA((n + 2,)),
        pltpu.SemaphoreType.DMA((8,)),
    ]
    shape = jax.ShapeDtypeStruct
    return pl.pallas_call(
        functools.partial(compute_kernel, dims),
        out_shape=(
            shape((PIECES, piece, width), BF16),
            shape((PIECES, piece, width), BF16),
            shape((samples, half_tok, width), BF16),
            shape((n, half_tok, width), BF16),
            shape((samples, 1, keys, width), BF16),
            shape((n, keys, width), BF16),
            shape((samples, 1, ptok, feats), BF16),
            shape((n, ptok, feats), BF16),
        ),
        in_specs=[SMEM] * 3 + [ANY] * 3 + [VMEM] * 16,
        out_specs=(ANY,) * 8,
        scratch_shapes=scratch,
        compiler_params=pltpu.CompilerParams(vmem_limit_bytes=56 * 2**20),
        name="stem_trunk",
    )(embodiment, ctx_steps, view_mask, images, proprio, out_grad, *weights)


def own_bits():
    dp, sec = lax.axis_index("dp"), lax.axis_index("section")
    low, high = dp % 2, (dp // 2) % 2
    return jnp.where(sec == 0, low, high), jnp.where(sec == 0, high, low)


def add_split_kernel(which, held, came, keep, send):
    bit = own_bits()[which]
    keep[...] = (held[bit].astype(F32) + came[bit].astype(F32)).astype(BF16)
    send[...] = (held[1 - bit].astype(F32) + came[1 - bit].astype(F32)).astype(BF16)


def add_split(which, held, came):
    held, came = (v.reshape((2, -1) + v.shape[-1:]) for v in (held, came))
    shape = jax.ShapeDtypeStruct(held.shape[1:], BF16)
    return pl.pallas_call(
        functools.partial(add_split_kernel, which),
        out_shape=(shape, shape),
        in_specs=[VMEM] * 2,
        out_specs=(VMEM,) * 2,
        name=f"add_split_{which}",
    )(held, came)


def swap_cores(value):
    return lax.ppermute(value, "section", [(0, 1), (1, 0)])


def swap_chips(value, bits):
    count = lax.axis_size("dp")
    pairs = [
        (s * count + i, s * count + (i ^ (1 << bits[s]))) for s in range(CORES) for i in range(count)
    ]
    return lax.ppermute(value, ("section", "dp"), pairs)


def join_kernel(blk_in, img_in, prp_in, blk_r, img_r, prp_r, blk, img, prp, sem):
    n = blk_r.shape[0]
    other = pl.ds((1 - lax.axis_index("section")) * n, n)
    copies = (
        pltpu.make_async_copy(blk_r, blk.at[other], sem.at[0]),
        pltpu.make_async_copy(img_r, img.at[other, 0], sem.at[1]),
        pltpu.make_async_copy(prp_r, prp.at[other, 0], sem.at[2]),
    )
    for copy in copies:
        copy.start()
    for copy in copies:
        copy.wait()


def join(own, came):
    return pl.pallas_call(
        join_kernel,
        out_shape=tuple(jax.ShapeDtypeStruct(v.shape, v.dtype) for v in own),
        in_specs=[ANY] * 6,
        out_specs=(ANY,) * 3,
        input_output_aliases={0: 0, 1: 1, 2: 2},
        scratch_shapes=[pltpu.SemaphoreType.DMA((3,))],
        name="join_outputs",
    )(*own, *came)


def unpack_kernel(table, *refs):
    pieces, outs, (pack, sem) = refs[:8], refs[8:-2], refs[-2:]
    sec = lax.axis_index("section")
    one, two = own_bits()
    copies = []
    for owner in range(CORES):
        first, second = (one, two) if owner == 0 else (two, one)
        start = (sec if owner == 0 else 1 - sec) * PIECES
        for j in range(PIECES):
            x = first if j < 2 else 1 - first
            y = second if j % 2 == 0 else 1 - second
            at = start + 2 * x + y
            i = owner * PIECES + j
            copies.append(pltpu.make_async_copy(pieces[i], pack.at[at], sem.at[i]))
    for copy in copies:
        copy.start()
    for copy in copies:
        copy.wait()
    piece = pack.shape[1]

    def get(name, row, count, store):
        for at, lo, done, size in cuts(table[name][0] + row, count, piece):
            store(done, size, pack[at, lo : lo + size].astype(F32))

    def flat(ref, name):
        def store(done, size, value):
            ref[done : done + size] = value

        get(name, 0, ref.shape[0], store)

    def stacked(ref, name):
        for e in range(ref.shape[0]):

            def store(done, size, value, e=e):
                ref[e, done : done + size] = value

            get(name, e * ref.shape[1], ref.shape[1], store)

    def blocks(ref, name):
        depth, width = ref.shape[0], pack.shape[2]
        for j in range(ref.shape[1] // width):

            def store(done, size, value, j=j):
                ref[done : done + size, width * j : width * (j + 1)] = value

            get(name, j * depth, depth, store)

    q, k, v, stem, lift, mix, again, abias, qkv, aproj, mgain, mbias, up, upb, down, downb = outs
    for ref, name in ((q, "queries"), (k, "keyw"), (v, "valuew"), (lift, "lift"), (mix, "mixer")):
        stacked(ref, name)
    for ref, name in ((stem, "stem"), (aproj, "aproj"), (down, "down")):
        flat(ref, name)
    for ref, name in ((qkv, "qkv"), (up, "up")):
        blocks(ref, name)
    at, lo, _, _ = next(cuts(table["vectors"][0], 16, piece))
    vectors = pack[at, lo : lo + 16].astype(F32)
    width = pack.shape[2]
    for i, ref in enumerate((again, abias, mgain, mbias, downb)):
        ref[...] = vectors[i]
    for j in range(upb.shape[0] // width):
        upb[width * j : width * (j + 1)] = vectors[5 + j]


def unpack(pieces, table, shapes):
    return pl.pallas_call(
        functools.partial(unpack_kernel, table),
        out_shape=tuple(jax.ShapeDtypeStruct(s, F32) for s in shapes),
        in_specs=[ANY] * 8,
        out_specs=(VMEM,) * len(shapes),
        scratch_shapes=[
            pltpu.VMEM((CORES * PIECES,) + pieces[0].shape, BF16),
            pltpu.SemaphoreType.DMA((8,)),
        ],
        compiler_params=pltpu.CompilerParams(vmem_limit_bytes=32 * 2**20),
        name="unpack",
    )(*pieces)


def sum_chips(held, came):
    levels = lax.axis_size("dp").bit_length() - 1
    first, second = (0, 1), (1, 0)
    keep, send = add_split(0, held, came)
    keep, send = add_split(1, keep, swap_chips(send, first))
    total = keep + swap_chips(send, second)
    for bits in zip(range(2, levels), reversed(range(2, levels))):
        total = total + swap_chips(total, bits)
    by_second = swap_chips(total, second)
    by_first = swap_chips(total, first)
    by_both = swap_chips(by_second, first)
    return total, by_second, by_first, by_both


def per_device(*args):
    weights = args[5:21]
    emb, qry, width = weights[0].shape
    table, total = layout(width, weights[12].shape[1], emb, qry, weights[4].shape[1])
    keep, send, blk, blk_s, img, img_s, prp, prp_s = compute(args, table, total)
    came = swap_cores(send)
    others = tuple(swap_cores(v) for v in (blk_s, img_s, prp_s))
    pieces = sum_chips(keep, came)
    pieces += tuple(swap_cores(v) for v in pieces)
    blk, img, prp = join((blk, img, prp), others)
    grads = unpack(pieces, table, [w.shape for w in weights])
    return (blk, img, prp) + tuple(grads)


def solution(mesh):
    sample = [P("dp")] * 5
    return jax.shard_map(
        per_device,
        mesh=mesh,
        in_specs=tuple(sample + [P()] * 16 + [P("dp")]),
        out_specs=(P("dp", "section"),) * 3 + (P(),) * 16,
        check_vma=False,
    )
```

```python
import functools
import math

import jax
import jax.numpy as jnp
from jax import lax
from jax.experimental import pallas as pl
from jax.experimental.pallas import tpu as pltpu
from jax.sharding import PartitionSpec as P

HEADS = 8
F32 = jnp.float32
BF16 = jnp.bfloat16
CORES = 2
PIECES = 4
EPS = 1e-05
INV_SQRT2 = 1.0 / math.sqrt(2.0)
INV_SQRT2PI = 1.0 / math.sqrt(2.0 * math.pi)
ANY = pl.BlockSpec(memory_space=pl.ANY)
VMEM = pl.BlockSpec(memory_space=pltpu.VMEM)
SMEM = pl.BlockSpec(memory_space=pltpu.SMEM)


def mm(left, right):
    return lax.dot_general(left, right, (((1,), (0,)), ((), ())), preferred_element_type=F32)


def mm_bt(left, right):
    return lax.dot_general(left, right, (((1,), (1,)), ((), ())), preferred_element_type=F32)


def mm_at(left, right):
    return lax.dot_general(left, right, (((0,), (0,)), ((), ())), preferred_element_type=F32)


def layout(width, ffw, emb, queries, feats):
    counts = (
        ("keyw", emb * width),
        ("valuew", emb * width),
        ("mixer", emb * width),
        ("stem", width),
        ("lift", emb * feats),
        ("queries", emb * queries),
        ("qkv", 3 * width),
        ("aproj", width),
        ("up", ffw),
        ("down", ffw),
        ("vectors", 16),
    )
    table, first = {}, 0
    for name, rows in counts:
        table[name] = (first, rows)
        first += rows
    step = CORES * PIECES * 16
    return table, (first + step - 1) // step * step


def cuts(first, rows, piece):
    done = 0
    while done < rows:
        at = first + done
        count = min(rows - done, piece - at % piece)
        yield at // piece, at % piece, done, count
        done += count


def head_mask(rows, per_head, width):
    row = lax.broadcasted_iota(jnp.int32, (rows, width), 0) // per_head
    col = lax.broadcasted_iota(jnp.int32, (rows, width), 1) // (width // HEADS)
    return (row == col).astype(F32)


def spread(rows, mask):
    return jnp.concatenate([rows] * HEADS, axis=0) * mask


def fold(full, mask):
    per = full.shape[0] // HEADS
    return jnp.sum((full * mask).reshape(HEADS, per, full.shape[1]), axis=0)


def gelu_parts(values):
    cdf = 0.5 * (1.0 + lax.erf(values * INV_SQRT2))
    pdf = INV_SQRT2PI * jnp.exp(-0.5 * values * values)
    return values * cdf, cdf + values * pdf


def softmax_rows(scores, bias):
    scores = scores + bias
    expo = jnp.exp(scores - jnp.max(scores, axis=0, keepdims=True))
    return expo / jnp.sum(expo, axis=0, keepdims=True)


def per_step(row, reduce):
    part = reduce(row.reshape(-1, 8, row.shape[1]), axis=0)
    pair = jnp.maximum if reduce is jnp.max else jnp.add
    part = pair(part, pltpu.roll(part, 4, 0))
    return pair(part, pltpu.roll(part, 2, 0))


def softmax_lines(scores, bias):
    tiles = (scores + bias).reshape(-1, 8, scores.shape[1])
    expo = jnp.exp(tiles - per_step(scores + bias, jnp.max))
    return (expo * (1.0 / per_step(expo.reshape(scores.shape), jnp.sum))).reshape(scores.shape)


def softmax_lines_grad(probs, grad):
    terms = probs * grad
    total = per_step(terms, jnp.sum)
    tiles = (-1, 8, probs.shape[1])
    return (terms.reshape(tiles) - probs.reshape(tiles) * total).reshape(probs.shape)


def softmax_rows_grad(probs, grad):
    terms = probs * grad
    return terms - probs * jnp.sum(terms, axis=0, keepdims=True)


def norm_parts(values):
    center = values - jnp.mean(values, axis=-1, keepdims=True)
    rstd = lax.rsqrt(jnp.mean(center * center, axis=-1, keepdims=True) + EPS)
    return center * rstd, rstd


def norm_grad(grad, gain, hat, rstd):
    scaled = grad * gain
    first = jnp.mean(scaled, axis=-1, keepdims=True)
    second = jnp.mean(scaled * hat, axis=-1, keepdims=True)
    return rstd * (scaled - first - hat * second)


def compute_kernel(
    dims,
    emb_ref,
    steps_ref,
    views_ref,
    images,
    proprio,
    out_grad,
    queries,
    key_w,
    value_w,
    stem_proj,
    lift_w,
    mix_w,
    again,
    abias,
    qkv_w,
    aproj,
    mgain,
    mbias,
    up_w,
    up_b,
    down_w,
    down_b,
    keep,
    send,
    block_out,
    block_send,
    image_out,
    image_send,
    prop_out,
    prop_send,
    xin_s,
    x_s,
    p_s,
    g_s,
    qs_s,
    a_s,
    tok_s,
    xt_s,
    prob_s,
    mix_s,
    ab_s,
    ut_s,
    satt_s,
    act_s,
    dact_s,
    hat1_s,
    rstd1_s,
    norm1_s,
    qkv_s,
    tprob_s,
    att_s,
    hat2_s,
    rstd2_s,
    norm2_s,
    up_s,
    glow_s,
    gpre_s,
    gn2_s,
    gmid_s,
    gatt_s,
    gqkv_s,
    gtok_s,
    gsatt_s,
    blk_s,
    img_s,
    prp_s,
    macc_s,
    vacc_s,
    mixacc_s,
    liftacc_s,
    pack_s,
    in_sem,
    out_sem,
):
    n, steps, keys, width, qry, ptok, emb, ffw, table, views = dims
    half_tok = qry + ptok
    ctx = steps * half_tok
    rows = n * ctx
    scale = 1.0 / math.sqrt(width // HEADS)
    piece = pack_s.shape[2]
    sec = lax.axis_index("section")
    base = sec * n
    lines = steps * keys
    tall = x_s.shape[1]

    def put(name, row, value):
        first = table[name][0] + row
        for at, lo, done, count in cuts(first, value.shape[0], piece):
            pack_s[at // PIECES, at % PIECES, lo : lo + count] = value[done : done + count].astype(BF16)

    loads = [
        pltpu.make_async_copy(proprio.at[pl.ds(base, n)], p_s, in_sem.at[0]),
        pltpu.make_async_copy(
            images.at[pl.ds(pl.multiple_of(sec * n * lines, 16), n * lines)],
            xin_s.at[pl.ds(0, n * lines)],
            in_sem.at[1],
        ),
        pltpu.make_async_copy(out_grad.at[pl.ds(base, n)], g_s, in_sem.at[2]),
    ]
    for copy in loads:
        copy.start()

    smask = head_mask(HEADS * qry, qry, width)
    smask_low = smask.astype(BF16)
    tmask = head_mask(HEADS * ctx, ctx, width)
    tmask_low = tmask.astype(BF16)
    for e in range(emb):
        qs = spread(queries[e], smask_low)
        qs_s[e] = qs
        a_s[e] = (mm_bt(key_w[e], qs) * scale).astype(BF16)
        macc_s[e] = jnp.zeros((width, width), F32)
        vacc_s[e] = jnp.zeros((width, width), F32)
        mixacc_s[e] = jnp.zeros((width, width), F32)
        liftacc_s[e] = jnp.zeros(liftacc_s.shape[1:], F32)

    loads[0].wait()
    for s in range(n):
        e = emb_ref[base + s]
        lifted = mm(p_s[s].reshape(steps * ptok, -1), lift_w[e])
        act, dact = gelu_parts(lifted)
        act_low = act.astype(BF16)
        act_s[s] = act_low
        dact_s[s] = dact
        tok_s[s, :, qry:] = mm(act_low, mix_w[e]).astype(BF16).reshape(steps, ptok, width)

    loads[1].wait()
    xin_s[n * lines :] = jnp.zeros((xin_s.shape[0] - n * lines, width), BF16)
    edge = lines // 16 * 16
    inside = lax.broadcasted_iota(jnp.int32, (tall - edge, width), 0) < lines - edge
    for s in range(n):
        x_s[s] = xin_s[lines * s : lines * s + tall]
        last = x_s[s, edge:].astype(F32)
        x_s[s, edge:] = jnp.where(inside, last, 0.0).astype(BF16)

    row = lax.broadcasted_iota(jnp.int32, (tall, width), 0)
    first_step = row % steps == 0
    for s in range(n):
        e = emb_ref[base + s]
        bias = jnp.full((tall, width), -1e30, F32)
        for v in reversed(range(views)):
            lost = jnp.where(views_ref[v, base + s] > 0, 0.0, -1e30).astype(F32)
            bias = jnp.where(row < lines // views * (v + 1), lost, bias)
        prob = softmax_lines(mm(x_s[s], a_s[e]), bias)
        prob_s[s] = prob
        mix_s[s, :, :width] = jnp.where(first_step, prob, 0.0).astype(BF16)
        mix_s[s, :, width : 2 * width] = jnp.where(first_step, 0.0, prob).astype(BF16)
        turned = x_s[s].T
        xt_s[s] = turned
        ut = mm(turned, mix_s[s, :, : 2 * width]).astype(BF16)
        ut_s[s] = ut
        values = mm(ut.T, value_w[e])
        for t in range(steps):
            satt_s[s, t] = fold(values[width * t : width * (t + 1)], smask).astype(BF16)
    image_tok = mm(satt_s[...].reshape(n * steps * qry, width), stem_proj[...])
    tok_s[:, :, :qry] = image_tok.astype(BF16).reshape(n, steps, qry, width)

    chunk = CORES * ctx
    spans = [pl.ds(i * chunk, chunk) for i in range(rows // chunk)]
    again_row = again[...].astype(F32).reshape(1, width)
    abias_row = abias[...].astype(F32).reshape(1, width)
    mgain_row = mgain[...].astype(F32).reshape(1, width)
    mbias_row = mbias[...].astype(F32).reshape(1, width)
    upb_row = up_b[...].astype(F32).reshape(1, ffw)
    downb_row = down_b[...].astype(F32).reshape(1, width)

    def tokens_of(i):
        return tok_s[CORES * i : CORES * (i + 1)].reshape(chunk, width).astype(F32)

    for i, span in enumerate(spans):
        hat, rstd = norm_parts(tokens_of(i))
        hat1_s[span] = hat
        rstd1_s[span] = jnp.broadcast_to(rstd, hat.shape)
        norm1 = (hat * again_row + abias_row).astype(BF16)
        norm1_s[span] = norm1
        qkv_s[span] = mm(norm1, qkv_w[...]).astype(BF16)

    key_step = lax.broadcasted_iota(jnp.int32, (ctx, 1), 0) // half_tok
    for s in range(n):
        mine = pl.ds(s * ctx, ctx)
        query, key, value = (qkv_s[mine, width * j : width * (j + 1)] for j in range(3))
        dead = jnp.where(key_step < steps_ref[base + s], 0.0, -1e30).astype(F32)
        prob = softmax_rows(mm_bt(key, spread(query, tmask_low)) * scale, dead)
        tprob_s[s] = prob
        att_s[mine] = fold(mm_at(prob.astype(BF16), value), tmask).astype(BF16)

    loads[2].wait()
    row_step = lax.broadcasted_iota(jnp.int32, (ctx, 1), 0) // half_tok
    mgain_sum = jnp.zeros((1, width), F32)
    mbias_sum = jnp.zeros((1, width), F32)
    downb_sum = jnp.zeros((1, width), F32)
    upb_sum = jnp.zeros((1, ffw), F32)
    for i, span in enumerate(spans):
        middle = tokens_of(i) + mm(att_s[span], aproj[...])
        hat, rstd = norm_parts(middle)
        hat2_s[span] = hat
        rstd2_s[span] = jnp.broadcast_to(rstd, hat.shape)
        norm2 = (hat * mgain_row + mbias_row).astype(BF16)
        norm2_s[span] = norm2
        act, dact = gelu_parts(mm(norm2, up_w[...]) + upb_row)
        act_low = act.astype(BF16)
        up_s[span] = act_low
        live = jnp.concatenate(
            [
                jnp.where(row_step < steps_ref[base + CORES * i + j], 1.0, 0.0).astype(F32)
                for j in range(CORES)
            ],
            axis=0,
        )
        result = (middle + mm(act_low, down_w[...]) + downb_row) * live
        blk_s[CORES * i : CORES * (i + 1)] = result.astype(BF16).reshape(CORES, steps, half_tok, width)
        grad = g_s[CORES * i : CORES * (i + 1)].reshape(chunk, width).astype(F32) * live
        grad_low = grad.astype(BF16)
        glow_s[span] = grad_low
        downb_sum += jnp.sum(grad, axis=0, keepdims=True)
        grad_up = mm_bt(grad_low, down_w[...]).astype(BF16).astype(F32)
        grad_pre = (grad_up * dact).astype(BF16)
        gpre_s[span] = grad_pre
        upb_sum += jnp.sum(grad_pre.astype(F32), axis=0, keepdims=True)
        grad_norm2 = mm_bt(grad_pre, up_w[...]).astype(BF16).astype(F32)
        mgain_sum += jnp.sum(grad_norm2 * hat, axis=0, keepdims=True)
        mbias_sum += jnp.sum(grad_norm2, axis=0, keepdims=True)
        grad_mid = norm_grad(grad_norm2, mgain_row, hat, rstd) + grad
        gn2_s[span] = grad_mid
        grad_mid_low = grad_mid.astype(BF16)
        gmid_s[span] = grad_mid_low
        gatt_s[span] = mm_bt(grad_mid_low, aproj[...]).astype(BF16)
    put("aproj", 0, mm_at(att_s[...], gmid_s[...]))
    put("down", 0, mm_at(up_s[...], glow_s[...]))
    for j in range(ffw // width):
        cols = slice(width * j, width * (j + 1))
        put("up", width * j, mm_at(norm2_s[...], gpre_s[:, cols]))

    for s in range(n):
        mine = pl.ds(s * ctx, ctx)
        query, key, value = (qkv_s[mine, width * j : width * (j + 1)] for j in range(3))
        query_spread = spread(query, tmask_low)
        grad_spread = spread(gatt_s[mine], tmask_low)
        prob = tprob_s[s]
        grad_prob = mm_bt(value, grad_spread).astype(BF16).astype(F32)
        grad_raw = (softmax_rows_grad(prob, grad_prob) * scale).astype(BF16)
        grad_query = fold(mm_at(grad_raw, key), tmask)
        gqkv_s[mine, :width] = grad_query.astype(BF16)
        gqkv_s[mine, width : 2 * width] = mm(grad_raw, query_spread).astype(BF16)
        gqkv_s[mine, 2 * width :] = mm(prob.astype(BF16), grad_spread).astype(BF16)
    again_sum = jnp.zeros((1, width), F32)
    abias_sum = jnp.zeros((1, width), F32)
    for i, span in enumerate(spans):
        grad_norm1 = mm_bt(gqkv_s[span], qkv_w[...]).astype(BF16).astype(F32)
        hat = hat1_s[span]
        again_sum += jnp.sum(grad_norm1 * hat, axis=0, keepdims=True)
        abias_sum += jnp.sum(grad_norm1, axis=0, keepdims=True)
        grad_tok = norm_grad(grad_norm1, again_row, hat, rstd1_s[span]) + gn2_s[span]
        gtok_s[CORES * i : CORES * (i + 1)] = grad_tok.astype(BF16).reshape(CORES, steps, half_tok, width)
    for j in range(3):
        cols = slice(width * j, width * (j + 1))
        put("qkv", width * j, mm_at(norm1_s[...], gqkv_s[:, cols]))
    vectors = [again_sum, abias_sum, mgain_sum, mbias_sum, downb_sum]
    vectors += [upb_sum[:, width * j : width * (j + 1)] for j in range(ffw // width)]
    vectors += [jnp.zeros((16 - len(vectors), width), F32)]
    put("vectors", 0, jnp.concatenate(vectors, axis=0))

    for s in range(n):
        e = emb_ref[base + s]
        grad_prop = gtok_s[s, :, qry:].reshape(steps * ptok, width)
        mixacc_s[e] += mm_at(act_s[s], grad_prop)
        grad_act = mm_bt(grad_prop, mix_w[e]).astype(BF16).astype(F32)
        grad_lift = (grad_act * dact_s[s]).astype(BF16)
        liftacc_s[e] += mm_at(p_s[s].reshape(steps * ptok, -1), grad_lift)
        prp_s[s] = mm_bt(grad_lift, lift_w[e]).astype(BF16).reshape(steps, ptok, -1)

    grad_img = gtok_s[:, :, :qry].reshape(n * steps * qry, width)
    put("stem", 0, mm_at(satt_s[...].reshape(n * steps * qry, width), grad_img))
    gsatt_s[...] = mm_bt(grad_img, stem_proj[...]).astype(BF16).reshape(n, steps, qry, width)
    for s in range(n):
        e = emb_ref[base + s]
        grad_spread = jnp.concatenate([spread(gsatt_s[s, t], smask_low) for t in range(steps)], axis=0)
        back = mm_bt(value_w[e], grad_spread).astype(BF16)
        ab_s[s, :, : 2 * width] = back
        ab_s[s, :, 2 * width :] = a_s[e]
        both = mm(x_s[s], back)
        grad_prob = jnp.where(first_step, both[:, :width], both[:, width:])
        grad_raw = softmax_lines_grad(prob_s[s], grad_prob.astype(BF16).astype(F32)).astype(BF16)
        mix_s[s, :, 2 * width :] = grad_raw
        macc_s[e] += mm(xt_s[s], grad_raw)
        vacc_s[e] += mm(ut_s[s], grad_spread)

    for s in range(n):
        img_s[pl.ds(s, tall, stride=n)] = mm_bt(mix_s[s], ab_s[s])

    for e in range(emb):
        moment = (macc_s[e] * scale).astype(BF16)
        put("keyw", width * e, mm(moment, qs_s[e]))
        put("queries", qry * e, fold(mm_at(moment, key_w[e]), smask))
        put("valuew", width * e, vacc_s[e])
        put("mixer", width * e, mixacc_s[e])
        put("lift", liftacc_s.shape[1] * e, liftacc_s[e])
    used = max(first + count for first, count in table.values())
    for at, lo, _, count in cuts(used, 2 * PIECES * piece - used, piece):
        pack_s[at // PIECES, at % PIECES, lo : lo + count] = jnp.zeros((count, width), BF16)

    other = 1 - sec
    image = img_s.reshape(tall // steps, steps, n, width)
    stores = (
        (pack_s.at[sec], keep),
        (pack_s.at[other], send),
        (blk_s.at[:, sec], block_out),
        (blk_s.at[:, other], block_send),
        (image.at[pl.ds(0, keys), sec], image_out),
        (image.at[pl.ds(0, keys), other], image_send),
        (prp_s.at[:, sec], prop_out),
        (prp_s.at[:, other], prop_send),
    )
    stores = [pltpu.make_async_copy(a, b, out_sem.at[i]) for i, (a, b) in enumerate(stores)]
    for copy in stores:
        copy.start()
    for copy in stores:
        copy.wait()


def rows_of(images):
    return images.transpose(0, 2, 1, 3).reshape(-1, images.shape[-1])


def compute(args, table, total):
    images, proprio, view_mask, embodiment, ctx_steps = args[:5]
    weights, out_grad = args[5:21], args[21]
    samples, steps, keys, width = images.shape
    ptok, feats = proprio.shape[2:]
    emb, qry = weights[0].shape[:2]
    ffw = weights[12].shape[1]
    n = samples // CORES
    half_tok = qry + ptok
    ctx = steps * half_tok
    rows = n * ctx
    piece = total // (CORES * PIECES)
    lines = steps * keys
    tall = (lines + 15) // 16 * 16
    dims = (n, steps, keys, width, qry, ptok, emb, ffw, table, view_mask.shape[1])

    def low(*shape):
        return pltpu.VMEM(shape, BF16)

    def full(*shape):
        return pltpu.VMEM(shape, F32)

    scratch = [
        low((n * lines + 31) // 16 * 16, width),
        low(n, tall, width),
        low(n, steps, ptok, feats),
        low(n, ctx, width),
        low(emb, HEADS * qry, width),
        low(emb, width, HEADS * qry),
        low(n, steps, half_tok, width),
        low(n, width, tall),
        full(n, tall, HEADS * qry),
        low(n, tall, (steps + 1) * width),
        low(n, width, (steps + 1) * width),
        low(n, width, steps * width),
        low(n, steps, qry, width),
        low(n, steps * ptok, width),
        full(n, steps * ptok, width),
        full(rows, width),
        full(rows, width),
        low(rows, width),
        low(rows, 3 * width),
        full(n, ctx, HEADS * ctx),
        low(rows, width),
        full(rows, width),
        full(rows, width),
        low(rows, width),
        low(rows, ffw),
        low(rows, width),
        low(rows, ffw),
        full(rows, width),
        low(rows, width),
        low(rows, width),
        low(rows, 3 * width),
        low(n, steps, half_tok, width),
        low(n, steps, qry, width),
        low(n, steps, half_tok, width),
        full(tall * n, width),
        low(n, steps, ptok, feats),
        full(emb, width, HEADS * qry),
        full(emb, width, width),
        full(emb, width, width),
        full(emb, feats, width),
        low(CORES, PIECES, piece, width),
        pltpu.SemaphoreType.DMA((3,)),
        pltpu.SemaphoreType.DMA((8,)),
    ]
    shape = jax.ShapeDtypeStruct
    return pl.pallas_call(
        functools.partial(compute_kernel, dims),
        out_shape=(
            shape((PIECES, piece, width), BF16),
            shape((PIECES, piece, width), BF16),
            shape((n, half_tok, width), BF16),
            shape((n, half_tok, width), BF16),
            shape((keys, n, width), F32),
            shape((keys, n, width), F32),
            shape((n, ptok, feats), BF16),
            shape((n, ptok, feats), BF16),
        ),
        in_specs=[SMEM] * 3 + [ANY] * 3 + [VMEM] * 16,
        out_specs=(ANY,) * 8,
        scratch_shapes=scratch,
        compiler_params=pltpu.CompilerParams(vmem_limit_bytes=56 * 2**20),
        name="stem_trunk",
    )(embodiment, ctx_steps, view_mask.T, rows_of(images), proprio, out_grad, *weights)


def own_bits():
    dp, sec = lax.axis_index("dp"), lax.axis_index("section")
    low, high = dp % 2, (dp // 2) % 2
    return jnp.where(sec == 0, low, high), jnp.where(sec == 0, high, low)


def add_split(bit, held, came):
    total = (held.astype(F32) + came.astype(F32)).astype(BF16)
    low, high = total.reshape((2, -1, total.shape[-1]))
    return jnp.where(bit == 0, low, high), jnp.where(bit == 0, high, low)


def swap_cores(value):
    return lax.ppermute(value, "section", [(0, 1), (1, 0)])


def swap_chips(value, bits):
    count = lax.axis_size("dp")
    pairs = [
        (s * count + i, s * count + (i ^ (1 << bits[s]))) for s in range(CORES) for i in range(count)
    ]
    return lax.ppermute(value, ("section", "dp"), pairs)


def join(own, came, axis):
    first = lax.axis_index("section") == 0
    return jnp.where(first, jnp.concatenate([own, came], axis), jnp.concatenate([came, own], axis))


def unpack_kernel(table, *refs):
    pieces, outs, (pack, sem) = refs[:8], refs[8:-2], refs[-2:]
    sec = lax.axis_index("section")
    one, two = own_bits()
    copies = []
    for owner in range(CORES):
        first, second = (one, two) if owner == 0 else (two, one)
        start = (sec if owner == 0 else 1 - sec) * PIECES
        for j in range(PIECES):
            x = first if j < 2 else 1 - first
            y = second if j % 2 == 0 else 1 - second
            at = start + 2 * x + y
            i = owner * PIECES + j
            copies.append(pltpu.make_async_copy(pieces[i], pack.at[at], sem.at[i]))
    for copy in copies:
        copy.start()
    for copy in copies:
        copy.wait()
    piece = pack.shape[1]

    def get(name, row, count, store):
        for at, lo, done, size in cuts(table[name][0] + row, count, piece):
            store(done, size, pack[at, lo : lo + size].astype(F32))

    def flat(ref, name):
        def store(done, size, value):
            ref[done : done + size] = value

        get(name, 0, ref.shape[0], store)

    def stacked(ref, name):
        for e in range(ref.shape[0]):

            def store(done, size, value, e=e):
                ref[e, done : done + size] = value

            get(name, e * ref.shape[1], ref.shape[1], store)

    def blocks(ref, name):
        depth, width = ref.shape[0], pack.shape[2]
        for j in range(ref.shape[1] // width):

            def store(done, size, value, j=j):
                ref[done : done + size, width * j : width * (j + 1)] = value

            get(name, j * depth, depth, store)

    q, k, v, stem, lift, mix, again, abias, qkv, aproj, mgain, mbias, up, upb, down, downb = outs
    for ref, name in ((q, "queries"), (k, "keyw"), (v, "valuew"), (lift, "lift"), (mix, "mixer")):
        stacked(ref, name)
    for ref, name in ((stem, "stem"), (aproj, "aproj"), (down, "down")):
        flat(ref, name)
    for ref, name in ((qkv, "qkv"), (up, "up")):
        blocks(ref, name)
    at, lo, _, _ = next(cuts(table["vectors"][0], 16, piece))
    vectors = pack[at, lo : lo + 16].astype(F32)
    width = pack.shape[2]
    for i, ref in enumerate((again, abias, mgain, mbias, downb)):
        ref[...] = vectors[i]
    for j in range(upb.shape[0] // width):
        upb[width * j : width * (j + 1)] = vectors[5 + j]


def unpack(pieces, table, shapes):
    return pl.pallas_call(
        functools.partial(unpack_kernel, table),
        out_shape=tuple(jax.ShapeDtypeStruct(s, F32) for s in shapes),
        in_specs=[ANY] * 8,
        out_specs=(VMEM,) * len(shapes),
        scratch_shapes=[
            pltpu.VMEM((CORES * PIECES,) + pieces[0].shape, BF16),
            pltpu.SemaphoreType.DMA((8,)),
        ],
        compiler_params=pltpu.CompilerParams(vmem_limit_bytes=32 * 2**20),
        name="unpack",
    )(*pieces)


def sum_chips(held, came):
    levels = lax.axis_size("dp").bit_length() - 1
    first, second = (0, 1), (1, 0)
    one, two = own_bits()
    keep, send = add_split(one, held, came)
    keep, send = add_split(two, keep, swap_chips(send, first))
    total = keep + swap_chips(send, second)
    for bits in zip(range(2, levels), reversed(range(2, levels))):
        total = total + swap_chips(total, bits)
    by_second = swap_chips(total, second)
    by_first = swap_chips(total, first)
    by_both = swap_chips(by_second, first)
    return total, by_second, by_first, by_both


def per_device(*args):
    weights = args[5:21]
    emb, qry, width = weights[0].shape
    table, total = layout(width, weights[12].shape[1], emb, qry, weights[4].shape[1])
    keep, send, blk, blk_s, img, img_s, prp, prp_s = compute(args, table, total)
    came = swap_cores(send)
    blk_r, img_r, prp_r = (swap_cores(v) for v in (blk_s, img_s, prp_s))
    pieces = sum_chips(keep, came)
    pieces += tuple(swap_cores(v) for v in pieces)
    blk = join(blk, blk_r, 0)
    prp = join(prp, prp_r, 0)[:, None]
    img = join(img, img_r, 1).astype(BF16).transpose(1, 0, 2)[:, None]
    grads = unpack(pieces, table, [w.shape for w in weights])
    return (blk, img, prp) + tuple(grads)


def solution(mesh):
    sample = [P("dp")] * 5
    return jax.shard_map(
        per_device,
        mesh=mesh,
        in_specs=tuple(sample + [P()] * 16 + [P("dp")]),
        out_specs=(P("dp", "section"),) * 3 + (P(),) * 16,
        check_vma=False,
    )
```

```python
import functools
import math

import jax
import jax.numpy as jnp
from jax import lax
from jax.experimental import pallas as pl
from jax.experimental.pallas import tpu as pltpu
from jax.sharding import PartitionSpec as P

HEADS = 8
F32 = jnp.float32
BF16 = jnp.bfloat16
CORES = 2
CHAINS = 2
PIECES = 2 * CHAINS
EPS = 1e-05
INV_SQRT2 = 1.0 / math.sqrt(2.0)
INV_SQRT2PI = 1.0 / math.sqrt(2.0 * math.pi)
ANY = pl.BlockSpec(memory_space=pl.ANY)
VMEM = pl.BlockSpec(memory_space=pltpu.VMEM)
SMEM = pl.BlockSpec(memory_space=pltpu.SMEM)


def mm(left, right):
    return lax.dot_general(left, right, (((1,), (0,)), ((), ())), preferred_element_type=F32)


def mm_bt(left, right):
    return lax.dot_general(left, right, (((1,), (1,)), ((), ())), preferred_element_type=F32)


def mm_at(left, right):
    return lax.dot_general(left, right, (((0,), (0,)), ((), ())), preferred_element_type=F32)


def layout(width, ffw, emb, queries, feats):
    counts = (
        ("keyw", emb * width),
        ("valuew", emb * width),
        ("mixer", emb * width),
        ("stem", width),
        ("lift", emb * feats),
        ("queries", emb * queries),
        ("qkv", 3 * width),
        ("aproj", width),
        ("up", ffw),
        ("down", ffw),
        ("vectors", 16),
    )
    table, first = {}, 0
    for name, rows in counts:
        table[name] = (first, rows)
        first += rows
    step = CORES * PIECES * 32
    return table, (first + step - 1) // step * step


def cuts(first, rows, piece):
    done = 0
    while done < rows:
        at = first + done
        count = min(rows - done, piece - at % piece)
        yield at // piece, at % piece, done, count
        done += count


def head_mask(rows, per_head, width):
    row = lax.broadcasted_iota(jnp.int32, (rows, width), 0) // per_head
    col = lax.broadcasted_iota(jnp.int32, (rows, width), 1) // (width // HEADS)
    return (row == col).astype(F32)


def spread(rows, mask):
    return jnp.concatenate([rows] * HEADS, axis=0) * mask


def fold(full, mask):
    per = full.shape[0] // HEADS
    return jnp.sum((full * mask).reshape(HEADS, per, full.shape[1]), axis=0)


def gelu_parts(values):
    cdf = 0.5 * (1.0 + lax.erf(values * INV_SQRT2))
    pdf = INV_SQRT2PI * jnp.exp(-0.5 * values * values)
    return values * cdf, cdf + values * pdf


def staged(count, *stages):
    for step in range(count + len(stages) - 1):
        for lag, stage in enumerate(stages):
            if 0 <= step - lag < count:
                stage(step - lag)


def softmax_rows(scores):
    expo = jnp.exp(scores - jnp.max(scores, axis=0, keepdims=True))
    return expo / jnp.sum(expo, axis=0, keepdims=True)


def per_step(row, reduce):
    part = reduce(row.reshape(-1, 8, row.shape[1]), axis=0)
    pair = jnp.maximum if reduce is jnp.max else jnp.add
    part = pair(part, pltpu.roll(part, 4, 0))
    return pair(part, pltpu.roll(part, 2, 0))


def softmax_lines(scores):
    expo = jnp.exp(scores.reshape(-1, 8, scores.shape[1]) - per_step(scores, jnp.max))
    return (expo * (1.0 / per_step(expo.reshape(scores.shape), jnp.sum))).reshape(scores.shape)


def softmax_lines_grad(probs, grad):
    terms = probs * grad
    total = per_step(terms, jnp.sum)
    tiles = (-1, 8, probs.shape[1])
    return (terms.reshape(tiles) - probs.reshape(tiles) * total).reshape(probs.shape)


def softmax_rows_grad(probs, grad):
    terms = probs * grad
    return terms - probs * jnp.sum(terms, axis=0, keepdims=True)


def norm_parts(values):
    center = values - jnp.mean(values, axis=-1, keepdims=True)
    rstd = lax.rsqrt(jnp.mean(center * center, axis=-1, keepdims=True) + EPS)
    return center * rstd, rstd


def norm_grad(grad, gain, hat, rstd):
    scaled = grad * gain
    first = jnp.mean(scaled, axis=-1, keepdims=True)
    second = jnp.mean(scaled * hat, axis=-1, keepdims=True)
    return rstd * (scaled - first - hat * second)


def compute_kernel(
    dims,
    emb_ref,
    steps_ref,
    views_ref,
    images,
    proprio,
    out_grad,
    queries_h,
    key_h,
    value_h,
    stem_h,
    lift_h,
    mix_h,
    again,
    abias,
    qkv_h,
    aproj_h,
    mgain,
    mbias,
    up_h,
    up_b,
    down_h,
    down_b,
    keep0,
    keep1,
    send0,
    send1,
    block_out,
    block_send,
    image_out,
    image_send,
    prop_out,
    prop_send,
    queries,
    key_w,
    value_w,
    stem_proj,
    lift_w,
    mix_w,
    qkv_w,
    aproj,
    up_w,
    down_w,
    xin_s,
    x_s,
    p_s,
    g_s,
    qs_s,
    a_s,
    tok_s,
    xt_s,
    prob_s,
    sgrad_s,
    mix_s,
    ab_s,
    ut_s,
    satt_s,
    act_s,
    dact_s,
    hat1_s,
    rstd1_s,
    norm1_s,
    qkv_s,
    tprob_s,
    tlow_s,
    gprob_s,
    att_s,
    hat2_s,
    rstd2_s,
    norm2_s,
    up_s,
    glow_s,
    gpre_s,
    gn2_s,
    gmid_s,
    gatt_s,
    gqkv_s,
    gtok_s,
    gsatt_s,
    blk_s,
    img_s,
    prp_s,
    macc_s,
    vacc_s,
    mixacc_s,
    liftacc_s,
    pack_s,
    in_sem,
    out_sem,
):
    n, steps, keys, width, qry, ptok, emb, ffw, table, views = dims
    half_tok = qry + ptok
    ctx = steps * half_tok
    rows = n * ctx
    scale = 1.0 / math.sqrt(width // HEADS)
    piece = pack_s.shape[2]
    sec = lax.axis_index("section")
    base = sec * n
    lines = steps * keys
    tall = x_s.shape[1]
    embs = [emb_ref[base + s] for s in range(n)]

    def put(name, row, value):
        first = table[name][0] + row
        for at, lo, done, count in cuts(first, value.shape[0], piece):
            pack_s[at // PIECES, at % PIECES, lo : lo + count] = value[done : done + count].astype(BF16)

    loads = [
        pltpu.make_async_copy(a, b, in_sem.at[i])
        for i, (a, b) in enumerate(
            (
                (queries_h, queries),
                (key_h, key_w),
                (images.at[pl.ds(pl.multiple_of(sec * n * lines, 16), n * lines)], xin_s.at[pl.ds(0, n * lines)]),
                (proprio.at[pl.ds(base, n)], p_s),
                (lift_h, lift_w),
                (mix_h, mix_w),
                (value_h, value_w),
                (stem_h, stem_proj),
                (qkv_h, qkv_w),
                (aproj_h, aproj),
                (up_h, up_w),
                (down_h, down_w),
                (out_grad.at[pl.ds(base, n)], g_s),
            )
        )
    ]
    for copy in loads:
        copy.start()

    smask = head_mask(HEADS * qry, qry, width)
    smask_low = smask.astype(BF16)
    tmask = head_mask(HEADS * ctx, ctx, width)
    tmask_low = tmask.astype(BF16)
    for e in range(emb):
        macc_s[e] = jnp.zeros((width, width), F32)
        vacc_s[e] = jnp.zeros((width, width), F32)
        mixacc_s[e] = jnp.zeros((width, width), F32)
        liftacc_s[e] = jnp.zeros(liftacc_s.shape[1:], F32)
    used = max(first + count for first, count in table.values())
    for at, lo, _, count in cuts(used, CORES * PIECES * piece - used, piece):
        pack_s[at // PIECES, at % PIECES, lo : lo + count] = jnp.zeros((count, width), BF16)
    xin_s[n * lines :] = jnp.zeros((xin_s.shape[0] - n * lines, width), BF16)
    loads[0].wait()
    loads[1].wait()
    for e in range(emb):
        qs = spread(queries[e], smask_low)
        qs_s[e] = qs
        a_s[e] = (mm_bt(key_w[e], qs) * scale).astype(BF16)

    loads[2].wait()
    edge = lines // 16 * 16
    inside = lax.broadcasted_iota(jnp.int32, (tall - edge, width), 0) < lines - edge
    for s in range(n):
        x_s[s] = xin_s[lines * s : lines * s + tall]
        last = x_s[s, edge:].astype(F32)
        x_s[s, edge:] = jnp.where(inside, last, 0.0).astype(BF16)

    loads[3].wait()
    loads[4].wait()
    loads[5].wait()
    loads[6].wait()
    for s, e in enumerate(embs):
        lifted = mm(p_s[s].reshape(steps * ptok, -1), lift_w[e])
        act, dact = gelu_parts(lifted)
        act_low = act.astype(BF16)
        act_s[s] = act_low
        dact_s[s] = dact
        tok_s[s, :, qry:] = mm(act_low, mix_w[e]).astype(BF16).reshape(steps, ptok, width)

    first_step = lax.broadcasted_iota(jnp.int32, (tall, width), 0) % steps == 0

    def view_bias(s):
        lost = [jnp.where(views_ref[v, base + s] > 0, 0.0, -1e30).astype(F32) for v in range(views)]
        lost.append(jnp.float32(-1e30))
        ends = [lines // views * (v + 1) for v in range(views)]
        tiles, at = [], 0
        while at < tall:
            view = sum(at >= end for end in ends)
            stop = min([end // 8 * 8 for end in ends if end // 8 * 8 > at] + [tall])
            if view < views and ends[view] < at + 8:
                row = lax.broadcasted_iota(jnp.int32, (8, width), 0)
                tiles.append(jnp.where(row < ends[view] - at, lost[view], lost[view + 1]))
                at += 8
            else:
                tiles.append(jnp.full((stop - at, width), lost[view], F32))
                at = stop
        return jnp.concatenate(tiles, axis=0)

    def stem_scores(s):
        prob_s[s] = mm(x_s[s], a_s[embs[s]]) + view_bias(s)

    def stem_softmax(s):
        prob = softmax_lines(prob_s[s])
        prob_s[s] = prob
        mix_s[s, :, :width] = jnp.where(first_step, prob, 0.0).astype(BF16)
        mix_s[s, :, width : 2 * width] = jnp.where(first_step, 0.0, prob).astype(BF16)

    def stem_moments(s):
        turned = x_s[s].T
        xt_s[s] = turned
        ut_s[s] = mm(turned, mix_s[s, :, : 2 * width]).astype(BF16)

    def stem_values(s):
        values = mm(ut_s[s].T, value_w[embs[s]])
        for t in range(steps):
            satt_s[s, t] = fold(values[width * t : width * (t + 1)], smask).astype(BF16)

    staged(n, stem_scores, stem_softmax, stem_moments, stem_values)
    loads[7].wait()
    image_tok = mm(satt_s[...].reshape(n * steps * qry, width), stem_proj[...])
    tok_s[:, :, :qry] = image_tok.astype(BF16).reshape(n, steps, qry, width)

    loads[8].wait()
    chunk = CORES * ctx
    spans = [pl.ds(i * chunk, chunk) for i in range(rows // chunk)]
    again_row = again[...].astype(F32).reshape(1, width)
    abias_row = abias[...].astype(F32).reshape(1, width)
    mgain_row = mgain[...].astype(F32).reshape(1, width)
    mbias_row = mbias[...].astype(F32).reshape(1, width)
    upb_row = up_b[...].astype(F32).reshape(1, ffw)
    downb_row = down_b[...].astype(F32).reshape(1, width)

    def tokens_of(i):
        return tok_s[CORES * i : CORES * (i + 1)].reshape(chunk, width).astype(F32)

    for i, span in enumerate(spans):
        hat, rstd = norm_parts(tokens_of(i))
        hat1_s[span] = hat
        rstd1_s[span] = jnp.broadcast_to(rstd, hat.shape)
        norm1 = (hat * again_row + abias_row).astype(BF16)
        norm1_s[span] = norm1
        qkv_s[span] = mm(norm1, qkv_w[...]).astype(BF16)

    key_step = lax.broadcasted_iota(jnp.int32, (ctx, 1), 0) // half_tok
    def trunk_rows(s):
        mine = pl.ds(s * ctx, ctx)
        return (qkv_s[mine, width * j : width * (j + 1)] for j in range(3))

    def trunk_scores(s):
        query, key, _ = trunk_rows(s)
        dead = jnp.where(key_step < steps_ref[base + s], 0.0, -1e30).astype(F32)
        tprob_s[s] = mm_bt(key, spread(query, tmask_low)) * scale + dead

    def trunk_softmax(s):
        prob = softmax_rows(tprob_s[s])
        tprob_s[s] = prob
        tlow_s[s] = prob.astype(BF16)

    def trunk_values(s):
        _, _, value = trunk_rows(s)
        att_s[pl.ds(s * ctx, ctx)] = fold(mm_at(tlow_s[s], value), tmask).astype(BF16)

    staged(n, trunk_scores, trunk_softmax, trunk_values)

    for load in loads[9:]:
        load.wait()
    row_step = lax.broadcasted_iota(jnp.int32, (ctx, 1), 0) // half_tok
    mgain_sum = jnp.zeros((1, width), F32)
    mbias_sum = jnp.zeros((1, width), F32)
    downb_sum = jnp.zeros((1, width), F32)
    upb_sum = jnp.zeros((1, ffw), F32)
    for i, span in enumerate(spans):
        middle = tokens_of(i) + mm(att_s[span], aproj[...])
        hat, rstd = norm_parts(middle)
        hat2_s[span] = hat
        rstd2_s[span] = jnp.broadcast_to(rstd, hat.shape)
        norm2 = (hat * mgain_row + mbias_row).astype(BF16)
        norm2_s[span] = norm2
        act, dact = gelu_parts(mm(norm2, up_w[...]) + upb_row)
        act_low = act.astype(BF16)
        up_s[span] = act_low
        live = jnp.concatenate(
            [
                jnp.where(row_step < steps_ref[base + CORES * i + j], 1.0, 0.0).astype(F32)
                for j in range(CORES)
            ],
            axis=0,
        )
        result = (middle + mm(act_low, down_w[...]) + downb_row) * live
        blk_s[CORES * i : CORES * (i + 1)] = result.astype(BF16).reshape(CORES, steps, half_tok, width)
        grad = g_s[CORES * i : CORES * (i + 1)].reshape(chunk, width).astype(F32) * live
        grad_low = grad.astype(BF16)
        glow_s[span] = grad_low
        downb_sum += jnp.sum(grad, axis=0, keepdims=True)
        grad_up = mm_bt(grad_low, down_w[...]).astype(BF16).astype(F32)
        grad_pre = (grad_up * dact).astype(BF16)
        gpre_s[span] = grad_pre
        upb_sum += jnp.sum(grad_pre.astype(F32), axis=0, keepdims=True)
        grad_norm2 = mm_bt(grad_pre, up_w[...]).astype(BF16).astype(F32)
        mgain_sum += jnp.sum(grad_norm2 * hat, axis=0, keepdims=True)
        mbias_sum += jnp.sum(grad_norm2, axis=0, keepdims=True)
        grad_mid = norm_grad(grad_norm2, mgain_row, hat, rstd) + grad
        gn2_s[span] = grad_mid
        grad_mid_low = grad_mid.astype(BF16)
        gmid_s[span] = grad_mid_low
        gatt_s[span] = mm_bt(grad_mid_low, aproj[...]).astype(BF16)
    put("aproj", 0, mm_at(att_s[...], gmid_s[...]))
    put("down", 0, mm_at(up_s[...], glow_s[...]))
    for j in range(ffw // width):
        cols = slice(width * j, width * (j + 1))
        put("up", width * j, mm_at(norm2_s[...], gpre_s[:, cols]))

    def trunk_back_probs(s):
        _, _, value = trunk_rows(s)
        grad_spread = spread(gatt_s[pl.ds(s * ctx, ctx)], tmask_low)
        gprob_s[s] = mm_bt(value, grad_spread)
        gqkv_s[pl.ds(s * ctx, ctx), 2 * width :] = mm(tlow_s[s], grad_spread).astype(BF16)

    def trunk_back_softmax(s):
        grad_prob = gprob_s[s].astype(BF16).astype(F32)
        tlow_s[s] = (softmax_rows_grad(tprob_s[s], grad_prob) * scale).astype(BF16)

    def trunk_back_rows(s):
        query, key, _ = trunk_rows(s)
        mine = pl.ds(s * ctx, ctx)
        gqkv_s[mine, :width] = fold(mm_at(tlow_s[s], key), tmask).astype(BF16)
        gqkv_s[mine, width : 2 * width] = mm(tlow_s[s], spread(query, tmask_low)).astype(BF16)

    staged(n, trunk_back_probs, trunk_back_softmax, trunk_back_rows)

    again_sum = jnp.zeros((1, width), F32)
    abias_sum = jnp.zeros((1, width), F32)
    for i, span in enumerate(spans):
        grad_norm1 = mm_bt(gqkv_s[span], qkv_w[...]).astype(BF16).astype(F32)
        hat = hat1_s[span]
        again_sum += jnp.sum(grad_norm1 * hat, axis=0, keepdims=True)
        abias_sum += jnp.sum(grad_norm1, axis=0, keepdims=True)
        grad_tok = norm_grad(grad_norm1, again_row, hat, rstd1_s[span]) + gn2_s[span]
        gtok_s[CORES * i : CORES * (i + 1)] = grad_tok.astype(BF16).reshape(CORES, steps, half_tok, width)
    for j in range(3):
        cols = slice(width * j, width * (j + 1))
        put("qkv", width * j, mm_at(norm1_s[...], gqkv_s[:, cols]))
    vectors = [again_sum, abias_sum, mgain_sum, mbias_sum, downb_sum]
    vectors += [upb_sum[:, width * j : width * (j + 1)] for j in range(ffw // width)]
    vectors += [jnp.zeros((16 - len(vectors), width), F32)]
    put("vectors", 0, jnp.concatenate(vectors, axis=0))

    for s, e in enumerate(embs):
        grad_prop = gtok_s[s, :, qry:].reshape(steps * ptok, width)
        mixacc_s[e] += mm_at(act_s[s], grad_prop)
        grad_act = mm_bt(grad_prop, mix_w[e]).astype(BF16).astype(F32)
        grad_lift = (grad_act * dact_s[s]).astype(BF16)
        liftacc_s[e] += mm_at(p_s[s].reshape(steps * ptok, -1), grad_lift)
        prp_s[s] = mm_bt(grad_lift, lift_w[e]).astype(BF16).reshape(steps, ptok, -1)

    grad_img = gtok_s[:, :, :qry].reshape(n * steps * qry, width)
    put("stem", 0, mm_at(satt_s[...].reshape(n * steps * qry, width), grad_img))
    gsatt_s[...] = mm_bt(grad_img, stem_proj[...]).astype(BF16).reshape(n, steps, qry, width)

    def stem_back_values(s):
        spreads = [spread(gsatt_s[s, t], smask_low) for t in range(steps)]
        grad_spread = jnp.concatenate(spreads, axis=0)
        ab_s[s, :, : 2 * width] = mm_bt(value_w[embs[s]], grad_spread).astype(BF16)
        ab_s[s, :, 2 * width :] = a_s[embs[s]]
        vacc_s[embs[s]] += mm(ut_s[s], grad_spread)

    def stem_back_probs(s):
        both = mm(x_s[s], ab_s[s, :, : 2 * width])
        sgrad_s[s] = jnp.where(first_step, both[:, :width], both[:, width:])

    def stem_back_softmax(s):
        grad_prob = sgrad_s[s].astype(BF16).astype(F32)
        mix_s[s, :, 2 * width :] = softmax_lines_grad(prob_s[s], grad_prob).astype(BF16)

    def stem_back_moments(s):
        macc_s[embs[s]] += mm(xt_s[s], mix_s[s, :, 2 * width :])

    def image_gradient(s):
        img_s[pl.ds(s, tall, stride=n)] = mm_bt(mix_s[s], ab_s[s])

    staged(n, stem_back_values, stem_back_probs, stem_back_softmax, stem_back_moments, image_gradient)

    for e in range(emb):
        moment = (macc_s[e] * scale).astype(BF16)
        put("keyw", width * e, mm(moment, qs_s[e]))
        put("queries", qry * e, fold(mm_at(moment, key_w[e]), smask))
        put("valuew", width * e, vacc_s[e])
        put("mixer", width * e, mixacc_s[e])
        put("lift", liftacc_s.shape[1] * e, liftacc_s[e])
    other = 1 - sec
    half = own_half()
    image = img_s.reshape(tall // steps, steps, n, width)
    stores = (
        (image.at[pl.ds(0, keys), sec], image_out),
        (image.at[pl.ds(0, keys), other], image_send),
        (blk_s.at[:, sec], block_out),
        (blk_s.at[:, other], block_send),
        (prp_s.at[:, sec], prop_out),
        (prp_s.at[:, other], prop_send),
        (pack_s.at[half, pl.ds(0, 2)], keep0),
        (pack_s.at[half, pl.ds(2, 2)], keep1),
        (pack_s.at[1 - half, pl.ds(0, 2)], send0),
        (pack_s.at[1 - half, pl.ds(2, 2)], send1),
    )
    stores = [pltpu.make_async_copy(a, b, out_sem.at[i]) for i, (a, b) in enumerate(stores)]
    for copy in stores:
        copy.start()
    for copy in stores:
        copy.wait()


def rows_of(images):
    return images.transpose(0, 2, 1, 3).reshape(-1, images.shape[-1])


def compute(args, table, total):
    images, proprio, view_mask, embodiment, ctx_steps = args[:5]
    weights, out_grad = args[5:21], args[21]
    samples, steps, keys, width = images.shape
    ptok, feats = proprio.shape[2:]
    emb, qry = weights[0].shape[:2]
    ffw = weights[12].shape[1]
    n = samples // CORES
    half_tok = qry + ptok
    ctx = steps * half_tok
    rows = n * ctx
    piece = total // (CORES * PIECES)
    lines = steps * keys
    tall = (lines + 15) // 16 * 16
    dims = (n, steps, keys, width, qry, ptok, emb, ffw, table, view_mask.shape[1])

    def low(*shape):
        return pltpu.VMEM(shape, BF16)

    def full(*shape):
        return pltpu.VMEM(shape, F32)

    held = [0, 1, 2, 3, 4, 5, 8, 9, 12, 14]
    scratch = [low(*weights[i].shape) for i in held]
    scratch += [
        low((n * lines + 31) // 16 * 16, width),
        low(n, tall, width),
        low(n, steps, ptok, feats),
        low(n, ctx, width),
        low(emb, HEADS * qry, width),
        low(emb, width, HEADS * qry),
        low(n, steps, half_tok, width),
        low(n, width, tall),
        full(n, tall, HEADS * qry),
        full(n, tall, HEADS * qry),
        low(n, tall, (steps + 1) * width),
        low(n, width, (steps + 1) * width),
        low(n, width, steps * width),
        low(n, steps, qry, width),
        low(n, steps * ptok, width),
        full(n, steps * ptok, width),
        full(rows, width),
        full(rows, width),
        low(rows, width),
        low(rows, 3 * width),
        full(n, ctx, HEADS * ctx),
        low(n, ctx, HEADS * ctx),
        full(n, ctx, HEADS * ctx),
        low(rows, width),
        full(rows, width),
        full(rows, width),
        low(rows, width),
        low(rows, ffw),
        low(rows, width),
        low(rows, ffw),
        full(rows, width),
        low(rows, width),
        low(rows, width),
        low(rows, 3 * width),
        low(n, steps, half_tok, width),
        low(n, steps, qry, width),
        low(n, steps, half_tok, width),
        full(tall * n, width),
        low(n, steps, ptok, feats),
        full(emb, width, HEADS * qry),
        full(emb, width, width),
        full(emb, width, width),
        full(emb, feats, width),
        low(CORES, PIECES, piece, width),
        pltpu.SemaphoreType.DMA((13,)),
        pltpu.SemaphoreType.DMA((10,)),
    ]
    shape = jax.ShapeDtypeStruct
    return pl.pallas_call(
        functools.partial(compute_kernel, dims),
        out_shape=(
            shape((2, piece, width), BF16),
            shape((2, piece, width), BF16),
            shape((2, piece, width), BF16),
            shape((2, piece, width), BF16),
            shape((n, half_tok, width), BF16),
            shape((n, half_tok, width), BF16),
            shape((keys, n, width), F32),
            shape((keys, n, width), F32),
            shape((n, ptok, feats), BF16),
            shape((n, ptok, feats), BF16),
        ),
        in_specs=[SMEM] * 3 + [ANY] * 3 + [ANY if i in held else VMEM for i in range(16)],
        out_specs=(ANY,) * 10,
        scratch_shapes=scratch,
        compiler_params=pltpu.CompilerParams(vmem_limit_bytes=56 * 2**20),
        name="stem_trunk",
    )(embodiment, ctx_steps, view_mask.T, rows_of(images), proprio, out_grad, *weights)


def parity(index, levels):
    total = index & 1
    for level in range(1, levels):
        total = total ^ ((index >> level) & 1)
    return total


def own_half():
    levels = lax.axis_size("dp").bit_length() - 1
    return lax.axis_index("section") ^ parity(lax.axis_index("dp"), levels)


def own_bits(half):
    dp = lax.axis_index("dp")
    low, high = dp & 1, (dp >> 1) & 1
    return jnp.where(half == 0, low, high), jnp.where(half == 0, high, low)


def select(bit, low, high):
    return jnp.where(bit == 0, low, high)


def add(held, came):
    return (held.astype(F32) + came.astype(F32)).astype(BF16)


def swap_cores(value):
    return lax.ppermute(value, "section", [(0, 1), (1, 0)])


def swap_chips(value, bits):
    count = lax.axis_size("dp")
    levels = count.bit_length() - 1
    pairs = []
    for core in range(CORES):
        for i in range(count):
            bit = bits[core ^ parity(i, levels)]
            pairs.append((core * count + i, (1 - core) * count + (i ^ (1 << bit))))
    return lax.ppermute(value, ("section", "dp"), pairs)


def join(own, came, axis):
    first = lax.axis_index("section") == 0
    return jnp.where(first, jnp.concatenate([own, came], axis), jnp.concatenate([came, own], axis))


def unpack_kernel(table, *refs):
    pieces, outs, (pack, sem) = refs[:8], refs[8:-2], refs[-2:]
    own = own_half()
    copies = []
    for i, ref in enumerate(pieces):
        half = own if i < PIECES else 1 - own
        first = own_bits(half)[0]
        chain, far = i % CHAINS, i // CHAINS % 2
        at = half * PIECES + chain * 2 + (first ^ far)
        copies.append(pltpu.make_async_copy(ref, pack.at[at], sem.at[i]))
    for copy in copies:
        copy.start()
    for copy in copies:
        copy.wait()
    piece = pack.shape[1]

    def get(name, row, count, store):
        for at, lo, done, size in cuts(table[name][0] + row, count, piece):
            store(done, size, pack[at, lo : lo + size].astype(F32))

    def flat(ref, name):
        def store(done, size, value):
            ref[done : done + size] = value

        get(name, 0, ref.shape[0], store)

    def stacked(ref, name):
        for e in range(ref.shape[0]):

            def store(done, size, value, e=e):
                ref[e, done : done + size] = value

            get(name, e * ref.shape[1], ref.shape[1], store)

    def blocks(ref, name):
        depth, width = ref.shape[0], pack.shape[2]
        for j in range(ref.shape[1] // width):

            def store(done, size, value, j=j):
                ref[done : done + size, width * j : width * (j + 1)] = value

            get(name, j * depth, depth, store)

    q, k, v, stem, lift, mix, again, abias, qkv, aproj, mgain, mbias, up, upb, down, downb = outs
    for ref, name in ((q, "queries"), (k, "keyw"), (v, "valuew"), (lift, "lift"), (mix, "mixer")):
        stacked(ref, name)
    for ref, name in ((stem, "stem"), (aproj, "aproj"), (down, "down")):
        flat(ref, name)
    for ref, name in ((qkv, "qkv"), (up, "up")):
        blocks(ref, name)
    at, lo, _, _ = next(cuts(table["vectors"][0], 16, piece))
    vectors = pack[at, lo : lo + 16].astype(F32)
    width = pack.shape[2]
    for i, ref in enumerate((again, abias, mgain, mbias, downb)):
        ref[...] = vectors[i]
    for j in range(upb.shape[0] // width):
        upb[width * j : width * (j + 1)] = vectors[5 + j]


def unpack(pieces, table, shapes):
    return pl.pallas_call(
        functools.partial(unpack_kernel, table),
        out_shape=tuple(jax.ShapeDtypeStruct(s, F32) for s in shapes),
        in_specs=[ANY] * 8,
        out_specs=(VMEM,) * len(shapes),
        scratch_shapes=[
            pltpu.VMEM((CORES * PIECES,) + pieces[0].shape, BF16),
            pltpu.SemaphoreType.DMA((8,)),
        ],
        compiler_params=pltpu.CompilerParams(vmem_limit_bytes=32 * 2**20),
        name="unpack",
    )(*pieces)


def sum_chips(held, came):
    levels = lax.axis_size("dp").bit_length() - 1
    first, second = (0, 1), (1, 0)
    one, two = own_bits(own_half())
    totals = [add(a, b) for a, b in zip(held, came)]
    for bit, bits in ((one, first), (two, second)):
        split = [t.reshape((2, -1, t.shape[-1])) for t in totals]
        sent = [swap_chips(select(bit, t[1], t[0]), bits) for t in split]
        totals = [add(select(bit, t[0], t[1]), c) for t, c in zip(split, sent)]
    for bits in zip(range(2, levels), reversed(range(2, levels))):
        sent = [swap_chips(t, bits) for t in totals]
        totals = [add(t, c) for t, c in zip(totals, sent)]
    sent = [swap_chips(t, second) for t in totals]
    near = [
        select(two, jnp.concatenate([t, c]), jnp.concatenate([c, t])) for t, c in zip(totals, sent)
    ]
    far = [swap_chips(t, first) for t in near]
    return tuple(near) + tuple(far)


def per_device(*args):
    weights = args[5:21]
    emb, qry, width = weights[0].shape
    table, total = layout(width, weights[12].shape[1], emb, qry, weights[4].shape[1])
    *packed, blk, blk_s, img, img_s, prp, prp_s = compute(args, table, total)
    keep, send = packed[:CHAINS], packed[CHAINS:]
    came = [swap_cores(v) for v in send]
    blk_r, img_r, prp_r = (swap_cores(v) for v in (blk_s, img_s, prp_s))
    pieces = sum_chips(keep, came)
    pieces += tuple(swap_cores(v) for v in pieces)
    blk = join(blk, blk_r, 0)
    prp = join(prp, prp_r, 0)[:, None]
    img = join(img, img_r, 1).astype(BF16).transpose(1, 0, 2)[:, None]
    grads = unpack(pieces, table, [w.shape for w in weights])
    return (blk, img, prp) + tuple(grads)


def solution(mesh):
    sample = [P("dp")] * 5
    return jax.shard_map(
        per_device,
        mesh=mesh,
        in_specs=tuple(sample + [P()] * 16 + [P("dp")]),
        out_specs=(P("dp", "section"),) * 3 + (P(),) * 16,
        check_vma=False,
    )
```

```python
import functools
import math

import jax
import jax.numpy as jnp
from jax import lax
from jax.experimental import pallas as pl
from jax.experimental.pallas import tpu as pltpu
from jax.sharding import PartitionSpec as P

HEADS = 8
F32 = jnp.float32
BF16 = jnp.bfloat16
CORES = 2
CHAINS = 2
PIECES = 2 * CHAINS
EPS = 1e-05
INV_SQRT2 = 1.0 / math.sqrt(2.0)
INV_SQRT2PI = 1.0 / math.sqrt(2.0 * math.pi)
ANY = pl.BlockSpec(memory_space=pl.ANY)
VMEM = pl.BlockSpec(memory_space=pltpu.VMEM)
SMEM = pl.BlockSpec(memory_space=pltpu.SMEM)


def mm(left, right):
    return lax.dot_general(left, right, (((1,), (0,)), ((), ())), preferred_element_type=F32)


def mm_bt(left, right):
    return lax.dot_general(left, right, (((1,), (1,)), ((), ())), preferred_element_type=F32)


def mm_at(left, right):
    return lax.dot_general(left, right, (((0,), (0,)), ((), ())), preferred_element_type=F32)


def layout(width, ffw, emb, queries, feats):
    counts = (
        ("keyw", emb * width),
        ("valuew", emb * width),
        ("mixer", emb * width),
        ("stem", width),
        ("lift", emb * feats),
        ("queries", emb * queries),
        ("qkv", 3 * width),
        ("aproj", width),
        ("up", ffw),
        ("down", ffw),
        ("vectors", 16),
    )
    table, first = {}, 0
    for name, rows in counts:
        table[name] = (first, rows)
        first += rows
    step = CORES * PIECES * 32
    return table, (first + step - 1) // step * step


def cuts(first, rows, piece):
    done = 0
    while done < rows:
        at = first + done
        count = min(rows - done, piece - at % piece)
        yield at // piece, at % piece, done, count
        done += count


def head_mask(rows, per_head, width):
    row = lax.broadcasted_iota(jnp.int32, (rows, width), 0) // per_head
    col = lax.broadcasted_iota(jnp.int32, (rows, width), 1) // (width // HEADS)
    return (row == col).astype(F32)


def spread(rows, mask):
    return jnp.concatenate([rows] * HEADS, axis=0) * mask


def fold(full, mask):
    per = full.shape[0] // HEADS
    return jnp.sum((full * mask).reshape(HEADS, per, full.shape[1]), axis=0)


def gelu_parts(values):
    cdf = 0.5 * (1.0 + lax.erf(values * INV_SQRT2))
    pdf = INV_SQRT2PI * jnp.exp(-0.5 * values * values)
    return values * cdf, cdf + values * pdf


def staged(count, *stages):
    for step in range(count + len(stages) - 1):
        for lag, stage in enumerate(stages):
            if 0 <= step - lag < count:
                stage(step - lag)


def softmax_rows(scores):
    expo = jnp.exp(scores - jnp.max(scores, axis=0, keepdims=True))
    return expo / jnp.sum(expo, axis=0, keepdims=True)


def per_step(row, reduce):
    part = reduce(row.reshape(-1, 8, row.shape[1]), axis=0)
    pair = jnp.maximum if reduce is jnp.max else jnp.add
    part = pair(part, pltpu.roll(part, 4, 0))
    return pair(part, pltpu.roll(part, 2, 0))


def softmax_lines(scores):
    expo = jnp.exp(scores.reshape(-1, 8, scores.shape[1]) - per_step(scores, jnp.max))
    return (expo * (1.0 / per_step(expo.reshape(scores.shape), jnp.sum))).reshape(scores.shape)


def softmax_lines_grad(probs, grad):
    terms = probs * grad
    total = per_step(terms, jnp.sum)
    tiles = (-1, 8, probs.shape[1])
    return (terms.reshape(tiles) - probs.reshape(tiles) * total).reshape(probs.shape)


def softmax_rows_grad(probs, grad):
    terms = probs * grad
    return terms - probs * jnp.sum(terms, axis=0, keepdims=True)


def norm_parts(values):
    center = values - jnp.mean(values, axis=-1, keepdims=True)
    rstd = lax.rsqrt(jnp.mean(center * center, axis=-1, keepdims=True) + EPS)
    return center * rstd, rstd


def norm_grad(grad, gain, hat, rstd):
    scaled = grad * gain
    first = jnp.mean(scaled, axis=-1, keepdims=True)
    second = jnp.mean(scaled * hat, axis=-1, keepdims=True)
    return rstd * (scaled - first - hat * second)


def compute_kernel(
    dims,
    emb_h,
    steps_h,
    views_h,
    images,
    proprio,
    out_grad,
    queries_h,
    key_h,
    value_h,
    stem_h,
    lift_h,
    mix_h,
    again_h,
    abias_h,
    qkv_h,
    aproj_h,
    mgain_h,
    mbias_h,
    up_h,
    up_bh,
    down_h,
    down_bh,
    keep0,
    keep1,
    send0,
    send1,
    block_out,
    block_send,
    image_out,
    image_send,
    prop_out,
    prop_send,
    emb_ref,
    steps_ref,
    views_ref,
    queries,
    key_w,
    value_w,
    stem_proj,
    lift_w,
    mix_w,
    again,
    abias,
    qkv_w,
    aproj,
    mgain,
    mbias,
    up_w,
    up_b,
    down_w,
    down_b,
    xin_s,
    x_s,
    p_s,
    g_s,
    qs_s,
    a_s,
    tok_s,
    xt_s,
    prob_s,
    sgrad_s,
    mix_s,
    ab_s,
    ut_s,
    satt_s,
    act_s,
    dact_s,
    hat1_s,
    rstd1_s,
    norm1_s,
    qkv_s,
    tprob_s,
    tlow_s,
    gprob_s,
    att_s,
    mid_s,
    pre_s,
    hat2_s,
    rstd2_s,
    norm2_s,
    up_s,
    glow_s,
    gpre_s,
    gn2_s,
    gmid_s,
    gatt_s,
    gqkv_s,
    gtok_s,
    gsatt_s,
    blk_s,
    img_s,
    prp_s,
    macc_s,
    vacc_s,
    pack_s,
    in_sem,
):
    n, steps, keys, width, qry, ptok, emb, ffw, table, views = dims
    half_tok = qry + ptok
    ctx = steps * half_tok
    rows = n * ctx
    scale = 1.0 / math.sqrt(width // HEADS)
    piece = pack_s.shape[2]
    sec = lax.axis_index("section")
    base = sec * n
    lines = steps * keys
    tall = x_s.shape[1]
    def put(name, row, value):
        first = table[name][0] + row
        for at, lo, done, count in cuts(first, value.shape[0], piece):
            pack_s[at // PIECES, at % PIECES, lo : lo + count] = value[done : done + count].astype(BF16)

    sources = (
        (emb_h, emb_ref),
        (queries_h, queries),
        (key_h, key_w),
        (images.at[pl.ds(pl.multiple_of(sec * n * lines, 16), n * lines)], xin_s.at[pl.ds(0, n * lines)]),
        (views_h, views_ref),
        (value_h, value_w),
        (proprio.at[pl.ds(base, n)], p_s),
        (lift_h, lift_w),
        (mix_h, mix_w),
        (stem_h, stem_proj),
        (again_h, again),
        (abias_h, abias),
        (qkv_h, qkv_w),
        (steps_h, steps_ref),
        (aproj_h, aproj),
        (mgain_h, mgain),
        (mbias_h, mbias),
        (up_h, up_w),
        (up_bh, up_b),
        (down_h, down_w),
        (down_bh, down_b),
        (out_grad.at[pl.ds(base, n)], g_s),
    )
    loads = [pltpu.make_async_copy(a, b, in_sem.at[i]) for i, (a, b) in enumerate(sources)]
    for copy in loads:
        copy.start()
    waited = [0]

    def ready(count):
        for copy in loads[waited[0] : count]:
            copy.wait()
        waited[0] = max(waited[0], count)

    smask = head_mask(HEADS * qry, qry, width)
    smask_low = smask.astype(BF16)
    tmask = head_mask(HEADS * ctx, ctx, width)
    tmask_low = tmask.astype(BF16)
    for e in range(emb):
        macc_s[e] = jnp.zeros((width, width), F32)
        vacc_s[e] = jnp.zeros((width, width), F32)
    used = max(first + count for first, count in table.values())
    for at, lo, _, count in cuts(used, CORES * PIECES * piece - used, piece):
        pack_s[at // PIECES, at % PIECES, lo : lo + count] = jnp.zeros((count, width), BF16)
    xin_s[n * lines :] = jnp.zeros((xin_s.shape[0] - n * lines, width), BF16)
    ready(3)
    embs = [emb_ref[base + s] for s in range(n)]
    for e in range(emb):
        qs = spread(queries[e], smask_low)
        qs_s[e] = qs
        a_s[e] = (mm_bt(key_w[e], qs) * scale).astype(BF16)

    ready(4)
    edge = lines // 16 * 16
    inside = lax.broadcasted_iota(jnp.int32, (tall - edge, width), 0) < lines - edge
    for s in range(n):
        x_s[s] = xin_s[lines * s : lines * s + tall]
        last = x_s[s, edge:].astype(F32)
        x_s[s, edge:] = jnp.where(inside, last, 0.0).astype(BF16)

    first_step = lax.broadcasted_iota(jnp.int32, (tall, width), 0) % steps == 0

    def view_bias(s):
        lost = [jnp.where(views_ref[v, base + s] > 0, 0.0, -1e30).astype(F32) for v in range(views)]
        lost.append(jnp.float32(-1e30))
        ends = [lines // views * (v + 1) for v in range(views)]
        tiles, at = [], 0
        while at < tall:
            view = sum(at >= end for end in ends)
            stop = min([end // 8 * 8 for end in ends if end // 8 * 8 > at] + [tall])
            if view < views and ends[view] < at + 8:
                row = lax.broadcasted_iota(jnp.int32, (8, width), 0)
                tiles.append(jnp.where(row < ends[view] - at, lost[view], lost[view + 1]))
                at += 8
            else:
                tiles.append(jnp.full((stop - at, width), lost[view], F32))
                at = stop
        return jnp.concatenate(tiles, axis=0)

    def stem_scores(s):
        prob_s[s] = mm(x_s[s], a_s[embs[s]]) + view_bias(s)

    def stem_softmax(s):
        prob = softmax_lines(prob_s[s])
        prob_s[s] = prob
        mix_s[s, :, :width] = jnp.where(first_step, prob, 0.0).astype(BF16)
        mix_s[s, :, width : 2 * width] = jnp.where(first_step, 0.0, prob).astype(BF16)

    def stem_moments(s):
        turned = x_s[s].T
        xt_s[s] = turned
        ut_s[s] = mm(turned, mix_s[s, :, : 2 * width]).astype(BF16)

    def stem_values(s):
        values = mm(ut_s[s].T, value_w[embs[s]])
        for t in range(steps):
            satt_s[s, t] = fold(values[width * t : width * (t + 1)], smask).astype(BF16)

    ready(6)
    staged(n, stem_scores, stem_softmax, stem_moments, stem_values)
    ready(9)
    emb_rows = jnp.concatenate([jnp.full((steps * ptok, width), e) for e in embs], axis=0)
    lift_cat = jnp.concatenate([lift_w[e] for e in range(emb)], axis=1)
    mix_cat = jnp.concatenate([mix_w[e] for e in range(emb)], axis=1)

    def own_columns(values):
        result = values[:, :width]
        for e in range(1, emb):
            result = jnp.where(emb_rows == e, values[:, width * e : width * (e + 1)], result)
        return result

    def spread_columns(values):
        parts = [jnp.where(emb_rows == e, values, 0.0).astype(BF16) for e in range(emb)]
        return jnp.concatenate(parts, axis=1)

    prop_rows = p_s[...].reshape(n * steps * ptok, -1)
    act, dact = gelu_parts(own_columns(mm(prop_rows, lift_cat)))
    act_s[...] = act.astype(BF16)
    dact_s[...] = dact
    prop_tok = own_columns(mm(act_s[...], mix_cat)).astype(BF16)
    tok_s[:, :, qry:] = prop_tok.reshape(n, steps, ptok, width)

    ready(10)
    image_tok = mm(satt_s[...].reshape(n * steps * qry, width), stem_proj[...])
    tok_s[:, :, :qry] = image_tok.astype(BF16).reshape(n, steps, qry, width)

    ready(len(loads))
    chunk = CORES * ctx
    spans = [pl.ds(i * chunk, chunk) for i in range(rows // chunk)]
    again_row = again[...].astype(F32).reshape(1, width)
    abias_row = abias[...].astype(F32).reshape(1, width)
    mgain_row = mgain[...].astype(F32).reshape(1, width)
    mbias_row = mbias[...].astype(F32).reshape(1, width)
    upb_row = up_b[...].astype(F32).reshape(1, ffw)
    downb_row = down_b[...].astype(F32).reshape(1, width)

    def tokens_of(i):
        return tok_s[CORES * i : CORES * (i + 1)].reshape(chunk, width).astype(F32)

    for i, span in enumerate(spans):
        hat, rstd = norm_parts(tokens_of(i))
        hat1_s[span] = hat
        rstd1_s[span] = jnp.broadcast_to(rstd, hat.shape)
        norm1 = (hat * again_row + abias_row).astype(BF16)
        norm1_s[span] = norm1
        qkv_s[span] = mm(norm1, qkv_w[...]).astype(BF16)

    key_step = lax.broadcasted_iota(jnp.int32, (ctx, 1), 0) // half_tok
    def trunk_rows(s):
        mine = pl.ds(s * ctx, ctx)
        return (qkv_s[mine, width * j : width * (j + 1)] for j in range(3))

    def trunk_scores(s):
        query, key, _ = trunk_rows(s)
        dead = jnp.where(key_step < steps_ref[base + s], 0.0, -1e30).astype(F32)
        tprob_s[s] = mm_bt(key, spread(query, tmask_low)) * scale + dead

    def trunk_softmax(s):
        prob = softmax_rows(tprob_s[s])
        tprob_s[s] = prob
        tlow_s[s] = prob.astype(BF16)

    def trunk_values(s):
        _, _, value = trunk_rows(s)
        att_s[pl.ds(s * ctx, ctx)] = fold(mm_at(tlow_s[s], value), tmask).astype(BF16)

    staged(n, trunk_scores, trunk_softmax, trunk_values)

    row_step = lax.broadcasted_iota(jnp.int32, (ctx, 1), 0) // half_tok
    sums = {name: jnp.zeros((1, width), F32) for name in ("mgain", "mbias", "downb")}
    sums["upb"] = jnp.zeros((1, ffw), F32)

    def total(name, values):
        sums[name] += jnp.sum(values, axis=0, keepdims=True)

    def live_rows(i):
        parts = [row_step < steps_ref[base + CORES * i + j] for j in range(CORES)]
        return jnp.concatenate([jnp.where(part, 1.0, 0.0).astype(F32) for part in parts], axis=0)

    def mlp_in(i):
        span = spans[i]
        middle = tokens_of(i) + mm(att_s[span], aproj[...])
        mid_s[span] = middle
        hat, rstd = norm_parts(middle)
        hat2_s[span] = hat
        rstd2_s[span] = jnp.broadcast_to(rstd, hat.shape)
        norm2 = (hat * mgain_row + mbias_row).astype(BF16)
        norm2_s[span] = norm2
        pre_s[span] = mm(norm2, up_w[...]) + upb_row

    def mlp_gelu(i):
        span = spans[i]
        act, dact = gelu_parts(pre_s[span])
        up_s[span] = act.astype(BF16)
        pre_s[span] = dact

    def mlp_back(i):
        span = spans[i]
        grad = g_s[CORES * i : CORES * (i + 1)].reshape(chunk, width).astype(F32) * live_rows(i)
        grad_low = grad.astype(BF16)
        glow_s[span] = grad_low
        total("downb", grad)
        grad_up = mm_bt(grad_low, down_w[...]).astype(BF16).astype(F32)
        grad_pre = (grad_up * pre_s[span]).astype(BF16)
        gpre_s[span] = grad_pre
        total("upb", grad_pre.astype(F32))

    def mlp_norm_back(i):
        span = spans[i]
        grad_norm2 = mm_bt(gpre_s[span], up_w[...]).astype(BF16).astype(F32)
        hat = hat2_s[span]
        total("mgain", grad_norm2 * hat)
        total("mbias", grad_norm2)
        grad_mid = norm_grad(grad_norm2, mgain_row, hat, rstd2_s[span]) + glow_s[span].astype(F32)
        gn2_s[span] = grad_mid
        grad_mid_low = grad_mid.astype(BF16)
        gmid_s[span] = grad_mid_low
        gatt_s[span] = mm_bt(grad_mid_low, aproj[...]).astype(BF16)

    def mlp_out(i):
        span = spans[i]
        result = (mid_s[span] + mm(up_s[span], down_w[...]) + downb_row) * live_rows(i)
        blk_s[CORES * i : CORES * (i + 1)] = result.astype(BF16).reshape(CORES, steps, half_tok, width)

    staged(len(spans), mlp_in, mlp_gelu, mlp_back, mlp_norm_back, mlp_out)

    put("aproj", 0, mm_at(att_s[...], gmid_s[...]))
    down = mm_at(glow_s[...], up_s[...]).astype(BF16)
    up = mm_at(norm2_s[...], gpre_s[...])
    for j in range(ffw // width):
        cols = slice(width * j, width * (j + 1))
        put("down", width * j, down[:, cols].T)
        put("up", width * j, up[:, cols])

    def trunk_back_probs(s):
        _, _, value = trunk_rows(s)
        grad_spread = spread(gatt_s[pl.ds(s * ctx, ctx)], tmask_low)
        gprob_s[s] = mm_bt(value, grad_spread)
        gqkv_s[pl.ds(s * ctx, ctx), 2 * width :] = mm(tlow_s[s], grad_spread).astype(BF16)

    def trunk_back_softmax(s):
        grad_prob = gprob_s[s].astype(BF16).astype(F32)
        tlow_s[s] = (softmax_rows_grad(tprob_s[s], grad_prob) * scale).astype(BF16)

    def trunk_back_rows(s):
        query, key, _ = trunk_rows(s)
        mine = pl.ds(s * ctx, ctx)
        gqkv_s[mine, :width] = fold(mm_at(tlow_s[s], key), tmask).astype(BF16)
        gqkv_s[mine, width : 2 * width] = mm(tlow_s[s], spread(query, tmask_low)).astype(BF16)

    staged(n, trunk_back_probs, trunk_back_softmax, trunk_back_rows)

    again_sum = jnp.zeros((1, width), F32)
    abias_sum = jnp.zeros((1, width), F32)
    for i, span in enumerate(spans):
        grad_norm1 = mm_bt(gqkv_s[span], qkv_w[...]).astype(BF16).astype(F32)
        hat = hat1_s[span]
        again_sum += jnp.sum(grad_norm1 * hat, axis=0, keepdims=True)
        abias_sum += jnp.sum(grad_norm1, axis=0, keepdims=True)
        grad_tok = norm_grad(grad_norm1, again_row, hat, rstd1_s[span]) + gn2_s[span]
        gtok_s[CORES * i : CORES * (i + 1)] = grad_tok.astype(BF16).reshape(CORES, steps, half_tok, width)
    qkv = mm_at(norm1_s[...], gqkv_s[...])
    for j in range(3):
        put("qkv", width * j, qkv[:, width * j : width * (j + 1)])
    vectors = [again_sum, abias_sum, sums["mgain"], sums["mbias"], sums["downb"]]
    vectors += [sums["upb"][:, width * j : width * (j + 1)] for j in range(ffw // width)]
    vectors += [jnp.zeros((16 - len(vectors), width), F32)]
    put("vectors", 0, jnp.concatenate(vectors, axis=0))

    grad_prop = spread_columns(gtok_s[:, :, qry:].reshape(n * steps * ptok, width).astype(F32))
    mixer = mm_at(act_s[...], grad_prop)
    grad_act = mm_bt(grad_prop, mix_cat).astype(BF16).astype(F32)
    grad_lift = spread_columns((grad_act * dact_s[...]).astype(BF16).astype(F32))
    lift = mm_at(prop_rows, grad_lift)
    for e in range(emb):
        put("mixer", width * e, mixer[:, width * e : width * (e + 1)])
        put("lift", lift.shape[0] * e, lift[:, width * e : width * (e + 1)])
    prp_s[...] = mm_bt(grad_lift, lift_cat).astype(BF16).reshape(n, steps, ptok, -1)

    grad_img = gtok_s[:, :, :qry].reshape(n * steps * qry, width)
    put("stem", 0, mm_at(satt_s[...].reshape(n * steps * qry, width), grad_img))
    gsatt_s[...] = mm_bt(grad_img, stem_proj[...]).astype(BF16).reshape(n, steps, qry, width)

    def stem_back_values(s):
        spreads = [spread(gsatt_s[s, t], smask_low) for t in range(steps)]
        grad_spread = jnp.concatenate(spreads, axis=0)
        ab_s[s, :, : 2 * width] = mm_bt(value_w[embs[s]], grad_spread).astype(BF16)
        ab_s[s, :, 2 * width :] = a_s[embs[s]]
        vacc_s[embs[s]] += mm(ut_s[s], grad_spread)

    def stem_back_probs(s):
        both = mm(x_s[s], ab_s[s, :, : 2 * width])
        sgrad_s[s] = jnp.where(first_step, both[:, :width], both[:, width:])

    def stem_back_softmax(s):
        grad_prob = sgrad_s[s].astype(BF16).astype(F32)
        mix_s[s, :, 2 * width :] = softmax_lines_grad(prob_s[s], grad_prob).astype(BF16)

    def stem_back_moments(s):
        macc_s[embs[s]] += mm(xt_s[s], mix_s[s, :, 2 * width :])

    def image_gradient(s):
        img_s[pl.ds(s, tall, stride=n)] = mm_bt(mix_s[s], ab_s[s])

    staged(n, stem_back_values, stem_back_probs, stem_back_softmax, stem_back_moments, image_gradient)

    for e in range(emb):
        moment = (macc_s[e] * scale).astype(BF16)
        put("keyw", width * e, mm(moment, qs_s[e]))
        put("queries", qry * e, fold(mm_at(moment, key_w[e]), smask))
        put("valuew", width * e, vacc_s[e])
    other = 1 - sec
    half = own_half()
    image = img_s.reshape(tall // steps, steps, n, width)
    for ref, at in ((image_out, sec), (image_send, other)):
        ref[...] = image[:keys, at]
    for ref, at in ((block_out, sec), (block_send, other)):
        ref[...] = blk_s[:, at]
    for ref, at in ((prop_out, sec), (prop_send, other)):
        ref[...] = prp_s[:, at]
    for ref, at, chain in ((keep0, half, 0), (keep1, half, 1), (send0, 1 - half, 0), (send1, 1 - half, 1)):
        ref[...] = pack_s[at, 2 * chain : 2 * chain + 2]


def rows_of(images):
    return images.transpose(0, 2, 1, 3).reshape(-1, images.shape[-1])


def compute(args, table, total):
    images, proprio, view_mask, embodiment, ctx_steps = args[:5]
    weights, out_grad = args[5:21], args[21]
    samples, steps, keys, width = images.shape
    ptok, feats = proprio.shape[2:]
    emb, qry = weights[0].shape[:2]
    ffw = weights[12].shape[1]
    n = samples // CORES
    half_tok = qry + ptok
    ctx = steps * half_tok
    rows = n * ctx
    piece = total // (CORES * PIECES)
    lines = steps * keys
    tall = (lines + 15) // 16 * 16
    dims = (n, steps, keys, width, qry, ptok, emb, ffw, table, view_mask.shape[1])

    def low(*shape):
        return pltpu.VMEM(shape, BF16)

    def full(*shape):
        return pltpu.VMEM(shape, F32)

    small = (embodiment, ctx_steps, view_mask.T)
    scratch = [pltpu.SMEM(v.shape, v.dtype) for v in small]
    scratch += [low(*w.shape) for w in weights]
    scratch += [
        low((n * lines + 31) // 16 * 16, width),
        low(n, tall, width),
        low(n, steps, ptok, feats),
        low(n, ctx, width),
        low(emb, HEADS * qry, width),
        low(emb, width, HEADS * qry),
        low(n, steps, half_tok, width),
        low(n, width, tall),
        full(n, tall, HEADS * qry),
        full(n, tall, HEADS * qry),
        low(n, tall, (steps + 1) * width),
        low(n, width, (steps + 1) * width),
        low(n, width, steps * width),
        low(n, steps, qry, width),
        low(n * steps * ptok, width),
        full(n * steps * ptok, width),
        full(rows, width),
        full(rows, width),
        low(rows, width),
        low(rows, 3 * width),
        full(n, ctx, HEADS * ctx),
        low(n, ctx, HEADS * ctx),
        full(n, ctx, HEADS * ctx),
        low(rows, width),
        full(rows, width),
        full(rows, ffw),
        full(rows, width),
        full(rows, width),
        low(rows, width),
        low(rows, ffw),
        low(rows, width),
        low(rows, ffw),
        full(rows, width),
        low(rows, width),
        low(rows, width),
        low(rows, 3 * width),
        low(n, steps, half_tok, width),
        low(n, steps, qry, width),
        low(n, steps, half_tok, width),
        full(tall * n, width),
        low(n, steps, ptok, feats),
        full(emb, width, HEADS * qry),
        full(emb, width, width),
        low(CORES, PIECES, piece, width),
        pltpu.SemaphoreType.DMA((22,)),
    ]
    inputs = (*small, rows_of(images), proprio, out_grad, *weights)
    return pl.pallas_call(
        functools.partial(compute_kernel, dims),
        out_shape=(
            low(2, piece, width),
            low(2, piece, width),
            low(2, piece, width),
            low(2, piece, width),
            low(n, half_tok, width),
            low(n, half_tok, width),
            full(keys, n, width),
            full(keys, n, width),
            low(n, ptok, feats),
            low(n, ptok, feats),
        ),
        in_specs=[ANY] * 22,
        out_specs=(VMEM,) * 10,
        scratch_shapes=scratch,
        compiler_params=pltpu.CompilerParams(vmem_limit_bytes=40 * 2**20),
        name="stem_trunk",
    )(*(pltpu.with_memory_space_constraint(v, pltpu.HBM) for v in inputs))


def parity(index, levels):
    total = index & 1
    for level in range(1, levels):
        total = total ^ ((index >> level) & 1)
    return total


def own_half():
    levels = lax.axis_size("dp").bit_length() - 1
    return lax.axis_index("section") ^ parity(lax.axis_index("dp"), levels)


def own_bits(half):
    dp = lax.axis_index("dp")
    low, high = dp & 1, (dp >> 1) & 1
    return jnp.where(half == 0, low, high), jnp.where(half == 0, high, low)


def select(bit, low, high):
    return jnp.where(bit == 0, low, high)


def add(held, came):
    return (held.astype(F32) + came.astype(F32)).astype(BF16)


def swap_cores(value):
    return lax.ppermute(value, "section", [(0, 1), (1, 0)])


def swap_chips(value, bits):
    count = lax.axis_size("dp")
    levels = count.bit_length() - 1
    pairs = []
    for core in range(CORES):
        for i in range(count):
            bit = bits[core ^ parity(i, levels)]
            pairs.append((core * count + i, (1 - core) * count + (i ^ (1 << bit))))
    return lax.ppermute(value, ("section", "dp"), pairs)


def join(own, came, axis):
    first = lax.axis_index("section") == 0
    return jnp.where(first, jnp.concatenate([own, came], axis), jnp.concatenate([came, own], axis))


def unpack_kernel(table, *refs):
    pieces, outs, (pack, sem) = refs[:8], refs[8:-2], refs[-2:]
    own = own_half()
    copies = []
    for i, ref in enumerate(pieces):
        half = own if i < PIECES else 1 - own
        first = own_bits(half)[0]
        chain, far = i % CHAINS, i // CHAINS % 2
        at = half * PIECES + chain * 2 + (first ^ far)
        copies.append(pltpu.make_async_copy(ref, pack.at[at], sem.at[i]))
    for copy in copies:
        copy.start()
    for copy in copies:
        copy.wait()
    piece = pack.shape[1]

    def get(name, row, count, store):
        for at, lo, done, size in cuts(table[name][0] + row, count, piece):
            store(done, size, pack[at, lo : lo + size].astype(F32))

    def flat(ref, name):
        def store(done, size, value):
            ref[done : done + size] = value

        get(name, 0, ref.shape[0], store)

    def stacked(ref, name):
        for e in range(ref.shape[0]):

            def store(done, size, value, e=e):
                ref[e, done : done + size] = value

            get(name, e * ref.shape[1], ref.shape[1], store)

    def blocks(ref, name):
        depth, width = ref.shape[0], pack.shape[2]
        for j in range(ref.shape[1] // width):

            def store(done, size, value, j=j):
                ref[done : done + size, width * j : width * (j + 1)] = value

            get(name, j * depth, depth, store)

    q, k, v, stem, lift, mix, again, abias, qkv, aproj, mgain, mbias, up, upb, down, downb = outs
    for ref, name in ((q, "queries"), (k, "keyw"), (v, "valuew"), (lift, "lift"), (mix, "mixer")):
        stacked(ref, name)
    for ref, name in ((stem, "stem"), (aproj, "aproj"), (down, "down")):
        flat(ref, name)
    for ref, name in ((qkv, "qkv"), (up, "up")):
        blocks(ref, name)
    at, lo, _, _ = next(cuts(table["vectors"][0], 16, piece))
    vectors = pack[at, lo : lo + 16].astype(F32)
    width = pack.shape[2]
    for i, ref in enumerate((again, abias, mgain, mbias, downb)):
        ref[...] = vectors[i]
    for j in range(upb.shape[0] // width):
        upb[width * j : width * (j + 1)] = vectors[5 + j]


def unpack(pieces, table, shapes):
    return pl.pallas_call(
        functools.partial(unpack_kernel, table),
        out_shape=tuple(jax.ShapeDtypeStruct(s, F32) for s in shapes),
        in_specs=[ANY] * 8,
        out_specs=(VMEM,) * len(shapes),
        scratch_shapes=[
            pltpu.VMEM((CORES * PIECES,) + pieces[0].shape, BF16),
            pltpu.SemaphoreType.DMA((8,)),
        ],
        compiler_params=pltpu.CompilerParams(vmem_limit_bytes=32 * 2**20),
        name="unpack",
    )(*pieces)


def sum_chips(held, came):
    levels = lax.axis_size("dp").bit_length() - 1
    first, second = (0, 1), (1, 0)
    one, two = own_bits(own_half())
    totals = [add(a, b) for a, b in zip(held, came)]
    for bit, bits in ((one, first), (two, second)):
        split = [t.reshape((2, -1, t.shape[-1])) for t in totals]
        sent = [swap_chips(select(bit, t[1], t[0]), bits) for t in split]
        totals = [add(select(bit, t[0], t[1]), c) for t, c in zip(split, sent)]
    for bits in zip(range(2, levels), reversed(range(2, levels))):
        sent = [swap_chips(t, bits) for t in totals]
        totals = [add(t, c) for t, c in zip(totals, sent)]
    sent = [swap_chips(t, second) for t in totals]
    near = [
        select(two, jnp.concatenate([t, c]), jnp.concatenate([c, t])) for t, c in zip(totals, sent)
    ]
    far = [swap_chips(t, first) for t in near]
    return tuple(near) + tuple(far)


def per_device(*args):
    weights = args[5:21]
    emb, qry, width = weights[0].shape
    table, total = layout(width, weights[12].shape[1], emb, qry, weights[4].shape[1])
    *packed, blk, blk_s, img, img_s, prp, prp_s = compute(args, table, total)
    keep, send = packed[:CHAINS], packed[CHAINS:]
    came = [swap_cores(v) for v in send]
    blk_r, img_r, prp_r = (swap_cores(v) for v in (blk_s, img_s, prp_s))
    pieces = sum_chips(keep, came)
    pieces += tuple(swap_cores(v) for v in pieces)
    blk = join(blk, blk_r, 0)
    prp = join(prp, prp_r, 0)[:, None]
    img = join(img, img_r, 1).astype(BF16).transpose(1, 0, 2)[:, None]
    grads = unpack(pieces, table, [w.shape for w in weights])
    return (blk, img, prp) + tuple(grads)


def solution(mesh):
    sample = [P("dp")] * 5
    return jax.shard_map(
        per_device,
        mesh=mesh,
        in_specs=tuple(sample + [P()] * 16 + [P("dp")]),
        out_specs=(P("dp", "section"),) * 3 + (P(),) * 16,
        check_vma=False,
    )
```

```python
import functools
import math

import jax
import jax.numpy as jnp
from jax import lax
from jax.experimental import pallas as pl
from jax.experimental.pallas import tpu as pltpu
from jax.sharding import PartitionSpec as P

HEADS = 8
F32 = jnp.float32
BF16 = jnp.bfloat16
CORES = 2
CHAINS = 2
PIECES = 2 * CHAINS
EPS = 1e-05
INV_SQRT2 = 1.0 / math.sqrt(2.0)
INV_SQRT2PI = 1.0 / math.sqrt(2.0 * math.pi)
ANY = pl.BlockSpec(memory_space=pl.ANY)
VMEM = pl.BlockSpec(memory_space=pltpu.VMEM)
SMEM = pl.BlockSpec(memory_space=pltpu.SMEM)


def mm(left, right):
    return lax.dot_general(left, right, (((1,), (0,)), ((), ())), preferred_element_type=F32)


def mm_bt(left, right):
    return lax.dot_general(left, right, (((1,), (1,)), ((), ())), preferred_element_type=F32)


def mm_at(left, right):
    return lax.dot_general(left, right, (((0,), (0,)), ((), ())), preferred_element_type=F32)


def layout(width, ffw, emb, queries, feats):
    counts = (
        ("keyw", emb * width),
        ("valuew", emb * width),
        ("mixer", emb * width),
        ("stem", width),
        ("lift", emb * feats),
        ("queries", emb * queries),
        ("qkv", 3 * width),
        ("aproj", width),
        ("up", ffw),
        ("down", ffw),
        ("vectors", 16),
    )
    table, first = {}, 0
    for name, rows in counts:
        table[name] = (first, rows)
        first += rows
    step = CORES * PIECES * 32
    return table, (first + step - 1) // step * step


def cuts(first, rows, piece):
    done = 0
    while done < rows:
        at = first + done
        count = min(rows - done, piece - at % piece)
        yield at // piece, at % piece, done, count
        done += count


def head_mask(rows, per_head, width):
    row = lax.broadcasted_iota(jnp.int32, (rows, width), 0) // per_head
    col = lax.broadcasted_iota(jnp.int32, (rows, width), 1) // (width // HEADS)
    return (row == col).astype(F32)


def spread(rows, mask):
    return jnp.concatenate([rows] * HEADS, axis=0) * mask


def fold(full, mask):
    per = full.shape[0] // HEADS
    return jnp.sum((full * mask).reshape(HEADS, per, full.shape[1]), axis=0)


def gelu_parts(values):
    cdf = 0.5 * (1.0 + lax.erf(values * INV_SQRT2))
    pdf = INV_SQRT2PI * jnp.exp(-0.5 * values * values)
    return values * cdf, cdf + values * pdf


def staged(count, *stages):
    for step in range(count + len(stages) - 1):
        for lag, stage in enumerate(stages):
            if 0 <= step - lag < count:
                stage(step - lag)


def softmax_rows(scores):
    expo = jnp.exp(scores - jnp.max(scores, axis=0, keepdims=True))
    return expo / jnp.sum(expo, axis=0, keepdims=True)


def per_step(row, reduce):
    part = reduce(row.reshape(-1, 8, row.shape[1]), axis=0)
    pair = jnp.maximum if reduce is jnp.max else jnp.add
    part = pair(part, pltpu.roll(part, 4, 0))
    return pair(part, pltpu.roll(part, 2, 0))


def softmax_lines(scores):
    expo = jnp.exp(scores.reshape(-1, 8, scores.shape[1]) - per_step(scores, jnp.max))
    return (expo * (1.0 / per_step(expo.reshape(scores.shape), jnp.sum))).reshape(scores.shape)


def softmax_lines_grad(probs, grad):
    terms = probs * grad
    total = per_step(terms, jnp.sum)
    tiles = (-1, 8, probs.shape[1])
    return (terms.reshape(tiles) - probs.reshape(tiles) * total).reshape(probs.shape)


def softmax_rows_grad(probs, grad):
    terms = probs * grad
    return terms - probs * jnp.sum(terms, axis=0, keepdims=True)


def norm_parts(values):
    center = values - jnp.mean(values, axis=-1, keepdims=True)
    rstd = lax.rsqrt(jnp.mean(center * center, axis=-1, keepdims=True) + EPS)
    return center * rstd, rstd


def norm_grad(grad, gain, hat, rstd):
    scaled = grad * gain
    first = jnp.mean(scaled, axis=-1, keepdims=True)
    second = jnp.mean(scaled * hat, axis=-1, keepdims=True)
    return rstd * (scaled - first - hat * second)


def compute_kernel(
    dims,
    emb_h,
    steps_h,
    views_h,
    images,
    proprio,
    out_grad,
    queries_h,
    key_h,
    value_h,
    stem_h,
    lift_h,
    mix_h,
    again_h,
    abias_h,
    qkv_h,
    aproj_h,
    mgain_h,
    mbias_h,
    up_h,
    up_bh,
    down_h,
    down_bh,
    keep0,
    keep1,
    send0,
    send1,
    extra_keep,
    extra_send,
    emb_ref,
    steps_ref,
    views_ref,
    queries,
    key_w,
    value_w,
    stem_proj,
    lift_w,
    mix_w,
    again,
    abias,
    qkv_w,
    aproj,
    mgain,
    mbias,
    up_w,
    up_b,
    down_w,
    down_b,
    xin_s,
    x_s,
    p_s,
    g_s,
    qs_s,
    a_s,
    tok_s,
    xt_s,
    prob_s,
    sgrad_s,
    mix_s,
    ab_s,
    ut_s,
    satt_s,
    act_s,
    dact_s,
    hat1_s,
    rstd1_s,
    norm1_s,
    qkv_s,
    tprob_s,
    tlow_s,
    gprob_s,
    att_s,
    mid_s,
    pre_s,
    hat2_s,
    rstd2_s,
    norm2_s,
    up_s,
    glow_s,
    gpre_s,
    gn2_s,
    gmid_s,
    gatt_s,
    gqkv_s,
    gtok_s,
    gsatt_s,
    blk_s,
    img_s,
    prp_s,
    macc_s,
    vacc_s,
    pack_s,
    in_sem,
):
    n, steps, keys, width, qry, ptok, emb, ffw, table, views = dims
    half_tok = qry + ptok
    ctx = steps * half_tok
    rows = n * ctx
    scale = 1.0 / math.sqrt(width // HEADS)
    piece = pack_s.shape[2]
    sec = lax.axis_index("section")
    base = sec * n
    lines = steps * keys
    tall = x_s.shape[1]
    def put(name, row, value):
        first = table[name][0] + row
        for at, lo, done, count in cuts(first, value.shape[0], piece):
            pack_s[at // PIECES, at % PIECES, lo : lo + count] = value[done : done + count].astype(BF16)

    sources = (
        (emb_h, emb_ref),
        (queries_h, queries),
        (key_h, key_w),
        (images.at[pl.ds(pl.multiple_of(sec * n * lines, 16), n * lines)], xin_s.at[pl.ds(0, n * lines)]),
        (views_h, views_ref),
        (value_h, value_w),
        (proprio.at[pl.ds(base, n)], p_s),
        (lift_h, lift_w),
        (mix_h, mix_w),
        (stem_h, stem_proj),
        (again_h, again),
        (abias_h, abias),
        (qkv_h, qkv_w),
        (steps_h, steps_ref),
        (aproj_h, aproj),
        (mgain_h, mgain),
        (mbias_h, mbias),
        (up_h, up_w),
        (up_bh, up_b),
        (down_h, down_w),
        (down_bh, down_b),
        (out_grad.at[pl.ds(base, n)], g_s),
    )
    loads = [pltpu.make_async_copy(a, b, in_sem.at[i]) for i, (a, b) in enumerate(sources)]
    for copy in loads:
        copy.start()
    waited = [0]

    def ready(count):
        for copy in loads[waited[0] : count]:
            copy.wait()
        waited[0] = max(waited[0], count)

    smask = head_mask(HEADS * qry, qry, width)
    smask_low = smask.astype(BF16)
    tmask = head_mask(HEADS * ctx, ctx, width)
    tmask_low = tmask.astype(BF16)
    for e in range(emb):
        macc_s[e] = jnp.zeros((width, width), F32)
        vacc_s[e] = jnp.zeros((width, width), F32)
    used = max(first + count for first, count in table.values())
    for at, lo, _, count in cuts(used, CORES * PIECES * piece - used, piece):
        pack_s[at // PIECES, at % PIECES, lo : lo + count] = jnp.zeros((count, width), BF16)
    xin_s[n * lines :] = jnp.zeros((xin_s.shape[0] - n * lines, width), BF16)
    ready(3)
    embs = [emb_ref[base + s] for s in range(n)]
    for e in range(emb):
        qs = spread(queries[e], smask_low)
        qs_s[e] = qs
        a_s[e] = (mm_bt(key_w[e], qs) * scale).astype(BF16)

    ready(4)
    edge = lines // 16 * 16
    inside = lax.broadcasted_iota(jnp.int32, (tall - edge, width), 0) < lines - edge
    for s in range(n):
        x_s[s] = xin_s[lines * s : lines * s + tall]
        last = x_s[s, edge:].astype(F32)
        x_s[s, edge:] = jnp.where(inside, last, 0.0).astype(BF16)

    first_step = lax.broadcasted_iota(jnp.int32, (tall, width), 0) % steps == 0

    def view_bias(s):
        lost = [jnp.where(views_ref[v, base + s] > 0, 0.0, -1e30).astype(F32) for v in range(views)]
        lost.append(jnp.float32(-1e30))
        ends = [lines // views * (v + 1) for v in range(views)]
        tiles, at = [], 0
        while at < tall:
            view = sum(at >= end for end in ends)
            stop = min([end // 8 * 8 for end in ends if end // 8 * 8 > at] + [tall])
            if view < views and ends[view] < at + 8:
                row = lax.broadcasted_iota(jnp.int32, (8, width), 0)
                tiles.append(jnp.where(row < ends[view] - at, lost[view], lost[view + 1]))
                at += 8
            else:
                tiles.append(jnp.full((stop - at, width), lost[view], F32))
                at = stop
        return jnp.concatenate(tiles, axis=0)

    def stem_scores(s):
        prob_s[s] = mm(x_s[s], a_s[embs[s]]) + view_bias(s)

    def stem_softmax(s):
        prob = softmax_lines(prob_s[s])
        prob_s[s] = prob
        mix_s[s, :, :width] = jnp.where(first_step, prob, 0.0).astype(BF16)
        mix_s[s, :, width : 2 * width] = jnp.where(first_step, 0.0, prob).astype(BF16)

    def stem_moments(s):
        turned = x_s[s].T
        xt_s[s] = turned
        ut_s[s] = mm(turned, mix_s[s, :, : 2 * width]).astype(BF16)

    def stem_values(s):
        values = mm(ut_s[s].T, value_w[embs[s]])
        for t in range(steps):
            satt_s[s, t] = fold(values[width * t : width * (t + 1)], smask).astype(BF16)

    ready(6)
    staged(n, stem_scores, stem_softmax, stem_moments, stem_values)
    ready(9)
    emb_rows = jnp.concatenate([jnp.full((steps * ptok, width), e) for e in embs], axis=0)
    lift_cat = jnp.concatenate([lift_w[e] for e in range(emb)], axis=1)
    mix_cat = jnp.concatenate([mix_w[e] for e in range(emb)], axis=1)

    def own_columns(values):
        result = values[:, :width]
        for e in range(1, emb):
            result = jnp.where(emb_rows == e, values[:, width * e : width * (e + 1)], result)
        return result

    def spread_columns(values):
        parts = [jnp.where(emb_rows == e, values, 0.0).astype(BF16) for e in range(emb)]
        return jnp.concatenate(parts, axis=1)

    prop_rows = p_s[...].reshape(n * steps * ptok, -1)
    act, dact = gelu_parts(own_columns(mm(prop_rows, lift_cat)))
    act_s[...] = act.astype(BF16)
    dact_s[...] = dact
    prop_tok = own_columns(mm(act_s[...], mix_cat)).astype(BF16)
    tok_s[:, :, qry:] = prop_tok.reshape(n, steps, ptok, width)

    ready(10)
    image_tok = mm(satt_s[...].reshape(n * steps * qry, width), stem_proj[...])
    tok_s[:, :, :qry] = image_tok.astype(BF16).reshape(n, steps, qry, width)

    ready(len(loads))
    group = n
    chunk = group * ctx
    spans = [pl.ds(i * chunk, chunk) for i in range(rows // chunk)]
    again_row = again[...].astype(F32).reshape(1, width)
    abias_row = abias[...].astype(F32).reshape(1, width)
    mgain_row = mgain[...].astype(F32).reshape(1, width)
    mbias_row = mbias[...].astype(F32).reshape(1, width)
    upb_row = up_b[...].astype(F32).reshape(1, ffw)
    downb_row = down_b[...].astype(F32).reshape(1, width)

    def tokens_of(i):
        return tok_s[group * i : group * (i + 1)].reshape(chunk, width).astype(F32)

    for i, span in enumerate(spans):
        hat, rstd = norm_parts(tokens_of(i))
        hat1_s[span] = hat
        rstd1_s[span] = jnp.broadcast_to(rstd, hat.shape)
        norm1 = (hat * again_row + abias_row).astype(BF16)
        norm1_s[span] = norm1
        qkv_s[span] = mm(norm1, qkv_w[...]).astype(BF16)

    key_step = lax.broadcasted_iota(jnp.int32, (ctx, 1), 0) // half_tok
    def trunk_rows(s):
        mine = pl.ds(s * ctx, ctx)
        return (qkv_s[mine, width * j : width * (j + 1)] for j in range(3))

    def trunk_scores(s):
        query, key, _ = trunk_rows(s)
        dead = jnp.where(key_step < steps_ref[base + s], 0.0, -1e30).astype(F32)
        tprob_s[s] = mm_bt(key, spread(query, tmask_low)) * scale + dead

    def trunk_softmax(s):
        prob = softmax_rows(tprob_s[s])
        tprob_s[s] = prob
        tlow_s[s] = prob.astype(BF16)

    def trunk_values(s):
        _, _, value = trunk_rows(s)
        att_s[pl.ds(s * ctx, ctx)] = fold(mm_at(tlow_s[s], value), tmask).astype(BF16)

    staged(n, trunk_scores, trunk_softmax, trunk_values)

    row_step = lax.broadcasted_iota(jnp.int32, (ctx, 1), 0) // half_tok
    sums = {name: jnp.zeros((1, width), F32) for name in ("mgain", "mbias", "downb")}
    sums["upb"] = jnp.zeros((1, ffw), F32)

    def total(name, values):
        sums[name] += jnp.sum(values, axis=0, keepdims=True)

    def live_rows(i):
        parts = [row_step < steps_ref[base + group * i + j] for j in range(group)]
        return jnp.concatenate([jnp.where(part, 1.0, 0.0).astype(F32) for part in parts], axis=0)

    def mlp_in(i):
        span = spans[i]
        middle = tokens_of(i) + mm(att_s[span], aproj[...])
        mid_s[span] = middle
        hat, rstd = norm_parts(middle)
        hat2_s[span] = hat
        rstd2_s[span] = jnp.broadcast_to(rstd, hat.shape)
        norm2 = (hat * mgain_row + mbias_row).astype(BF16)
        norm2_s[span] = norm2
        pre_s[span] = mm(norm2, up_w[...]) + upb_row

    def mlp_gelu(i):
        span = spans[i]
        act, dact = gelu_parts(pre_s[span])
        up_s[span] = act.astype(BF16)
        pre_s[span] = dact

    def mlp_back(i):
        span = spans[i]
        grad = g_s[group * i : group * (i + 1)].reshape(chunk, width).astype(F32) * live_rows(i)
        grad_low = grad.astype(BF16)
        glow_s[span] = grad_low
        total("downb", grad)
        grad_up = mm_bt(grad_low, down_w[...]).astype(BF16).astype(F32)
        grad_pre = (grad_up * pre_s[span]).astype(BF16)
        gpre_s[span] = grad_pre
        total("upb", grad_pre.astype(F32))

    def mlp_norm_back(i):
        span = spans[i]
        grad_norm2 = mm_bt(gpre_s[span], up_w[...]).astype(BF16).astype(F32)
        hat = hat2_s[span]
        total("mgain", grad_norm2 * hat)
        total("mbias", grad_norm2)
        grad_mid = norm_grad(grad_norm2, mgain_row, hat, rstd2_s[span]) + glow_s[span].astype(F32)
        gn2_s[span] = grad_mid
        grad_mid_low = grad_mid.astype(BF16)
        gmid_s[span] = grad_mid_low
        gatt_s[span] = mm_bt(grad_mid_low, aproj[...]).astype(BF16)

    def mlp_out(i):
        span = spans[i]
        result = (mid_s[span] + mm(up_s[span], down_w[...]) + downb_row) * live_rows(i)
        blk_s[group * i : group * (i + 1)] = result.astype(BF16).reshape(group, steps, half_tok, width)

    staged(len(spans), mlp_in, mlp_gelu, mlp_back, mlp_norm_back, mlp_out)

    put("aproj", 0, mm_at(att_s[...], gmid_s[...]))
    down = mm_at(glow_s[...], up_s[...]).astype(BF16)
    up = mm_at(norm2_s[...], gpre_s[...])
    for j in range(ffw // width):
        cols = slice(width * j, width * (j + 1))
        put("down", width * j, down[:, cols].T)
        put("up", width * j, up[:, cols])

    def trunk_back_probs(s):
        _, _, value = trunk_rows(s)
        grad_spread = spread(gatt_s[pl.ds(s * ctx, ctx)], tmask_low)
        gprob_s[s] = mm_bt(value, grad_spread)
        gqkv_s[pl.ds(s * ctx, ctx), 2 * width :] = mm(tlow_s[s], grad_spread).astype(BF16)

    def trunk_back_softmax(s):
        grad_prob = gprob_s[s].astype(BF16).astype(F32)
        tlow_s[s] = (softmax_rows_grad(tprob_s[s], grad_prob) * scale).astype(BF16)

    def trunk_back_rows(s):
        query, key, _ = trunk_rows(s)
        mine = pl.ds(s * ctx, ctx)
        gqkv_s[mine, :width] = fold(mm_at(tlow_s[s], key), tmask).astype(BF16)
        gqkv_s[mine, width : 2 * width] = mm(tlow_s[s], spread(query, tmask_low)).astype(BF16)

    staged(n, trunk_back_probs, trunk_back_softmax, trunk_back_rows)

    again_sum = jnp.zeros((1, width), F32)
    abias_sum = jnp.zeros((1, width), F32)
    for i, span in enumerate(spans):
        grad_norm1 = mm_bt(gqkv_s[span], qkv_w[...]).astype(BF16).astype(F32)
        hat = hat1_s[span]
        again_sum += jnp.sum(grad_norm1 * hat, axis=0, keepdims=True)
        abias_sum += jnp.sum(grad_norm1, axis=0, keepdims=True)
        grad_tok = norm_grad(grad_norm1, again_row, hat, rstd1_s[span]) + gn2_s[span]
        gtok_s[group * i : group * (i + 1)] = grad_tok.astype(BF16).reshape(group, steps, half_tok, width)
    qkv = mm_at(norm1_s[...], gqkv_s[...])
    for j in range(3):
        put("qkv", width * j, qkv[:, width * j : width * (j + 1)])
    vectors = [again_sum, abias_sum, sums["mgain"], sums["mbias"], sums["downb"]]
    vectors += [sums["upb"][:, width * j : width * (j + 1)] for j in range(ffw // width)]
    vectors += [jnp.zeros((16 - len(vectors), width), F32)]
    put("vectors", 0, jnp.concatenate(vectors, axis=0))

    grad_prop = spread_columns(gtok_s[:, :, qry:].reshape(n * steps * ptok, width).astype(F32))
    mixer = mm_at(act_s[...], grad_prop)
    grad_act = mm_bt(grad_prop, mix_cat).astype(BF16).astype(F32)
    grad_lift = spread_columns((grad_act * dact_s[...]).astype(BF16).astype(F32))
    lift = mm_at(prop_rows, grad_lift)
    for e in range(emb):
        put("mixer", width * e, mixer[:, width * e : width * (e + 1)])
        put("lift", lift.shape[0] * e, lift[:, width * e : width * (e + 1)])
    prp_s[...] = mm_bt(grad_lift, lift_cat).astype(BF16).reshape(n, steps, ptok, -1)

    grad_img = gtok_s[:, :, :qry].reshape(n * steps * qry, width)
    put("stem", 0, mm_at(satt_s[...].reshape(n * steps * qry, width), grad_img))
    gsatt_s[...] = mm_bt(grad_img, stem_proj[...]).astype(BF16).reshape(n, steps, qry, width)

    def stem_back_values(s):
        spreads = [spread(gsatt_s[s, t], smask_low) for t in range(steps)]
        grad_spread = jnp.concatenate(spreads, axis=0)
        ab_s[s, :, : 2 * width] = mm_bt(value_w[embs[s]], grad_spread).astype(BF16)
        ab_s[s, :, 2 * width :] = a_s[embs[s]]
        vacc_s[embs[s]] += mm(ut_s[s], grad_spread)

    def stem_back_probs(s):
        both = mm(x_s[s], ab_s[s, :, : 2 * width])
        sgrad_s[s] = jnp.where(first_step, both[:, :width], both[:, width:])

    def stem_back_softmax(s):
        grad_prob = sgrad_s[s].astype(BF16).astype(F32)
        mix_s[s, :, 2 * width :] = softmax_lines_grad(prob_s[s], grad_prob).astype(BF16)

    def stem_back_moments(s):
        macc_s[embs[s]] += mm(xt_s[s], mix_s[s, :, 2 * width :])

    def image_gradient(s):
        img_s[pl.ds(s, tall, stride=n)] = mm_bt(mix_s[s], ab_s[s])

    staged(n, stem_back_values, stem_back_probs, stem_back_softmax, stem_back_moments, image_gradient)

    for e in range(emb):
        moment = (macc_s[e] * scale).astype(BF16)
        put("keyw", width * e, mm(moment, qs_s[e]))
        put("queries", qry * e, fold(mm_at(moment, key_w[e]), smask))
        put("valuew", width * e, vacc_s[e])
    other = 1 - sec
    half = own_half()
    image = img_s.reshape(tall // steps, steps, n, width)
    first, second = keys * n, keys * n + n * half_tok
    for ref, at in ((extra_keep, sec), (extra_send, other)):
        ref[:first] = image[:keys, at].reshape(first, width).astype(BF16)
        ref[first:second] = blk_s[:, at].reshape(second - first, width)
        ref[second:, : prp_s.shape[3]] = prp_s[:, at].reshape(n * ptok, -1)
        ref[second:, prp_s.shape[3] :] = jnp.zeros((n * ptok, width - prp_s.shape[3]), BF16)
    for ref, at, chain in ((keep0, half, 0), (keep1, half, 1), (send0, 1 - half, 0), (send1, 1 - half, 1)):
        ref[...] = pack_s[at, 2 * chain : 2 * chain + 2]


def rows_of(images):
    return images.transpose(0, 2, 1, 3).reshape(-1, images.shape[-1])


def compute(args, table, total):
    images, proprio, view_mask, embodiment, ctx_steps = args[:5]
    weights, out_grad = args[5:21], args[21]
    samples, steps, keys, width = images.shape
    ptok, feats = proprio.shape[2:]
    emb, qry = weights[0].shape[:2]
    ffw = weights[12].shape[1]
    n = samples // CORES
    half_tok = qry + ptok
    ctx = steps * half_tok
    rows = n * ctx
    piece = total // (CORES * PIECES)
    lines = steps * keys
    tall = (lines + 15) // 16 * 16
    dims = (n, steps, keys, width, qry, ptok, emb, ffw, table, view_mask.shape[1])

    def low(*shape):
        return pltpu.VMEM(shape, BF16)

    def full(*shape):
        return pltpu.VMEM(shape, F32)

    small = (embodiment, ctx_steps, view_mask.T)
    scratch = [pltpu.SMEM(v.shape, v.dtype) for v in small]
    scratch += [low(*w.shape) for w in weights]
    scratch += [
        low((n * lines + 31) // 16 * 16, width),
        low(n, tall, width),
        low(n, steps, ptok, feats),
        low(n, ctx, width),
        low(emb, HEADS * qry, width),
        low(emb, width, HEADS * qry),
        low(n, steps, half_tok, width),
        low(n, width, tall),
        full(n, tall, HEADS * qry),
        full(n, tall, HEADS * qry),
        low(n, tall, (steps + 1) * width),
        low(n, width, (steps + 1) * width),
        low(n, width, steps * width),
        low(n, steps, qry, width),
        low(n * steps * ptok, width),
        full(n * steps * ptok, width),
        full(rows, width),
        full(rows, width),
        low(rows, width),
        low(rows, 3 * width),
        full(n, ctx, HEADS * ctx),
        low(n, ctx, HEADS * ctx),
        full(n, ctx, HEADS * ctx),
        low(rows, width),
        full(rows, width),
        full(rows, ffw),
        full(rows, width),
        full(rows, width),
        low(rows, width),
        low(rows, ffw),
        low(rows, width),
        low(rows, ffw),
        full(rows, width),
        low(rows, width),
        low(rows, width),
        low(rows, 3 * width),
        low(n, steps, half_tok, width),
        low(n, steps, qry, width),
        low(n, steps, half_tok, width),
        full(tall * n, width),
        low(n, steps, ptok, feats),
        full(emb, width, HEADS * qry),
        full(emb, width, width),
        low(CORES, PIECES, piece, width),
        pltpu.SemaphoreType.DMA((22,)),
    ]
    inputs = (*small, rows_of(images), proprio, out_grad, *weights)
    return pl.pallas_call(
        functools.partial(compute_kernel, dims),
        out_shape=(
            low(2, piece, width),
            low(2, piece, width),
            low(2, piece, width),
            low(2, piece, width),
            low(keys * n + n * half_tok + n * ptok, width),
            low(keys * n + n * half_tok + n * ptok, width),
        ),
        in_specs=[ANY] * 22,
        out_specs=(VMEM,) * 6,
        scratch_shapes=scratch,
        compiler_params=pltpu.CompilerParams(vmem_limit_bytes=40 * 2**20),
        name="stem_trunk",
    )(*(pltpu.with_memory_space_constraint(v, pltpu.HBM) for v in inputs))


def parity(index, levels):
    total = index & 1
    for level in range(1, levels):
        total = total ^ ((index >> level) & 1)
    return total


def own_half():
    levels = lax.axis_size("dp").bit_length() - 1
    return lax.axis_index("section") ^ parity(lax.axis_index("dp"), levels)


def own_bits(half):
    dp = lax.axis_index("dp")
    low, high = dp & 1, (dp >> 1) & 1
    return jnp.where(half == 0, low, high), jnp.where(half == 0, high, low)


def select(bit, low, high):
    return jnp.where(bit == 0, low, high)


def add(held, came):
    return (held.astype(F32) + came.astype(F32)).astype(BF16)


def swap_cores(value):
    return lax.ppermute(value, "section", [(0, 1), (1, 0)])


def swap_chips(value, bits):
    count = lax.axis_size("dp")
    levels = count.bit_length() - 1
    pairs = []
    for core in range(CORES):
        for i in range(count):
            bit = bits[core ^ parity(i, levels)]
            pairs.append((core * count + i, (1 - core) * count + (i ^ (1 << bit))))
    return lax.ppermute(value, ("section", "dp"), pairs)


def finish_kernel(table, pack, blk, img, prp, *refs):
    count = len(refs) // 2 - 2
    outs, held, sem = refs[: count + 3], refs[count + 3 : -1], refs[-1]
    copies = []

    def send(source, target):
        copy = pltpu.make_async_copy(source, target, sem.at[len(copies)])
        copy.start()
        copies.append(copy)

    for source, target in zip((blk, img, prp), outs):
        send(source, target)
    names = ("queries", "keyw", "valuew", "stem", "lift", "mixer", "again", "abias", "qkv", "aproj")
    names += ("mgain", "mbias", "up", "upb", "down", "downb")
    vectors = pack[pl.ds(table["vectors"][0], 16)].astype(F32)
    width = pack.shape[1]
    rows = {"again": 0, "abias": 1, "mgain": 2, "mbias": 3, "downb": 4}
    order = sorted(range(count), key=lambda i: table.get(names[i], (1 << 30,))[0])
    for i in order:
        name, ref = names[i], held[i]
        if name in rows:
            ref[...] = vectors[rows[name]]
        elif name == "upb":
            for j in range(ref.shape[0] // width):
                ref[width * j : width * (j + 1)] = vectors[5 + j]
        else:
            first, total = table[name]
            wide = ref.shape[-1] // width
            for j in range(wide):
                part = pack[first + total // wide * j : first + total // wide * (j + 1)].astype(F32)
                if ref.ndim == 3:
                    ref[...] = part.reshape(ref.shape)
                else:
                    ref[:, width * j : width * (j + 1)] = part
        send(ref, outs[3 + i])
    for copy in copies:
        copy.wait()


def finish(table, pack, blk, img, prp, shapes):
    inputs = (pack, blk, img, prp)
    return pl.pallas_call(
        functools.partial(finish_kernel, table),
        out_shape=tuple(jax.ShapeDtypeStruct(v.shape, BF16) for v in inputs[1:])
        + tuple(jax.ShapeDtypeStruct(v, F32) for v in shapes),
        in_specs=[VMEM] * 4,
        out_specs=(ANY,) * (3 + len(shapes)),
        scratch_shapes=[pltpu.VMEM(v, F32) for v in shapes]
        + [pltpu.SemaphoreType.DMA((3 + len(shapes),))],
        compiler_params=pltpu.CompilerParams(vmem_limit_bytes=24 * 2**20),
        name="finish",
    )(*(pltpu.with_memory_space_constraint(v, pltpu.VMEM) for v in inputs))


def sum_chips(held, came, extra):
    levels = lax.axis_size("dp").bit_length() - 1
    first, second = (0, 1), (1, 0)
    half = own_half()
    one, two = own_bits(half)
    totals = [add(a, b) for a, b in zip(held, came)]
    *totals[1:], extra = lax.optimization_barrier((*totals[1:], extra))
    for bit, bits in ((one, first), (two, second)):
        split = [t.reshape((2, -1, t.shape[-1])) for t in totals]
        sent = [swap_chips(select(bit, t[1], t[0]), bits) for t in split]
        totals = [add(select(bit, t[0], t[1]), c) for t, c in zip(split, sent)]
    extra = swap_cores(extra)
    for bits in zip(range(2, levels), reversed(range(2, levels))):
        sent = [swap_chips(t, bits) for t in totals]
        totals = [add(t, c) for t, c in zip(totals, sent)]
    sent = [swap_chips(t, second) for t in totals]
    near = [either(two, t, c) for t, c in zip(totals, sent)]
    far = [swap_chips(t, first) for t in near]
    own = [either(one, *v) for v in zip(near, far)]
    bit = own_bits(1 - half)[0]
    other = [either(bit, *v) for v in zip(*([swap_cores(t) for t in v] for v in (near, far)))]
    return either(half, jnp.concatenate(own), jnp.concatenate(other)), extra


def either(bit, mine, came, axis=0):
    return select(bit, jnp.concatenate([mine, came], axis), jnp.concatenate([came, mine], axis))


def per_device(*args):
    images, proprio, weights = args[0], args[1], args[5:21]
    emb, qry, width = weights[0].shape
    n, keys = images.shape[0] // CORES, images.shape[2]
    ptok, feats = proprio.shape[2:]
    table, total = layout(width, weights[12].shape[1], emb, qry, weights[4].shape[1])
    *packed, extra, extra_sent = compute(args, table, total)
    keep, send = packed[:CHAINS], packed[CHAINS:]
    pack, came = sum_chips(keep, [swap_cores(v) for v in send], extra_sent)
    sec = lax.axis_index("section")
    first, second = keys * n, keys * n + n * (qry + ptok)
    img = either(sec, *(v[:first].reshape(keys, n, width) for v in (extra, came)), 1)
    blk = either(sec, *(v[first:second].reshape(n, -1, width) for v in (extra, came)))
    prp = either(sec, *(v[second:, :feats].reshape(n, ptok, feats) for v in (extra, came)))
    blk, img, prp, *grads = finish(table, pack, blk, img, prp, [w.shape for w in weights])
    return (blk, img.transpose(1, 0, 2)[:, None], prp[:, None]) + tuple(grads)


def solution(mesh):
    sample = [P("dp")] * 5
    return jax.shard_map(
        per_device,
        mesh=mesh,
        in_specs=tuple(sample + [P()] * 16 + [P("dp")]),
        out_specs=(P("dp", "section"),) * 3 + (P(),) * 16,
        check_vma=False,
    )
```

```python
import functools
import math

import jax
import jax.numpy as jnp
from jax import lax
from jax.experimental import pallas as pl
from jax.experimental.pallas import tpu as pltpu
from jax.sharding import PartitionSpec as P

HEADS = 8
F32 = jnp.float32
BF16 = jnp.bfloat16
CORES = 2
CHAINS = 2
PIECES = 2 * CHAINS
EPS = 1e-05
LAG = 4
INV_SQRT2 = 1.0 / math.sqrt(2.0)
INV_SQRT2PI = 1.0 / math.sqrt(2.0 * math.pi)
ANY = pl.BlockSpec(memory_space=pl.ANY)
VMEM = pl.BlockSpec(memory_space=pltpu.VMEM)
SMEM = pl.BlockSpec(memory_space=pltpu.SMEM)


def mm(left, right):
    return lax.dot_general(left, right, (((1,), (0,)), ((), ())), preferred_element_type=F32)


def mm_bt(left, right):
    return lax.dot_general(left, right, (((1,), (1,)), ((), ())), preferred_element_type=F32)


def mm_at(left, right):
    return lax.dot_general(left, right, (((0,), (0,)), ((), ())), preferred_element_type=F32)


def layout(width, ffw, emb, queries, feats):
    counts = (
        ("keyw", emb * width),
        ("valuew", emb * width),
        ("mixer", emb * width),
        ("stem", width),
        ("lift", emb * feats),
        ("queries", emb * queries),
        ("qkv", 3 * width),
        ("aproj", width),
        ("up", ffw),
        ("down", ffw),
        ("vectors", 16),
    )
    table, first = {}, 0
    for name, rows in counts:
        table[name] = (first, rows)
        first += rows
    step = CORES * PIECES * 32
    return table, (first + step - 1) // step * step


def cuts(first, rows, piece):
    done = 0
    while done < rows:
        at = first + done
        count = min(rows - done, piece - at % piece)
        yield at // piece, at % piece, done, count
        done += count


def head_mask(rows, per_head, width):
    row = lax.broadcasted_iota(jnp.int32, (rows, width), 0) // per_head
    col = lax.broadcasted_iota(jnp.int32, (rows, width), 1) // (width // HEADS)
    return (row == col).astype(F32)


def spread(rows, mask):
    return jnp.concatenate([rows] * HEADS, axis=0) * mask


def fold(full, mask):
    per = full.shape[0] // HEADS
    return jnp.sum((full * mask).reshape(HEADS, per, full.shape[1]), axis=0)


def gelu_parts(values):
    cdf = 0.5 * (1.0 + lax.erf(values * INV_SQRT2))
    pdf = INV_SQRT2PI * jnp.exp(-0.5 * values * values)
    return values * cdf, cdf + values * pdf


def staged(count, *stages):
    for step in range(count + LAG * (len(stages) - 1)):
        for lag, stage in enumerate(stages):
            if 0 <= step - LAG * lag < count:
                stage(step - LAG * lag)


def softmax_rows(scores):
    expo = jnp.exp(scores - jnp.max(scores, axis=0, keepdims=True))
    return expo * (1.0 / jnp.sum(expo, axis=0, keepdims=True))


def per_step(row, reduce):
    part = reduce(row.reshape(-1, 8, row.shape[1]), axis=0)
    pair = jnp.maximum if reduce is jnp.max else jnp.add
    part = pair(part, pltpu.roll(part, 4, 0))
    return pair(part, pltpu.roll(part, 2, 0))


def softmax_lines(scores):
    expo = jnp.exp(scores.reshape(-1, 8, scores.shape[1]) - per_step(scores, jnp.max))
    return (expo * (1.0 / per_step(expo.reshape(scores.shape), jnp.sum))).reshape(scores.shape)


def softmax_lines_grad(probs, grad):
    terms = probs * grad
    total = per_step(terms, jnp.sum)
    tiles = (-1, 8, probs.shape[1])
    return (terms.reshape(tiles) - probs.reshape(tiles) * total).reshape(probs.shape)


def softmax_rows_grad(probs, grad):
    terms = probs * grad
    return terms - probs * jnp.sum(terms, axis=0, keepdims=True)


def row_mean(values):
    width = values.shape[1]
    high = values.astype(BF16)
    low = (values - high.astype(F32)).astype(BF16)
    ones = jnp.full((2 * width, width), 1.0 / width, BF16)
    return mm(jnp.concatenate([high, low], axis=1), ones)


def norm_parts(values):
    center = values - row_mean(values)
    rstd = lax.rsqrt(row_mean(center * center) + EPS)
    return center * rstd, rstd


def norm_grad(grad, gain, hat, rstd):
    scaled = grad * gain
    first = row_mean(scaled)
    second = row_mean(scaled * hat)
    return rstd * (scaled - first - hat * second)


def compute_kernel(
    dims,
    emb_h,
    steps_h,
    views_h,
    images,
    proprio,
    out_grad,
    queries_h,
    key_h,
    value_h,
    stem_h,
    lift_h,
    mix_h,
    again_h,
    abias_h,
    qkv_h,
    aproj_h,
    mgain_h,
    mbias_h,
    up_h,
    up_bh,
    down_h,
    down_bh,
    keep0,
    keep1,
    send0,
    send1,
    extra_keep,
    extra_send,
    emb_ref,
    steps_ref,
    views_ref,
    queries,
    key_w,
    value_w,
    stem_proj,
    lift_w,
    mix_w,
    again,
    abias,
    qkv_w,
    aproj,
    mgain,
    mbias,
    up_w,
    up_b,
    down_w,
    down_b,
    xin_s,
    x_s,
    p_s,
    g_s,
    qs_s,
    a_s,
    tok_s,
    xt_s,
    prob_s,
    sgrad_s,
    mix_s,
    ab_s,
    ut_s,
    satt_s,
    act_s,
    dact_s,
    hat1_s,
    rstd1_s,
    norm1_s,
    qkv_s,
    tprob_s,
    tlow_s,
    gprob_s,
    att_s,
    mid_s,
    pre_s,
    hat2_s,
    rstd2_s,
    norm2_s,
    up_s,
    glow_s,
    gpre_s,
    gn2_s,
    gmid_s,
    gatt_s,
    gqkv_s,
    gtok_s,
    gsatt_s,
    blk_s,
    img_s,
    prp_s,
    macc_s,
    vacc_s,
    pack_s,
    in_sem,
):
    n, steps, keys, width, qry, ptok, emb, ffw, table, views = dims
    half_tok = qry + ptok
    ctx = steps * half_tok
    rows = n * ctx
    scale = 1.0 / math.sqrt(width // HEADS)
    piece = pack_s.shape[2]
    sec = lax.axis_index("section")
    base = sec * n
    lines = steps * keys
    tall = x_s.shape[1]
    def put(name, row, value):
        first = table[name][0] + row
        for at, lo, done, count in cuts(first, value.shape[0], piece):
            pack_s[at // PIECES, at % PIECES, lo : lo + count] = value[done : done + count].astype(BF16)

    sources = (
        (emb_h, emb_ref),
        (queries_h, queries),
        (key_h, key_w),
        (images.at[pl.ds(pl.multiple_of(sec * n * lines, 16), n * lines)], xin_s.at[pl.ds(0, n * lines)]),
        (views_h, views_ref),
        (value_h, value_w),
        (proprio.at[pl.ds(base, n)], p_s),
        (lift_h, lift_w),
        (mix_h, mix_w),
        (stem_h, stem_proj),
        (again_h, again),
        (abias_h, abias),
        (qkv_h, qkv_w),
        (steps_h, steps_ref),
        (aproj_h, aproj),
        (mgain_h, mgain),
        (mbias_h, mbias),
        (up_h, up_w),
        (up_bh, up_b),
        (down_h, down_w),
        (down_bh, down_b),
        (out_grad.at[pl.ds(base, n)], g_s),
    )
    loads = [pltpu.make_async_copy(a, b, in_sem.at[i]) for i, (a, b) in enumerate(sources)]
    for copy in loads:
        copy.start()
    waited = [0]

    def ready(count):
        for copy in loads[waited[0] : count]:
            copy.wait()
        waited[0] = max(waited[0], count)

    smask = head_mask(HEADS * qry, qry, width)
    smask_low = smask.astype(BF16)
    tmask = head_mask(HEADS * ctx, ctx, width)
    tmask_low = tmask.astype(BF16)
    for e in range(emb):
        macc_s[e] = jnp.zeros((width, width), F32)
        vacc_s[e] = jnp.zeros((width, width), F32)
    used = max(first + count for first, count in table.values())
    for at, lo, _, count in cuts(used, CORES * PIECES * piece - used, piece):
        pack_s[at // PIECES, at % PIECES, lo : lo + count] = jnp.zeros((count, width), BF16)
    xin_s[n * lines :] = jnp.zeros((xin_s.shape[0] - n * lines, width), BF16)
    ready(3)
    embs = [emb_ref[base + s] for s in range(n)]
    for e in range(emb):
        qs = spread(queries[e], smask_low)
        qs_s[e] = qs
        a_s[e] = (mm_bt(key_w[e], qs) * scale).astype(BF16)

    ready(4)
    edge = lines // 16 * 16
    inside = lax.broadcasted_iota(jnp.int32, (tall - edge, width), 0) < lines - edge
    for s in range(n):
        x_s[s] = xin_s[lines * s : lines * s + tall]
        last = x_s[s, edge:].astype(F32)
        x_s[s, edge:] = jnp.where(inside, last, 0.0).astype(BF16)

    ready(9)
    emb_rows = jnp.concatenate([jnp.full((steps * ptok, width), e) for e in embs], axis=0)
    lift_cat = jnp.concatenate([lift_w[e] for e in range(emb)], axis=1)
    mix_cat = jnp.concatenate([mix_w[e] for e in range(emb)], axis=1)

    def own_columns(values):
        result = values[:, :width]
        for e in range(1, emb):
            result = jnp.where(emb_rows == e, values[:, width * e : width * (e + 1)], result)
        return result

    def spread_columns(values):
        parts = [jnp.where(emb_rows == e, values, 0.0).astype(BF16) for e in range(emb)]
        return jnp.concatenate(parts, axis=1)

    prop_rows = p_s[...].reshape(n * steps * ptok, -1)
    act, dact = gelu_parts(own_columns(mm(prop_rows, lift_cat)))
    act_s[...] = act.astype(BF16)
    dact_s[...] = dact
    prop_tok = own_columns(mm(act_s[...], mix_cat)).astype(BF16)
    tok_s[:, :, qry:] = prop_tok.reshape(n, steps, ptok, width)

    first_step = lax.broadcasted_iota(jnp.int32, (tall, width), 0) % steps == 0

    def view_bias(s):
        lost = [jnp.where(views_ref[v, base + s] > 0, 0.0, -1e30).astype(F32) for v in range(views)]
        lost.append(jnp.float32(-1e30))
        ends = [lines // views * (v + 1) for v in range(views)]
        tiles, at = [], 0
        while at < tall:
            view = sum(at >= end for end in ends)
            stop = min([end // 8 * 8 for end in ends if end // 8 * 8 > at] + [tall])
            if view < views and ends[view] < at + 8:
                row = lax.broadcasted_iota(jnp.int32, (8, width), 0)
                tiles.append(jnp.where(row < ends[view] - at, lost[view], lost[view + 1]))
                at += 8
            else:
                tiles.append(jnp.full((stop - at, width), lost[view], F32))
                at = stop
        return jnp.concatenate(tiles, axis=0)

    def stem_scores(s):
        prob_s[s] = mm(x_s[s], a_s[embs[s]]) + view_bias(s)

    def stem_softmax(s):
        prob = softmax_lines(prob_s[s])
        prob_s[s] = prob
        mix_s[s, :, :width] = jnp.where(first_step, prob, 0.0).astype(BF16)
        mix_s[s, :, width : 2 * width] = jnp.where(first_step, 0.0, prob).astype(BF16)

    def stem_moments(s):
        turned = x_s[s].T
        xt_s[s] = turned
        ut_s[s] = mm(turned, mix_s[s, :, : 2 * width]).astype(BF16)

    def stem_values(s):
        values = mm(ut_s[s].T, value_w[embs[s]])
        for t in range(steps):
            satt_s[s, t] = fold(values[width * t : width * (t + 1)], smask).astype(BF16)

    ready(6)
    staged(n, stem_scores, stem_softmax, stem_moments, stem_values)
    ready(10)
    image_tok = mm(satt_s[...].reshape(n * steps * qry, width), stem_proj[...])
    tok_s[:, :, :qry] = image_tok.astype(BF16).reshape(n, steps, qry, width)

    ready(len(loads))
    group = n
    chunk = group * ctx
    spans = [pl.ds(i * chunk, chunk) for i in range(rows // chunk)]
    again_row = again[...].astype(F32).reshape(1, width)
    abias_row = abias[...].astype(F32).reshape(1, width)
    mgain_row = mgain[...].astype(F32).reshape(1, width)
    mbias_row = mbias[...].astype(F32).reshape(1, width)
    upb_row = up_b[...].astype(F32).reshape(1, ffw)
    downb_row = down_b[...].astype(F32).reshape(1, width)

    def tokens_of(i):
        return tok_s[group * i : group * (i + 1)].reshape(chunk, width).astype(F32)

    for i, span in enumerate(spans):
        hat, rstd = norm_parts(tokens_of(i))
        hat1_s[span] = hat
        rstd1_s[span] = jnp.broadcast_to(rstd, hat.shape)
        norm1 = (hat * again_row + abias_row).astype(BF16)
        norm1_s[span] = norm1
        qkv_s[span] = mm(norm1, qkv_w[...]).astype(BF16)

    key_step = lax.broadcasted_iota(jnp.int32, (ctx, 1), 0) // half_tok
    def trunk_rows(s):
        mine = pl.ds(s * ctx, ctx)
        return (qkv_s[mine, width * j : width * (j + 1)] for j in range(3))

    def trunk_scores(s):
        query, key, _ = trunk_rows(s)
        dead = jnp.where(key_step < steps_ref[base + s], 0.0, -1e30).astype(F32)
        tprob_s[s] = mm_bt(key, spread(query, tmask_low)) * scale + dead

    def trunk_softmax(s):
        prob = softmax_rows(tprob_s[s])
        tprob_s[s] = prob
        tlow_s[s] = prob.astype(BF16)

    def trunk_values(s):
        _, _, value = trunk_rows(s)
        att_s[pl.ds(s * ctx, ctx)] = fold(mm_at(tlow_s[s], value), tmask).astype(BF16)

    staged(n, trunk_scores, trunk_softmax, trunk_values)

    row_step = lax.broadcasted_iota(jnp.int32, (ctx, 1), 0) // half_tok
    sums = {name: jnp.zeros((1, width), F32) for name in ("mgain", "mbias", "downb")}
    sums["upb"] = jnp.zeros((1, ffw), F32)

    def total(name, values):
        sums[name] += jnp.sum(values, axis=0, keepdims=True)

    def live_rows(i):
        parts = [row_step < steps_ref[base + group * i + j] for j in range(group)]
        return jnp.concatenate([jnp.where(part, 1.0, 0.0).astype(F32) for part in parts], axis=0)

    def mlp_in(i):
        span = spans[i]
        middle = tokens_of(i) + mm(att_s[span], aproj[...])
        mid_s[span] = middle
        hat, rstd = norm_parts(middle)
        hat2_s[span] = hat
        rstd2_s[span] = jnp.broadcast_to(rstd, hat.shape)
        norm2 = (hat * mgain_row + mbias_row).astype(BF16)
        norm2_s[span] = norm2
        pre_s[span] = mm(norm2, up_w[...]) + upb_row

    def mlp_gelu(i):
        span = spans[i]
        act, dact = gelu_parts(pre_s[span])
        up_s[span] = act.astype(BF16)
        pre_s[span] = dact

    def mlp_back(i):
        span = spans[i]
        grad = g_s[group * i : group * (i + 1)].reshape(chunk, width).astype(F32) * live_rows(i)
        grad_low = grad.astype(BF16)
        glow_s[span] = grad_low
        total("downb", grad)
        grad_up = mm_bt(grad_low, down_w[...]).astype(BF16).astype(F32)
        grad_pre = (grad_up * pre_s[span]).astype(BF16)
        gpre_s[span] = grad_pre
        total("upb", grad_pre.astype(F32))

    def mlp_norm_back(i):
        span = spans[i]
        grad_norm2 = mm_bt(gpre_s[span], up_w[...]).astype(BF16).astype(F32)
        hat = hat2_s[span]
        total("mgain", grad_norm2 * hat)
        total("mbias", grad_norm2)
        grad_mid = norm_grad(grad_norm2, mgain_row, hat, rstd2_s[span]) + glow_s[span].astype(F32)
        gn2_s[span] = grad_mid
        grad_mid_low = grad_mid.astype(BF16)
        gmid_s[span] = grad_mid_low
        gatt_s[span] = mm_bt(grad_mid_low, aproj[...]).astype(BF16)

    def mlp_out(i):
        span = spans[i]
        result = (mid_s[span] + mm(up_s[span], down_w[...]) + downb_row) * live_rows(i)
        blk_s[group * i : group * (i + 1)] = result.astype(BF16).reshape(group, steps, half_tok, width)

    staged(len(spans), mlp_in, mlp_gelu, mlp_back, mlp_norm_back, mlp_out)

    put("aproj", 0, mm_at(att_s[...], gmid_s[...]))
    down = mm_at(glow_s[...], up_s[...]).astype(BF16)
    up = mm_at(norm2_s[...], gpre_s[...])
    for j in range(ffw // width):
        cols = slice(width * j, width * (j + 1))
        put("down", width * j, down[:, cols].T)
        put("up", width * j, up[:, cols])

    def trunk_back_probs(s):
        _, _, value = trunk_rows(s)
        grad_spread = spread(gatt_s[pl.ds(s * ctx, ctx)], tmask_low)
        gprob_s[s] = mm_bt(value, grad_spread)
        gqkv_s[pl.ds(s * ctx, ctx), 2 * width :] = mm(tlow_s[s], grad_spread).astype(BF16)

    def trunk_back_softmax(s):
        grad_prob = gprob_s[s].astype(BF16).astype(F32)
        tlow_s[s] = (softmax_rows_grad(tprob_s[s], grad_prob) * scale).astype(BF16)

    def trunk_back_rows(s):
        query, key, _ = trunk_rows(s)
        mine = pl.ds(s * ctx, ctx)
        gqkv_s[mine, :width] = fold(mm_at(tlow_s[s], key), tmask).astype(BF16)
        gqkv_s[mine, width : 2 * width] = mm(tlow_s[s], spread(query, tmask_low)).astype(BF16)

    staged(n, trunk_back_probs, trunk_back_softmax, trunk_back_rows)

    again_sum = jnp.zeros((1, width), F32)
    abias_sum = jnp.zeros((1, width), F32)
    for i, span in enumerate(spans):
        grad_norm1 = mm_bt(gqkv_s[span], qkv_w[...]).astype(BF16).astype(F32)
        hat = hat1_s[span]
        again_sum += jnp.sum(grad_norm1 * hat, axis=0, keepdims=True)
        abias_sum += jnp.sum(grad_norm1, axis=0, keepdims=True)
        grad_tok = norm_grad(grad_norm1, again_row, hat, rstd1_s[span]) + gn2_s[span]
        gtok_s[group * i : group * (i + 1)] = grad_tok.astype(BF16).reshape(group, steps, half_tok, width)
    qkv = mm_at(norm1_s[...], gqkv_s[...])
    for j in range(3):
        put("qkv", width * j, qkv[:, width * j : width * (j + 1)])
    vectors = [again_sum, abias_sum, sums["mgain"], sums["mbias"], sums["downb"]]
    vectors += [sums["upb"][:, width * j : width * (j + 1)] for j in range(ffw // width)]
    vectors += [jnp.zeros((16 - len(vectors), width), F32)]
    put("vectors", 0, jnp.concatenate(vectors, axis=0))

    grad_prop = spread_columns(gtok_s[:, :, qry:].reshape(n * steps * ptok, width).astype(F32))
    mixer = mm_at(act_s[...], grad_prop)
    grad_act = mm_bt(grad_prop, mix_cat).astype(BF16).astype(F32)
    grad_lift = spread_columns((grad_act * dact_s[...]).astype(BF16).astype(F32))
    lift = mm_at(prop_rows, grad_lift)
    for e in range(emb):
        put("mixer", width * e, mixer[:, width * e : width * (e + 1)])
        put("lift", lift.shape[0] * e, lift[:, width * e : width * (e + 1)])
    prp_s[...] = mm_bt(grad_lift, lift_cat).astype(BF16).reshape(n, steps, ptok, -1)

    grad_img = gtok_s[:, :, :qry].reshape(n * steps * qry, width)
    put("stem", 0, mm_at(satt_s[...].reshape(n * steps * qry, width), grad_img))
    gsatt_s[...] = mm_bt(grad_img, stem_proj[...]).astype(BF16).reshape(n, steps, qry, width)

    def stem_back_values(s):
        spreads = [spread(gsatt_s[s, t], smask_low) for t in range(steps)]
        grad_spread = jnp.concatenate(spreads, axis=0)
        ab_s[s, :, : 2 * width] = mm_bt(value_w[embs[s]], grad_spread).astype(BF16)
        ab_s[s, :, 2 * width :] = a_s[embs[s]]
        vacc_s[embs[s]] += mm(ut_s[s], grad_spread)

    def stem_back_probs(s):
        both = mm(x_s[s], ab_s[s, :, : 2 * width])
        sgrad_s[s] = jnp.where(first_step, both[:, :width], both[:, width:])

    def stem_back_softmax(s):
        grad_prob = sgrad_s[s].astype(BF16).astype(F32)
        mix_s[s, :, 2 * width :] = softmax_lines_grad(prob_s[s], grad_prob).astype(BF16)

    def stem_back_moments(s):
        macc_s[embs[s]] += mm(xt_s[s], mix_s[s, :, 2 * width :])

    def image_gradient(s):
        img_s[pl.ds(s, tall, stride=n)] = mm_bt(mix_s[s], ab_s[s])

    staged(n, stem_back_values, stem_back_probs, stem_back_softmax, stem_back_moments, image_gradient)

    for e in range(emb):
        moment = (macc_s[e] * scale).astype(BF16)
        put("keyw", width * e, mm(moment, qs_s[e]))
        put("queries", qry * e, fold(mm_at(moment, key_w[e]), smask))
        put("valuew", width * e, vacc_s[e])
    other = 1 - sec
    half = own_half()
    image = img_s.reshape(tall // steps, steps, n, width)
    first, second = keys * n, keys * n + n * half_tok
    for ref, at in ((extra_keep, sec), (extra_send, other)):
        ref[:first] = image[:keys, at].reshape(first, width).astype(BF16)
        ref[first:second] = blk_s[:, at].reshape(second - first, width)
        ref[second:, : prp_s.shape[3]] = prp_s[:, at].reshape(n * ptok, -1)
        ref[second:, prp_s.shape[3] :] = jnp.zeros((n * ptok, width - prp_s.shape[3]), BF16)
    for ref, at, chain in ((keep0, half, 0), (keep1, half, 1), (send0, 1 - half, 0), (send1, 1 - half, 1)):
        ref[...] = pack_s[at, 2 * chain : 2 * chain + 2]


def rows_of(images):
    return images.transpose(0, 2, 1, 3).reshape(-1, images.shape[-1])


def compute(args, table, total):
    images, proprio, view_mask, embodiment, ctx_steps = args[:5]
    weights, out_grad = args[5:21], args[21]
    samples, steps, keys, width = images.shape
    ptok, feats = proprio.shape[2:]
    emb, qry = weights[0].shape[:2]
    ffw = weights[12].shape[1]
    n = samples // CORES
    half_tok = qry + ptok
    ctx = steps * half_tok
    rows = n * ctx
    piece = total // (CORES * PIECES)
    lines = steps * keys
    tall = (lines + 31) // 32 * 32
    dims = (n, steps, keys, width, qry, ptok, emb, ffw, table, view_mask.shape[1])

    def low(*shape):
        return pltpu.VMEM(shape, BF16)

    def full(*shape):
        return pltpu.VMEM(shape, F32)

    small = (embodiment, ctx_steps, view_mask.T)
    scratch = [pltpu.SMEM(v.shape, v.dtype) for v in small]
    scratch += [low(*w.shape) for w in weights]
    scratch += [
        low(((n - 1) * lines + tall + 15) // 16 * 16, width),
        low(n, tall, width),
        low(n, steps, ptok, feats),
        low(n, ctx, width),
        low(emb, HEADS * qry, width),
        low(emb, width, HEADS * qry),
        low(n, steps, half_tok, width),
        low(n, width, tall),
        full(n, tall, HEADS * qry),
        full(n, tall, HEADS * qry),
        low(n, tall, (steps + 1) * width),
        low(n, width, (steps + 1) * width),
        low(n, width, steps * width),
        low(n, steps, qry, width),
        low(n * steps * ptok, width),
        full(n * steps * ptok, width),
        full(rows, width),
        full(rows, width),
        low(rows, width),
        low(rows, 3 * width),
        full(n, ctx, HEADS * ctx),
        low(n, ctx, HEADS * ctx),
        full(n, ctx, HEADS * ctx),
        low(rows, width),
        full(rows, width),
        full(rows, ffw),
        full(rows, width),
        full(rows, width),
        low(rows, width),
        low(rows, ffw),
        low(rows, width),
        low(rows, ffw),
        full(rows, width),
        low(rows, width),
        low(rows, width),
        low(rows, 3 * width),
        low(n, steps, half_tok, width),
        low(n, steps, qry, width),
        low(n, steps, half_tok, width),
        full(tall * n, width),
        low(n, steps, ptok, feats),
        full(emb, width, HEADS * qry),
        full(emb, width, width),
        low(CORES, PIECES, piece, width),
        pltpu.SemaphoreType.DMA((22,)),
    ]
    inputs = (*small, rows_of(images), proprio, out_grad, *weights)
    return pl.pallas_call(
        functools.partial(compute_kernel, dims),
        out_shape=(
            low(2, piece, width),
            low(2, piece, width),
            low(2, piece, width),
            low(2, piece, width),
            low(keys * n + n * half_tok + n * ptok, width),
            low(keys * n + n * half_tok + n * ptok, width),
        ),
        in_specs=[ANY] * 22,
        out_specs=(VMEM,) * 6,
        scratch_shapes=scratch,
        compiler_params=pltpu.CompilerParams(vmem_limit_bytes=40 * 2**20),
        name="stem_trunk",
    )(*(pltpu.with_memory_space_constraint(v, pltpu.HBM) for v in inputs))


def parity(index, levels):
    total = index & 1
    for level in range(1, levels):
        total = total ^ ((index >> level) & 1)
    return total


def own_half():
    levels = lax.axis_size("dp").bit_length() - 1
    return lax.axis_index("section") ^ parity(lax.axis_index("dp"), levels)


def own_bits(half):
    dp = lax.axis_index("dp")
    low, high = dp & 1, (dp >> 1) & 1
    return jnp.where(half == 0, low, high), jnp.where(half == 0, high, low)


def select(bit, low, high):
    return jnp.where(bit == 0, low, high)


def add(held, came):
    return (held.astype(F32) + came.astype(F32)).astype(BF16)


def swap_cores(value):
    return lax.ppermute(value, "section", [(0, 1), (1, 0)])


def swap_chips(value, bits):
    count = lax.axis_size("dp")
    levels = count.bit_length() - 1
    pairs = []
    for core in range(CORES):
        for i in range(count):
            bit = bits[core ^ parity(i, levels)]
            pairs.append((core * count + i, (1 - core) * count + (i ^ (1 << bit))))
    return lax.ppermute(value, ("section", "dp"), pairs)


def send_kernel(count, *refs):
    sem = refs[-1]
    copies = [pltpu.make_async_copy(refs[i], refs[count + i], sem.at[i]) for i in range(count)]
    for copy in copies:
        copy.start()
    for copy in copies:
        copy.wait()


def send_out(*values):
    return pl.pallas_call(
        functools.partial(send_kernel, len(values)),
        out_shape=tuple(jax.ShapeDtypeStruct(v.shape, v.dtype) for v in values),
        in_specs=[VMEM] * len(values),
        out_specs=(ANY,) * len(values),
        scratch_shapes=[pltpu.SemaphoreType.DMA((len(values),))],
        compiler_params=pltpu.CompilerParams(vmem_limit_bytes=8 * 2**20),
        name="send_out",
    )(*(pltpu.with_memory_space_constraint(v, pltpu.VMEM) for v in values))


def finish_kernel(table, *refs):
    pieces, refs = refs[: CORES * PIECES], refs[CORES * PIECES :]
    count = len(refs) // 2 - 1
    outs, held, (pack, sem) = refs[:count], refs[count : 2 * count], refs[2 * count :]
    size, width = pieces[0].shape
    own = own_half()
    for i, ref in enumerate(pieces):
        half = own if i < PIECES else 1 - own
        chain, far = i % CHAINS, i // CHAINS % 2
        at = half * PIECES + chain * 2 + (own_bits(half)[0] ^ far)
        pack[pl.ds(pl.multiple_of(at * size, size), size)] = ref[...]
    names = ("queries", "keyw", "valuew", "stem", "lift", "mixer", "again", "abias", "qkv", "aproj")
    names += ("mgain", "mbias", "up", "upb", "down", "downb")
    vectors = pack[pl.ds(table["vectors"][0], 16)].astype(F32)
    rows = {"again": 0, "abias": 1, "mgain": 2, "mbias": 3, "downb": 4}
    copies = []
    for i, (name, out, ref) in enumerate(zip(names, outs, held)):
        if name in rows:
            ref[...] = vectors[rows[name]]
        elif name == "upb":
            for j in range(ref.shape[0] // width):
                ref[width * j : width * (j + 1)] = vectors[5 + j]
        else:
            first, total = table[name]
            wide = ref.shape[-1] // width
            for j in range(wide):
                part = pack[first + total // wide * j : first + total // wide * (j + 1)].astype(F32)
                if ref.ndim == 3:
                    ref[...] = part.reshape(ref.shape)
                else:
                    ref[:, width * j : width * (j + 1)] = part
        copies.append(pltpu.make_async_copy(ref, out, sem.at[i]))
        copies[-1].start()
    for copy in copies:
        copy.wait()


def finish(table, pieces, shapes):
    total = len(pieces) * pieces[0].shape[0]
    return pl.pallas_call(
        functools.partial(finish_kernel, table),
        out_shape=tuple(jax.ShapeDtypeStruct(v, F32) for v in shapes),
        in_specs=[VMEM] * len(pieces),
        out_specs=(ANY,) * len(shapes),
        scratch_shapes=[pltpu.VMEM(v, F32) for v in shapes]
        + [pltpu.VMEM((total, pieces[0].shape[1]), BF16), pltpu.SemaphoreType.DMA((len(shapes),))],
        compiler_params=pltpu.CompilerParams(vmem_limit_bytes=24 * 2**20),
        name="finish",
    )(*(pltpu.with_memory_space_constraint(v, pltpu.VMEM) for v in pieces))


def sum_chips(held, came, extra):
    levels = lax.axis_size("dp").bit_length() - 1
    first, second = (0, 1), (1, 0)
    half = own_half()
    one, two = own_bits(half)
    totals = [add(a, b) for a, b in zip(held, came)]
    *totals[1:], extra = lax.optimization_barrier((*totals[1:], extra))
    for bit, bits in ((one, first), (two, second)):
        split = [t.reshape((2, -1, t.shape[-1])) for t in totals]
        sent = [swap_chips(select(bit, t[1], t[0]), bits) for t in split]
        totals = [add(select(bit, t[0], t[1]), c) for t, c in zip(split, sent)]
    extra = swap_cores(extra)
    for bits in zip(range(2, levels), reversed(range(2, levels))):
        sent = [swap_chips(t, bits) for t in totals]
        totals = [add(t, c) for t, c in zip(totals, sent)]
    sent = [swap_chips(t, second) for t in totals]
    near = [either(two, t, c) for t, c in zip(totals, sent)]
    far = [swap_chips(t, first) for t in near]
    return near + far + [swap_cores(t) for t in near + far], extra


def either(bit, mine, came, axis=0):
    return select(bit, jnp.concatenate([mine, came], axis), jnp.concatenate([came, mine], axis))


def per_device(*args):
    images, proprio, weights = args[0], args[1], args[5:21]
    emb, qry, width = weights[0].shape
    n, keys = images.shape[0] // CORES, images.shape[2]
    ptok, feats = proprio.shape[2:]
    table, total = layout(width, weights[12].shape[1], emb, qry, weights[4].shape[1])
    *packed, extra, extra_sent = compute(args, table, total)
    keep, send = packed[:CHAINS], packed[CHAINS:]
    pieces, came = sum_chips(keep, [swap_cores(v) for v in send], extra_sent)
    sec = lax.axis_index("section")
    first, second = keys * n, keys * n + n * (qry + ptok)
    img = either(sec, *(v[:first].reshape(keys, n, width) for v in (extra, came)), 1)
    blk = either(sec, *(v[first:second].reshape(n, -1, width) for v in (extra, came)))
    prp = either(sec, *(v[second:, :feats].reshape(n, ptok, feats) for v in (extra, came)))
    blk, img, prp = send_out(blk, img, prp)
    grads = finish(table, pieces, [w.shape for w in weights])
    return (blk, img.transpose(1, 0, 2)[:, None], prp[:, None]) + tuple(grads)


def solution(mesh):
    sample = [P("dp")] * 5
    return jax.shard_map(
        per_device,
        mesh=mesh,
        in_specs=tuple(sample + [P()] * 16 + [P("dp")]),
        out_specs=(P("dp", "section"),) * 3 + (P(),) * 16,
        check_vma=False,
    )
```

```python
import functools
import math

import jax
import jax.numpy as jnp
from jax import lax
from jax.experimental import pallas as pl
from jax.experimental.pallas import tpu as pltpu
from jax.sharding import PartitionSpec as P

HEADS = 8
F32 = jnp.float32
BF16 = jnp.bfloat16
CORES = 2
CHAINS = 2
PIECES = 2 * CHAINS
EPS = 1e-05
LAG = 8
INV_SQRT2 = 1.0 / math.sqrt(2.0)
INV_SQRT2PI = 1.0 / math.sqrt(2.0 * math.pi)
ANY = pl.BlockSpec(memory_space=pl.ANY)
VMEM = pl.BlockSpec(memory_space=pltpu.VMEM)
SMEM = pl.BlockSpec(memory_space=pltpu.SMEM)


def mm(left, right):
    return lax.dot_general(left, right, (((1,), (0,)), ((), ())), preferred_element_type=F32)


def mm_bt(left, right):
    return lax.dot_general(left, right, (((1,), (1,)), ((), ())), preferred_element_type=F32)


def mm_at(left, right):
    return lax.dot_general(left, right, (((0,), (0,)), ((), ())), preferred_element_type=F32)


def layout(width, ffw, emb, queries, feats):
    counts = (
        ("keyw", emb * width),
        ("valuew", emb * width),
        ("mixer", emb * width),
        ("stem", width),
        ("lift", emb * feats),
        ("queries", emb * queries),
        ("qkv", 3 * width),
        ("aproj", width),
        ("up", ffw),
        ("down", ffw),
        ("vectors", 16),
    )
    table, first = {}, 0
    for name, rows in counts:
        table[name] = (first, rows)
        first += rows
    step = CORES * PIECES * 32
    return table, (first + step - 1) // step * step


def cuts(first, rows, piece):
    done = 0
    while done < rows:
        at = first + done
        count = min(rows - done, piece - at % piece)
        yield at // piece, at % piece, done, count
        done += count


def head_mask(rows, per_head, width):
    row = lax.broadcasted_iota(jnp.int32, (rows, width), 0) // per_head
    col = lax.broadcasted_iota(jnp.int32, (rows, width), 1) // (width // HEADS)
    return (row == col).astype(F32)


def spread(rows, mask):
    return jnp.concatenate([rows] * HEADS, axis=0) * mask


def fold(full, mask):
    per = full.shape[0] // HEADS
    return jnp.sum((full * mask).reshape(HEADS, per, full.shape[1]), axis=0)


def gelu_parts(values):
    cdf = 0.5 * (1.0 + lax.erf(values * INV_SQRT2))
    pdf = INV_SQRT2PI * jnp.exp(-0.5 * values * values)
    return values * cdf, cdf + values * pdf


def staged(count, *stages):
    for step in range(count + LAG * (len(stages) - 1)):
        for lag, stage in enumerate(stages):
            if 0 <= step - LAG * lag < count:
                stage(step - LAG * lag)


def softmax_rows(scores):
    expo = jnp.exp(scores - jnp.max(scores, axis=0, keepdims=True))
    return expo * (1.0 / jnp.sum(expo, axis=0, keepdims=True))


def per_step(row, reduce):
    part = reduce(row.reshape(-1, 8, row.shape[1]), axis=0)
    pair = jnp.maximum if reduce is jnp.max else jnp.add
    part = pair(part, pltpu.roll(part, 4, 0))
    return pair(part, pltpu.roll(part, 2, 0))


def softmax_lines(scores):
    expo = jnp.exp(scores.reshape(-1, 8, scores.shape[1]) - per_step(scores, jnp.max))
    return (expo * (1.0 / per_step(expo.reshape(scores.shape), jnp.sum))).reshape(scores.shape)


def softmax_lines_grad(probs, grad):
    terms = probs * grad
    total = per_step(terms, jnp.sum)
    tiles = (-1, 8, probs.shape[1])
    return (terms.reshape(tiles) - probs.reshape(tiles) * total).reshape(probs.shape)


def softmax_rows_grad(probs, grad):
    terms = probs * grad
    return terms - probs * jnp.sum(terms, axis=0, keepdims=True)


def row_mean(values):
    width = values.shape[1]
    high = values.astype(BF16)
    low = (values - high.astype(F32)).astype(BF16)
    ones = jnp.full((2 * width, width), 1.0 / width, BF16)
    return mm(jnp.concatenate([high, low], axis=1), ones)


def norm_parts(values):
    center = values - row_mean(values)
    rstd = lax.rsqrt(row_mean(center * center) + EPS)
    return center * rstd, rstd


def norm_grad(grad, gain, hat, rstd):
    scaled = grad * gain
    first = row_mean(scaled)
    second = row_mean(scaled * hat)
    return rstd * (scaled - first - hat * second)


def compute_kernel(
    dims,
    emb_h,
    steps_h,
    views_h,
    images,
    proprio,
    out_grad,
    queries_h,
    key_h,
    value_h,
    stem_h,
    lift_h,
    mix_h,
    again_h,
    abias_h,
    qkv_h,
    aproj_h,
    mgain_h,
    mbias_h,
    up_h,
    up_bh,
    down_h,
    down_bh,
    keep0,
    keep1,
    send0,
    send1,
    extra_keep,
    extra_send,
    emb_ref,
    steps_ref,
    views_ref,
    queries,
    key_w,
    value_w,
    stem_proj,
    lift_w,
    mix_w,
    again,
    abias,
    qkv_w,
    aproj,
    mgain,
    mbias,
    up_w,
    up_b,
    down_w,
    down_b,
    xin_s,
    x_s,
    p_s,
    g_s,
    qs_s,
    a_s,
    tok_s,
    xt_s,
    prob_s,
    sgrad_s,
    mix_s,
    ab_s,
    ut_s,
    satt_s,
    act_s,
    dact_s,
    hat1_s,
    rstd1_s,
    norm1_s,
    qkv_s,
    tprob_s,
    tlow_s,
    gprob_s,
    att_s,
    mid_s,
    pre_s,
    hat2_s,
    rstd2_s,
    norm2_s,
    up_s,
    glow_s,
    gpre_s,
    gn2_s,
    gmid_s,
    gatt_s,
    gqkv_s,
    gtok_s,
    gsatt_s,
    blk_s,
    img_s,
    prp_s,
    macc_s,
    vacc_s,
    pack_s,
    in_sem,
):
    n, steps, keys, width, qry, ptok, emb, ffw, table, views = dims
    half_tok = qry + ptok
    ctx = steps * half_tok
    rows = n * ctx
    scale = 1.0 / math.sqrt(width // HEADS)
    piece = pack_s.shape[2]
    scale_low = jnp.asarray(scale, BF16)
    sec = lax.axis_index("section")
    base = sec * n
    lines = steps * keys
    tall = x_s.shape[1]
    def put(name, row, value):
        first = table[name][0] + row
        for at, lo, done, count in cuts(first, value.shape[0], piece):
            pack_s[at // PIECES, at % PIECES, lo : lo + count] = value[done : done + count].astype(BF16)

    sources = (
        (emb_h, emb_ref),
        (queries_h, queries),
        (key_h, key_w),
        (images.at[pl.ds(pl.multiple_of(sec * n * lines, 16), n * lines)], xin_s.at[pl.ds(0, n * lines)]),
        (views_h, views_ref),
        (value_h, value_w),
        (proprio.at[pl.ds(base, n)], p_s),
        (lift_h, lift_w),
        (mix_h, mix_w),
        (stem_h, stem_proj),
        (again_h, again),
        (abias_h, abias),
        (qkv_h, qkv_w),
        (steps_h, steps_ref),
        (aproj_h, aproj),
        (mgain_h, mgain),
        (mbias_h, mbias),
        (up_h, up_w),
        (up_bh, up_b),
        (down_h, down_w),
        (down_bh, down_b),
        (out_grad.at[pl.ds(base, n)], g_s),
    )
    loads = [pltpu.make_async_copy(a, b, in_sem.at[i]) for i, (a, b) in enumerate(sources)]
    for copy in loads:
        copy.start()
    waited = [0]

    def ready(count):
        for copy in loads[waited[0] : count]:
            copy.wait()
        waited[0] = max(waited[0], count)

    smask = head_mask(HEADS * qry, qry, width)
    smask_low = smask.astype(BF16)
    tmask = head_mask(HEADS * ctx, ctx, width)
    tmask_low = tmask.astype(BF16)
    for e in range(emb):
        macc_s[e] = jnp.zeros((width, width), F32)
        vacc_s[e] = jnp.zeros((width, width), F32)
    used = max(first + count for first, count in table.values())
    for at, lo, _, count in cuts(used, CORES * PIECES * piece - used, piece):
        pack_s[at // PIECES, at % PIECES, lo : lo + count] = jnp.zeros((count, width), BF16)
    xin_s[n * lines :] = jnp.zeros((xin_s.shape[0] - n * lines, width), BF16)
    ready(3)
    embs = [emb_ref[base + s] for s in range(n)]
    for e in range(emb):
        qs = spread(queries[e], smask_low)
        qs_s[e] = qs
        a_s[e] = (mm_bt(key_w[e], qs) * scale).astype(BF16)

    ready(4)
    edge = lines // 16 * 16
    inside = lax.broadcasted_iota(jnp.int32, (tall - edge, width), 0) < lines - edge
    for s in range(n):
        x_s[s] = xin_s[lines * s : lines * s + tall]
        last = x_s[s, edge:].astype(F32)
        x_s[s, edge:] = jnp.where(inside, last, 0.0).astype(BF16)

    ready(9)
    emb_rows = jnp.concatenate([jnp.full((steps * ptok, width), e) for e in embs], axis=0)
    lift_cat = jnp.concatenate([lift_w[e] for e in range(emb)], axis=1)
    mix_cat = jnp.concatenate([mix_w[e] for e in range(emb)], axis=1)

    def own_columns(values):
        result = values[:, :width]
        for e in range(1, emb):
            result = jnp.where(emb_rows == e, values[:, width * e : width * (e + 1)], result)
        return result

    def spread_columns(values):
        parts = [jnp.where(emb_rows == e, values, 0.0).astype(BF16) for e in range(emb)]
        return jnp.concatenate(parts, axis=1)

    prop_rows = p_s[...].reshape(n * steps * ptok, -1)
    act, dact = gelu_parts(own_columns(mm(prop_rows, lift_cat)))
    act_s[...] = act.astype(BF16)
    dact_s[...] = dact
    prop_tok = own_columns(mm(act_s[...], mix_cat)).astype(BF16)
    tok_s[:, :, qry:] = prop_tok.reshape(n, steps, ptok, width)

    first_step = lax.broadcasted_iota(jnp.int32, (tall, width), 0) % steps == 0

    first_low = jnp.where(first_step, 1.0, 0.0).astype(BF16)

    def view_bias(s):
        lost = [jnp.where(views_ref[v, base + s] > 0, 0.0, -1e30).astype(F32) for v in range(views)]
        lost.append(jnp.float32(-1e30))
        ends = [lines // views * (v + 1) for v in range(views)]
        tiles, at = [], 0
        while at < tall:
            view = sum(at >= end for end in ends)
            stop = min([end // 8 * 8 for end in ends if end // 8 * 8 > at] + [tall])
            if view < views and ends[view] < at + 8:
                row = lax.broadcasted_iota(jnp.int32, (8, width), 0)
                tiles.append(jnp.where(row < ends[view] - at, lost[view], lost[view + 1]))
                at += 8
            else:
                tiles.append(jnp.full((stop - at, width), lost[view], F32))
                at = stop
        return jnp.concatenate(tiles, axis=0)

    def stem_scores(s):
        prob_s[s] = mm(x_s[s], a_s[embs[s]]) + view_bias(s)

    def stem_softmax(s):
        prob = softmax_lines(prob_s[s])
        prob_s[s] = prob
        prob_low = prob.astype(BF16)
        even = prob_low * first_low
        mix_s[s, :, :width] = even
        mix_s[s, :, width : 2 * width] = prob_low - even

    def stem_moments(s):
        turned = x_s[s].T
        xt_s[s] = turned
        ut_s[s] = mm(turned, mix_s[s, :, : 2 * width]).astype(BF16)

    def stem_values(s):
        values = mm(ut_s[s].T, value_w[embs[s]])
        for t in range(steps):
            satt_s[s, t] = fold(values[width * t : width * (t + 1)], smask).astype(BF16)

    ready(6)
    staged(n, stem_scores, stem_softmax, stem_moments, stem_values)
    ready(10)
    image_tok = mm(satt_s[...].reshape(n * steps * qry, width), stem_proj[...])
    tok_s[:, :, :qry] = image_tok.astype(BF16).reshape(n, steps, qry, width)

    ready(len(loads))
    group = n
    chunk = group * ctx
    spans = [pl.ds(i * chunk, chunk) for i in range(rows // chunk)]
    again_row = again[...].astype(F32).reshape(1, width)
    abias_row = abias[...].astype(F32).reshape(1, width)
    mgain_row = mgain[...].astype(F32).reshape(1, width)
    mbias_row = mbias[...].astype(F32).reshape(1, width)
    upb_row = up_b[...].astype(F32).reshape(1, ffw)
    downb_row = down_b[...].astype(F32).reshape(1, width)

    def tokens_of(i):
        return tok_s[group * i : group * (i + 1)].reshape(chunk, width).astype(F32)

    for i, span in enumerate(spans):
        hat, rstd = norm_parts(tokens_of(i))
        hat1_s[span] = hat
        rstd1_s[span] = jnp.broadcast_to(rstd, hat.shape)
        norm1 = (hat * again_row + abias_row).astype(BF16)
        norm1_s[span] = norm1
        qkv_s[span] = mm(norm1, qkv_w[...]).astype(BF16)

    key_step = lax.broadcasted_iota(jnp.int32, (ctx, 1), 0) // half_tok
    def trunk_rows(s):
        mine = pl.ds(s * ctx, ctx)
        return (qkv_s[mine, width * j : width * (j + 1)] for j in range(3))

    def trunk_scores(s):
        query, key, _ = trunk_rows(s)
        dead = jnp.where(key_step < steps_ref[base + s], 0.0, -1e30).astype(F32)
        tprob_s[s] = mm_bt(key, spread(query * scale_low, tmask_low)) + dead

    def trunk_softmax(s):
        prob = softmax_rows(tprob_s[s])
        tprob_s[s] = prob
        tlow_s[s] = prob.astype(BF16)

    def trunk_values(s):
        _, _, value = trunk_rows(s)
        att_s[pl.ds(s * ctx, ctx)] = fold(mm_at(tlow_s[s], value), tmask).astype(BF16)

    staged(n, trunk_scores, trunk_softmax, trunk_values)

    row_step = lax.broadcasted_iota(jnp.int32, (ctx, 1), 0) // half_tok
    sums = {name: jnp.zeros((1, width), F32) for name in ("mgain", "mbias", "downb")}
    sums["upb"] = jnp.zeros((1, ffw), F32)

    def total(name, values):
        sums[name] += jnp.sum(values, axis=0, keepdims=True)

    def live_rows(i):
        parts = [row_step < steps_ref[base + group * i + j] for j in range(group)]
        return jnp.concatenate([jnp.where(part, 1.0, 0.0).astype(F32) for part in parts], axis=0)

    def mlp_in(i):
        span = spans[i]
        middle = tokens_of(i) + mm(att_s[span], aproj[...])
        mid_s[span] = middle
        hat, rstd = norm_parts(middle)
        hat2_s[span] = hat
        rstd2_s[span] = jnp.broadcast_to(rstd, hat.shape)
        norm2 = (hat * mgain_row + mbias_row).astype(BF16)
        norm2_s[span] = norm2
        pre_s[span] = mm(norm2, up_w[...]) + upb_row

    def mlp_gelu(i):
        span = spans[i]
        act, dact = gelu_parts(pre_s[span])
        up_s[span] = act.astype(BF16)
        pre_s[span] = dact

    def mlp_back(i):
        span = spans[i]
        grad = g_s[group * i : group * (i + 1)].reshape(chunk, width).astype(F32) * live_rows(i)
        grad_low = grad.astype(BF16)
        glow_s[span] = grad_low
        total("downb", grad)
        grad_up = mm_bt(grad_low, down_w[...]).astype(BF16).astype(F32)
        grad_pre = (grad_up * pre_s[span]).astype(BF16)
        gpre_s[span] = grad_pre
        total("upb", grad_pre.astype(F32))

    def mlp_norm_back(i):
        span = spans[i]
        grad_norm2 = mm_bt(gpre_s[span], up_w[...]).astype(BF16).astype(F32)
        hat = hat2_s[span]
        total("mgain", grad_norm2 * hat)
        total("mbias", grad_norm2)
        grad_mid = norm_grad(grad_norm2, mgain_row, hat, rstd2_s[span]) + glow_s[span].astype(F32)
        gn2_s[span] = grad_mid
        grad_mid_low = grad_mid.astype(BF16)
        gmid_s[span] = grad_mid_low
        gatt_s[span] = mm_bt(grad_mid_low, aproj[...]).astype(BF16)

    def mlp_out(i):
        span = spans[i]
        result = (mid_s[span] + mm(up_s[span], down_w[...]) + downb_row) * live_rows(i)
        blk_s[group * i : group * (i + 1)] = result.astype(BF16).reshape(group, steps, half_tok, width)

    staged(len(spans), mlp_in, mlp_gelu, mlp_back, mlp_norm_back, mlp_out)

    def trunk_back_probs(s):
        _, _, value = trunk_rows(s)
        grad_spread = spread(gatt_s[pl.ds(s * ctx, ctx)], tmask_low)
        gprob_s[s] = mm_bt(value, grad_spread).astype(BF16)
        gqkv_s[pl.ds(s * ctx, ctx), 2 * width :] = mm(tlow_s[s], grad_spread).astype(BF16)

    def trunk_back_softmax(s):
        grad_prob = gprob_s[s].astype(F32)
        tlow_s[s] = softmax_rows_grad(tprob_s[s], grad_prob).astype(BF16)

    def trunk_back_rows(s):
        query, key, _ = trunk_rows(s)
        mine = pl.ds(s * ctx, ctx)
        gqkv_s[mine, :width] = (fold(mm_at(tlow_s[s], key), tmask) * scale).astype(BF16)
        gqkv_s[mine, width : 2 * width] = (mm(tlow_s[s], spread(query, tmask_low)) * scale).astype(BF16)

    staged(n, trunk_back_probs, trunk_back_softmax, trunk_back_rows)

    again_sum = jnp.zeros((1, width), F32)
    abias_sum = jnp.zeros((1, width), F32)
    for i, span in enumerate(spans):
        grad_norm1 = mm_bt(gqkv_s[span], qkv_w[...]).astype(BF16).astype(F32)
        hat = hat1_s[span]
        again_sum += jnp.sum(grad_norm1 * hat, axis=0, keepdims=True)
        abias_sum += jnp.sum(grad_norm1, axis=0, keepdims=True)
        grad_tok = norm_grad(grad_norm1, again_row, hat, rstd1_s[span]) + gn2_s[span]
        gtok_s[group * i : group * (i + 1)] = grad_tok.astype(BF16).reshape(group, steps, half_tok, width)
    qkv = mm_at(norm1_s[...], gqkv_s[...])
    for j in range(3):
        put("qkv", width * j, qkv[:, width * j : width * (j + 1)])
    vectors = [again_sum, abias_sum, sums["mgain"], sums["mbias"], sums["downb"]]
    vectors += [sums["upb"][:, width * j : width * (j + 1)] for j in range(ffw // width)]
    vectors += [jnp.zeros((16 - len(vectors), width), F32)]
    put("vectors", 0, jnp.concatenate(vectors, axis=0))

    put("aproj", 0, mm_at(att_s[...], gmid_s[...]))
    down = mm_at(glow_s[...], up_s[...]).astype(BF16)
    up = mm_at(norm2_s[...], gpre_s[...])
    for j in range(ffw // width):
        cols = slice(width * j, width * (j + 1))
        put("down", width * j, down[:, cols].T)
        put("up", width * j, up[:, cols])

    grad_prop = spread_columns(gtok_s[:, :, qry:].reshape(n * steps * ptok, width).astype(F32))
    mixer = mm_at(act_s[...], grad_prop)
    grad_act = mm_bt(grad_prop, mix_cat).astype(BF16).astype(F32)
    grad_lift = spread_columns((grad_act * dact_s[...]).astype(BF16).astype(F32))
    lift = mm_at(prop_rows, grad_lift)
    for e in range(emb):
        put("mixer", width * e, mixer[:, width * e : width * (e + 1)])
        put("lift", lift.shape[0] * e, lift[:, width * e : width * (e + 1)])
    prp_s[...] = mm_bt(grad_lift, lift_cat).astype(BF16).reshape(n, steps, ptok, -1)

    grad_img = gtok_s[:, :, :qry].reshape(n * steps * qry, width)
    put("stem", 0, mm_at(satt_s[...].reshape(n * steps * qry, width), grad_img))
    gsatt_s[...] = mm_bt(grad_img, stem_proj[...]).astype(BF16).reshape(n, steps, qry, width)

    def stem_back_values(s):
        spreads = [spread(gsatt_s[s, t], smask_low) for t in range(steps)]
        grad_spread = jnp.concatenate(spreads, axis=0)
        ab_s[s, :, : 2 * width] = mm_bt(value_w[embs[s]], grad_spread).astype(BF16)
        ab_s[s, :, 2 * width :] = a_s[embs[s]]
        vacc_s[embs[s]] += mm(ut_s[s], grad_spread)

    def stem_back_probs(s):
        both = mm(x_s[s], ab_s[s, :, : 2 * width])
        sgrad_s[s] = jnp.where(first_step, both[:, :width], both[:, width:]).astype(BF16)

    def stem_back_softmax(s):
        grad_prob = sgrad_s[s].astype(F32)
        mix_s[s, :, 2 * width :] = softmax_lines_grad(prob_s[s], grad_prob).astype(BF16)

    def stem_back_moments(s):
        macc_s[embs[s]] += mm(xt_s[s], mix_s[s, :, 2 * width :])

    def image_gradient(s):
        img_s[pl.ds(s, tall, stride=n)] = mm_bt(mix_s[s], ab_s[s])

    staged(n, stem_back_values, stem_back_probs, stem_back_softmax, stem_back_moments, image_gradient)

    for e in range(emb):
        moment = (macc_s[e] * scale).astype(BF16)
        put("keyw", width * e, mm(moment, qs_s[e]))
        put("queries", qry * e, fold(mm_at(moment, key_w[e]), smask))
        put("valuew", width * e, vacc_s[e])
    other = 1 - sec
    half = own_half()
    image = img_s.reshape(tall // steps, steps, n, width)
    first, second = keys * n, keys * n + n * half_tok
    for ref, at in ((extra_keep, sec), (extra_send, other)):
        ref[:first] = image[:keys, at].reshape(first, width).astype(BF16)
        ref[first:second] = blk_s[:, at].reshape(second - first, width)
        ref[second:, : prp_s.shape[3]] = prp_s[:, at].reshape(n * ptok, -1)
        ref[second:, prp_s.shape[3] :] = jnp.zeros((n * ptok, width - prp_s.shape[3]), BF16)
    for ref, at, chain in ((keep0, half, 0), (keep1, half, 1), (send0, 1 - half, 0), (send1, 1 - half, 1)):
        ref[...] = pack_s[at, 2 * chain : 2 * chain + 2]


def rows_of(images):
    return images.transpose(0, 2, 1, 3).reshape(-1, images.shape[-1])


def compute(args, table, total):
    images, proprio, view_mask, embodiment, ctx_steps = args[:5]
    weights, out_grad = args[5:21], args[21]
    samples, steps, keys, width = images.shape
    ptok, feats = proprio.shape[2:]
    emb, qry = weights[0].shape[:2]
    ffw = weights[12].shape[1]
    n = samples // CORES
    half_tok = qry + ptok
    ctx = steps * half_tok
    rows = n * ctx
    piece = total // (CORES * PIECES)
    lines = steps * keys
    tall = (lines + 31) // 32 * 32
    dims = (n, steps, keys, width, qry, ptok, emb, ffw, table, view_mask.shape[1])

    def low(*shape):
        return pltpu.VMEM(shape, BF16)

    def full(*shape):
        return pltpu.VMEM(shape, F32)

    small = (embodiment, ctx_steps, view_mask.T)
    scratch = [pltpu.SMEM(v.shape, v.dtype) for v in small]
    scratch += [low(*w.shape) for w in weights]
    scratch += [
        low(((n - 1) * lines + tall + 15) // 16 * 16, width),
        low(n, tall, width),
        low(n, steps, ptok, feats),
        low(n, ctx, width),
        low(emb, HEADS * qry, width),
        low(emb, width, HEADS * qry),
        low(n, steps, half_tok, width),
        low(n, width, tall),
        full(n, tall, HEADS * qry),
        low(n, tall, HEADS * qry),
        low(n, tall, (steps + 1) * width),
        low(n, width, (steps + 1) * width),
        low(n, width, steps * width),
        low(n, steps, qry, width),
        low(n * steps * ptok, width),
        full(n * steps * ptok, width),
        full(rows, width),
        full(rows, width),
        low(rows, width),
        low(rows, 3 * width),
        full(n, ctx, HEADS * ctx),
        low(n, ctx, HEADS * ctx),
        low(n, ctx, HEADS * ctx),
        low(rows, width),
        full(rows, width),
        full(rows, ffw),
        full(rows, width),
        full(rows, width),
        low(rows, width),
        low(rows, ffw),
        low(rows, width),
        low(rows, ffw),
        full(rows, width),
        low(rows, width),
        low(rows, width),
        low(rows, 3 * width),
        low(n, steps, half_tok, width),
        low(n, steps, qry, width),
        low(n, steps, half_tok, width),
        full(tall * n, width),
        low(n, steps, ptok, feats),
        full(emb, width, HEADS * qry),
        full(emb, width, width),
        low(CORES, PIECES, piece, width),
        pltpu.SemaphoreType.DMA((22,)),
    ]
    inputs = (*small, rows_of(images), proprio, out_grad, *weights)
    return pl.pallas_call(
        functools.partial(compute_kernel, dims),
        out_shape=(
            low(2, piece, width),
            low(2, piece, width),
            low(2, piece, width),
            low(2, piece, width),
            low(keys * n + n * half_tok + n * ptok, width),
            low(keys * n + n * half_tok + n * ptok, width),
        ),
        in_specs=[ANY] * 22,
        out_specs=(VMEM,) * 6,
        scratch_shapes=scratch,
        compiler_params=pltpu.CompilerParams(vmem_limit_bytes=40 * 2**20),
        name="stem_trunk",
    )(*(pltpu.with_memory_space_constraint(v, pltpu.HBM) for v in inputs))


def parity(index, levels):
    total = index & 1
    for level in range(1, levels):
        total = total ^ ((index >> level) & 1)
    return total


def own_half():
    levels = lax.axis_size("dp").bit_length() - 1
    return lax.axis_index("section") ^ parity(lax.axis_index("dp"), levels)


def own_bits(half):
    dp = lax.axis_index("dp")
    low, high = dp & 1, (dp >> 1) & 1
    return jnp.where(half == 0, low, high), jnp.where(half == 0, high, low)


def select(bit, low, high):
    return jnp.where(bit == 0, low, high)


def add(held, came):
    return (held.astype(F32) + came.astype(F32)).astype(BF16)


def swap_cores(value):
    return lax.ppermute(value, "section", [(0, 1), (1, 0)])


def swap_chips(value, bits):
    count = lax.axis_size("dp")
    levels = count.bit_length() - 1
    pairs = []
    for core in range(CORES):
        for i in range(count):
            bit = bits[core ^ parity(i, levels)]
            pairs.append((core * count + i, (1 - core) * count + (i ^ (1 << bit))))
    return lax.ppermute(value, ("section", "dp"), pairs)


def send_kernel(count, *refs):
    sem = refs[-1]
    copies = [pltpu.make_async_copy(refs[i], refs[count + i], sem.at[i]) for i in range(count)]
    for copy in copies:
        copy.start()
    for copy in copies:
        copy.wait()


def send_out(*values):
    return pl.pallas_call(
        functools.partial(send_kernel, len(values)),
        out_shape=tuple(jax.ShapeDtypeStruct(v.shape, v.dtype) for v in values),
        in_specs=[VMEM] * len(values),
        out_specs=(ANY,) * len(values),
        scratch_shapes=[pltpu.SemaphoreType.DMA((len(values),))],
        compiler_params=pltpu.CompilerParams(vmem_limit_bytes=8 * 2**20),
        name="send_out",
    )(*(pltpu.with_memory_space_constraint(v, pltpu.VMEM) for v in values))


def finish_kernel(table, *refs):
    pieces, refs = refs[: CORES * PIECES], refs[CORES * PIECES :]
    count = len(refs) // 2 - 1
    outs, held, (pack, sem) = refs[:count], refs[count : 2 * count], refs[2 * count :]
    size, width = pieces[0].shape
    own = own_half()
    for i, ref in enumerate(pieces):
        half = own if i < PIECES else 1 - own
        chain, far = i % CHAINS, i // CHAINS % 2
        at = half * PIECES + chain * 2 + (own_bits(half)[0] ^ far)
        pack[pl.ds(pl.multiple_of(at * size, size), size)] = ref[...]
    names = ("queries", "keyw", "valuew", "stem", "lift", "mixer", "again", "abias", "qkv", "aproj")
    names += ("mgain", "mbias", "up", "upb", "down", "downb")
    vectors = pack[pl.ds(table["vectors"][0], 16)].astype(F32)
    rows = {"again": 0, "abias": 1, "mgain": 2, "mbias": 3, "downb": 4}
    copies = []
    for i, (name, out, ref) in enumerate(zip(names, outs, held)):
        if name in rows:
            ref[...] = vectors[rows[name]]
        elif name == "upb":
            for j in range(ref.shape[0] // width):
                ref[width * j : width * (j + 1)] = vectors[5 + j]
        else:
            first, total = table[name]
            wide = ref.shape[-1] // width
            for j in range(wide):
                part = pack[first + total // wide * j : first + total // wide * (j + 1)].astype(F32)
                if ref.ndim == 3:
                    ref[...] = part.reshape(ref.shape)
                else:
                    ref[:, width * j : width * (j + 1)] = part
        copies.append(pltpu.make_async_copy(ref, out, sem.at[i]))
        copies[-1].start()
    for copy in copies:
        copy.wait()


def finish(table, pieces, shapes):
    total = len(pieces) * pieces[0].shape[0]
    return pl.pallas_call(
        functools.partial(finish_kernel, table),
        out_shape=tuple(jax.ShapeDtypeStruct(v, F32) for v in shapes),
        in_specs=[VMEM] * len(pieces),
        out_specs=(ANY,) * len(shapes),
        scratch_shapes=[pltpu.VMEM(v, F32) for v in shapes]
        + [pltpu.VMEM((total, pieces[0].shape[1]), BF16), pltpu.SemaphoreType.DMA((len(shapes),))],
        compiler_params=pltpu.CompilerParams(vmem_limit_bytes=24 * 2**20),
        name="finish",
    )(*(pltpu.with_memory_space_constraint(v, pltpu.VMEM) for v in pieces))


def sum_chips(held, came, extra):
    levels = lax.axis_size("dp").bit_length() - 1
    first, second = (0, 1), (1, 0)
    half = own_half()
    one, two = own_bits(half)
    totals = [add(a, b) for a, b in zip(held, came)]
    *totals[1:], extra = lax.optimization_barrier((*totals[1:], extra))
    for bit, bits in ((one, first), (two, second)):
        split = [t.reshape((2, -1, t.shape[-1])) for t in totals]
        sent = [swap_chips(select(bit, t[1], t[0]), bits) for t in split]
        totals = [add(select(bit, t[0], t[1]), c) for t, c in zip(split, sent)]
    extra = swap_cores(extra)
    for bits in zip(range(2, levels), reversed(range(2, levels))):
        sent = [swap_chips(t, bits) for t in totals]
        totals = [add(t, c) for t, c in zip(totals, sent)]
    sent = [swap_chips(t, second) for t in totals]
    near = [either(two, t, c) for t, c in zip(totals, sent)]
    far = [swap_chips(t, first) for t in near]
    return near + far + [swap_cores(t) for t in near + far], extra


def either(bit, mine, came, axis=0):
    return select(bit, jnp.concatenate([mine, came], axis), jnp.concatenate([came, mine], axis))


def per_device(*args):
    images, proprio, weights = args[0], args[1], args[5:21]
    emb, qry, width = weights[0].shape
    n, keys = images.shape[0] // CORES, images.shape[2]
    ptok, feats = proprio.shape[2:]
    table, total = layout(width, weights[12].shape[1], emb, qry, weights[4].shape[1])
    *packed, extra, extra_sent = compute(args, table, total)
    keep, send = packed[:CHAINS], packed[CHAINS:]
    pieces, came = sum_chips(keep, [swap_cores(v) for v in send], extra_sent)
    sec = lax.axis_index("section")
    first, second = keys * n, keys * n + n * (qry + ptok)
    img = either(sec, *(v[:first].reshape(keys, n, width) for v in (extra, came)), 1)
    blk = either(sec, *(v[first:second].reshape(n, -1, width) for v in (extra, came)))
    prp = either(sec, *(v[second:, :feats].reshape(n, ptok, feats) for v in (extra, came)))
    blk, img, prp = send_out(blk, img, prp)
    grads = finish(table, pieces, [w.shape for w in weights])
    return (blk, img.transpose(1, 0, 2)[:, None], prp[:, None]) + tuple(grads)


def solution(mesh):
    sample = [P("dp")] * 5
    return jax.shard_map(
        per_device,
        mesh=mesh,
        in_specs=tuple(sample + [P()] * 16 + [P("dp")]),
        out_specs=(P("dp", "section"),) * 3 + (P(),) * 16,
        check_vma=False,
    )
```

```python
import functools
import math

import jax
import jax.numpy as jnp
from jax import lax
from jax.experimental import pallas as pl
from jax.experimental.pallas import tpu as pltpu
from jax.sharding import PartitionSpec as P

HEADS = 8
F32 = jnp.float32
BF16 = jnp.bfloat16
CORES = 2
CHAINS = 2
PIECES = 2 * CHAINS
EPS = 1e-05
LAG = 8
INV_SQRT2 = 1.0 / math.sqrt(2.0)
INV_SQRT2PI = 1.0 / math.sqrt(2.0 * math.pi)
ANY = pl.BlockSpec(memory_space=pl.ANY)
VMEM = pl.BlockSpec(memory_space=pltpu.VMEM)
SMEM = pl.BlockSpec(memory_space=pltpu.SMEM)


def mm(left, right):
    return lax.dot_general(left, right, (((1,), (0,)), ((), ())), preferred_element_type=F32)


def mm_bt(left, right):
    return lax.dot_general(left, right, (((1,), (1,)), ((), ())), preferred_element_type=F32)


def mm_at(left, right):
    return lax.dot_general(left, right, (((0,), (0,)), ((), ())), preferred_element_type=F32)


def layout(width, ffw, emb, queries, feats):
    counts = (
        ("keyw", emb * width),
        ("valuew", emb * width),
        ("mixer", emb * width),
        ("stem", width),
        ("lift", emb * feats),
        ("queries", emb * queries),
        ("qkv", 3 * width),
        ("aproj", width),
        ("up", ffw),
        ("down", ffw),
        ("vectors", 16),
    )
    table, first = {}, 0
    for name, rows in counts:
        table[name] = (first, rows)
        first += rows
    step = CORES * PIECES * 32
    return table, (first + step - 1) // step * step


def cuts(first, rows, piece):
    done = 0
    while done < rows:
        at = first + done
        count = min(rows - done, piece - at % piece)
        yield at // piece, at % piece, done, count
        done += count


def head_mask(rows, per_head, width):
    row = lax.broadcasted_iota(jnp.int32, (rows, width), 0) // per_head
    col = lax.broadcasted_iota(jnp.int32, (rows, width), 1) // (width // HEADS)
    return (row == col).astype(F32)


def spread(rows, mask):
    return jnp.concatenate([rows] * HEADS, axis=0) * mask


def fold(full, mask):
    per = full.shape[0] // HEADS
    return jnp.sum((full * mask).reshape(HEADS, per, full.shape[1]), axis=0)


def gelu_parts(values):
    cdf = 0.5 * (1.0 + lax.erf(values * INV_SQRT2))
    pdf = INV_SQRT2PI * jnp.exp(-0.5 * values * values)
    return values * cdf, cdf + values * pdf


def staged(count, *stages):
    for step in range(count + LAG * (len(stages) - 1)):
        for lag, stage in enumerate(stages):
            if 0 <= step - LAG * lag < count:
                stage(step - LAG * lag)


def softmax_rows(scores):
    expo = jnp.exp(scores - jnp.max(scores, axis=0, keepdims=True))
    return expo * (1.0 / jnp.sum(expo, axis=0, keepdims=True))


def per_step(row, reduce):
    part = reduce(row.reshape(-1, 8, row.shape[1]), axis=0)
    pair = jnp.maximum if reduce is jnp.max else jnp.add
    part = pair(part, pltpu.roll(part, 4, 0))
    return pair(part, pltpu.roll(part, 2, 0))


def softmax_lines(scores):
    expo = jnp.exp(scores.reshape(-1, 8, scores.shape[1]) - per_step(scores, jnp.max))
    return (expo * (1.0 / per_step(expo.reshape(scores.shape), jnp.sum))).reshape(scores.shape)


def softmax_lines_grad(probs, grad):
    terms = probs * grad
    total = per_step(terms, jnp.sum)
    tiles = (-1, 8, probs.shape[1])
    return (terms.reshape(tiles) - probs.reshape(tiles) * total).reshape(probs.shape)


def softmax_rows_grad(probs, grad):
    terms = probs * grad
    return terms - probs * jnp.sum(terms, axis=0, keepdims=True)


def row_mean(values):
    width = values.shape[1]
    high = values.astype(BF16)
    low = (values - high.astype(F32)).astype(BF16)
    ones = jnp.full((2 * width, width), 1.0 / width, BF16)
    return mm(jnp.concatenate([high, low], axis=1), ones)


def norm_parts(values):
    center = values - row_mean(values)
    rstd = lax.rsqrt(row_mean(center * center) + EPS)
    return center * rstd, rstd


def norm_grad(grad, gain, hat, rstd):
    scaled = grad * gain
    first = row_mean(scaled)
    second = row_mean(scaled * hat)
    return rstd * (scaled - first - hat * second)


def compute_kernel(
    dims,
    emb_h,
    steps_h,
    views_h,
    images,
    proprio,
    out_grad,
    queries_h,
    key_h,
    value_h,
    stem_h,
    lift_h,
    mix_h,
    again_h,
    abias_h,
    qkv_h,
    aproj_h,
    mgain_h,
    mbias_h,
    up_h,
    up_bh,
    down_h,
    down_bh,
    keep0,
    keep1,
    send0,
    send1,
    extra_keep,
    extra_send,
    emb_ref,
    steps_ref,
    views_ref,
    queries,
    key_w,
    value_w,
    stem_proj,
    lift_w,
    mix_w,
    again,
    abias,
    qkv_w,
    aproj,
    mgain,
    mbias,
    up_w,
    up_b,
    down_w,
    down_b,
    xin_s,
    x_s,
    p_s,
    g_s,
    qs_s,
    qst_s,
    a_s,
    keys_s,
    tok_s,
    xt_s,
    prob_s,
    sgrad_s,
    mix_s,
    ab_s,
    ut_s,
    satt_s,
    act_s,
    dact_s,
    hat1_s,
    rstd1_s,
    norm1_s,
    qkv_s,
    tprob_s,
    tlow_s,
    gprob_s,
    att_s,
    mid_s,
    pre_s,
    hat2_s,
    rstd2_s,
    norm2_s,
    up_s,
    glow_s,
    gpre_s,
    gn2_s,
    gmid_s,
    gatt_s,
    gqkv_s,
    gtok_s,
    gsatt_s,
    blk_s,
    img_s,
    prp_s,
    macc_s,
    vacc_s,
    pack_s,
    in_sem,
):
    n, steps, keys, width, qry, ptok, emb, ffw, table, views = dims
    half_tok = qry + ptok
    ctx = steps * half_tok
    rows = n * ctx
    scale = 1.0 / math.sqrt(width // HEADS)
    piece = pack_s.shape[2]
    scale_low = jnp.asarray(scale, BF16)
    sec = lax.axis_index("section")
    base = sec * n
    lines = steps * keys
    tall = x_s.shape[1]
    def put(name, row, value):
        first = table[name][0] + row
        for at, lo, done, count in cuts(first, value.shape[0], piece):
            pack_s[at // PIECES, at % PIECES, lo : lo + count] = value[done : done + count].astype(BF16)

    sources = (
        (emb_h, emb_ref),
        (queries_h, queries),
        (key_h, key_w),
        (images.at[pl.ds(pl.multiple_of(sec * n * lines, 16), n * lines)], xin_s.at[pl.ds(0, n * lines)]),
        (views_h, views_ref),
        (value_h, value_w),
        (proprio.at[pl.ds(base, n)], p_s),
        (lift_h, lift_w),
        (mix_h, mix_w),
        (stem_h, stem_proj),
        (again_h, again),
        (abias_h, abias),
        (qkv_h, qkv_w),
        (steps_h, steps_ref),
        (aproj_h, aproj),
        (mgain_h, mgain),
        (mbias_h, mbias),
        (up_h, up_w),
        (up_bh, up_b),
        (down_h, down_w),
        (down_bh, down_b),
        (out_grad.at[pl.ds(base, n)], g_s),
    )
    loads = [pltpu.make_async_copy(a, b, in_sem.at[i]) for i, (a, b) in enumerate(sources)]
    for copy in loads:
        copy.start()
    waited = [0]

    def ready(count):
        for copy in loads[waited[0] : count]:
            copy.wait()
        waited[0] = max(waited[0], count)

    smask = head_mask(HEADS * qry, qry, width)
    smask_low = smask.astype(BF16)
    tmask = head_mask(HEADS * ctx, ctx, width)
    tmask_low = tmask.astype(BF16)
    for e in range(emb):
        macc_s[e] = jnp.zeros((width, width), F32)
        vacc_s[e] = jnp.zeros((width, width), F32)
    used = max(first + count for first, count in table.values())
    for at, lo, _, count in cuts(used, CORES * PIECES * piece - used, piece):
        pack_s[at // PIECES, at % PIECES, lo : lo + count] = jnp.zeros((count, width), BF16)
    xin_s[n * lines :] = jnp.zeros((xin_s.shape[0] - n * lines, width), BF16)
    ready(3)
    embs = [emb_ref[base + s] for s in range(n)]
    for e in range(emb):
        qs = spread(queries[e], smask_low)
        qs_s[e] = qs
        qst_s[e] = (qs * scale_low).T
        a_s[e] = (mm_bt(key_w[e], qs) * scale).astype(BF16)

    ready(4)
    edge = lines // 16 * 16
    inside = lax.broadcasted_iota(jnp.int32, (tall - edge, width), 0) < lines - edge
    for s in range(n):
        x_s[s] = xin_s[lines * s : lines * s + tall]
        last = x_s[s, edge:].astype(F32)
        x_s[s, edge:] = jnp.where(inside, last, 0.0).astype(BF16)

    ready(9)
    emb_rows = jnp.concatenate([jnp.full((steps * ptok, width), e) for e in embs], axis=0)
    lift_cat = jnp.concatenate([lift_w[e] for e in range(emb)], axis=1)
    mix_cat = jnp.concatenate([mix_w[e] for e in range(emb)], axis=1)

    def own_columns(values):
        result = values[:, :width]
        for e in range(1, emb):
            result = jnp.where(emb_rows == e, values[:, width * e : width * (e + 1)], result)
        return result

    def spread_columns(values):
        parts = [jnp.where(emb_rows == e, values, 0.0).astype(BF16) for e in range(emb)]
        return jnp.concatenate(parts, axis=1)

    prop_rows = p_s[...].reshape(n * steps * ptok, -1)
    act, dact = gelu_parts(own_columns(mm(prop_rows, lift_cat)))
    act_s[...] = act.astype(BF16)
    dact_s[...] = dact
    prop_tok = own_columns(mm(act_s[...], mix_cat)).astype(BF16)
    tok_s[:, :, qry:] = prop_tok.reshape(n, steps, ptok, width)

    first_step = lax.broadcasted_iota(jnp.int32, (tall, width), 0) % steps == 0

    first_low = jnp.where(first_step, 1.0, 0.0).astype(BF16)

    def view_bias(s):
        lost = [jnp.where(views_ref[v, base + s] > 0, 0.0, -1e30).astype(F32) for v in range(views)]
        lost.append(jnp.float32(-1e30))
        ends = [lines // views * (v + 1) for v in range(views)]
        tiles, at = [], 0
        while at < tall:
            view = sum(at >= end for end in ends)
            stop = min([end // 8 * 8 for end in ends if end // 8 * 8 > at] + [tall])
            if view < views and ends[view] < at + 8:
                row = lax.broadcasted_iota(jnp.int32, (8, width), 0)
                tiles.append(jnp.where(row < ends[view] - at, lost[view], lost[view + 1]))
                at += 8
            else:
                tiles.append(jnp.full((stop - at, width), lost[view], F32))
                at = stop
        return jnp.concatenate(tiles, axis=0)

    def stem_keys(s):
        keys_s[s] = mm(x_s[s], key_w[embs[s]]).astype(BF16)

    def stem_scores(s):
        prob_s[s] = mm(keys_s[s], qst_s[embs[s]]) + view_bias(s)

    def stem_softmax(s):
        prob = softmax_lines(prob_s[s])
        prob_s[s] = prob
        prob_low = prob.astype(BF16)
        even = prob_low * first_low
        mix_s[s, :, :width] = even
        mix_s[s, :, width : 2 * width] = prob_low - even

    def stem_moments(s):
        turned = x_s[s].T
        xt_s[s] = turned
        ut_s[s] = mm(turned, mix_s[s, :, : 2 * width]).astype(BF16)

    def stem_values(s):
        values = mm(ut_s[s].T, value_w[embs[s]])
        for t in range(steps):
            satt_s[s, t] = fold(values[width * t : width * (t + 1)], smask).astype(BF16)

    ready(6)
    staged(n, stem_keys, stem_scores, stem_softmax, stem_moments, stem_values)
    ready(10)
    image_tok = mm(satt_s[...].reshape(n * steps * qry, width), stem_proj[...])
    tok_s[:, :, :qry] = image_tok.astype(BF16).reshape(n, steps, qry, width)

    ready(len(loads))
    group = n
    chunk = group * ctx
    spans = [pl.ds(i * chunk, chunk) for i in range(rows // chunk)]
    again_row = again[...].astype(F32).reshape(1, width)
    abias_row = abias[...].astype(F32).reshape(1, width)
    mgain_row = mgain[...].astype(F32).reshape(1, width)
    mbias_row = mbias[...].astype(F32).reshape(1, width)
    upb_row = up_b[...].astype(F32).reshape(1, ffw)
    downb_row = down_b[...].astype(F32).reshape(1, width)

    def tokens_of(i):
        return tok_s[group * i : group * (i + 1)].reshape(chunk, width).astype(F32)

    for i, span in enumerate(spans):
        hat, rstd = norm_parts(tokens_of(i))
        hat1_s[span] = hat
        rstd1_s[span] = jnp.broadcast_to(rstd, hat.shape)
        norm1 = (hat * again_row + abias_row).astype(BF16)
        norm1_s[span] = norm1
        qkv_s[span] = mm(norm1, qkv_w[...]).astype(BF16)

    key_step = lax.broadcasted_iota(jnp.int32, (ctx, 1), 0) // half_tok
    def trunk_rows(s):
        mine = pl.ds(s * ctx, ctx)
        return (qkv_s[mine, width * j : width * (j + 1)] for j in range(3))

    def trunk_scores(s):
        query, key, _ = trunk_rows(s)
        dead = jnp.where(key_step < steps_ref[base + s], 0.0, -1e30).astype(F32)
        tprob_s[s] = mm_bt(key, spread(query * scale_low, tmask_low)) + dead

    def trunk_softmax(s):
        prob = softmax_rows(tprob_s[s])
        tprob_s[s] = prob
        tlow_s[s] = prob.astype(BF16)

    def trunk_values(s):
        _, _, value = trunk_rows(s)
        att_s[pl.ds(s * ctx, ctx)] = fold(mm_at(tlow_s[s], value), tmask).astype(BF16)

    staged(n, trunk_scores, trunk_softmax, trunk_values)

    row_step = lax.broadcasted_iota(jnp.int32, (ctx, 1), 0) // half_tok
    sums = {name: jnp.zeros((1, width), F32) for name in ("mgain", "mbias", "downb")}
    sums["upb"] = jnp.zeros((1, ffw), F32)

    def total(name, values):
        sums[name] += jnp.sum(values, axis=0, keepdims=True)

    def live_rows(i):
        parts = [row_step < steps_ref[base + group * i + j] for j in range(group)]
        return jnp.concatenate([jnp.where(part, 1.0, 0.0).astype(F32) for part in parts], axis=0)

    def mlp_in(i):
        span = spans[i]
        middle = tokens_of(i) + mm(att_s[span], aproj[...])
        mid_s[span] = middle
        hat, rstd = norm_parts(middle)
        hat2_s[span] = hat
        rstd2_s[span] = jnp.broadcast_to(rstd, hat.shape)
        norm2 = (hat * mgain_row + mbias_row).astype(BF16)
        norm2_s[span] = norm2
        pre_s[span] = mm(norm2, up_w[...]) + upb_row

    def mlp_gelu(i):
        span = spans[i]
        act, dact = gelu_parts(pre_s[span])
        up_s[span] = act.astype(BF16)
        pre_s[span] = dact

    def mlp_back(i):
        span = spans[i]
        grad = g_s[group * i : group * (i + 1)].reshape(chunk, width).astype(F32) * live_rows(i)
        grad_low = grad.astype(BF16)
        glow_s[span] = grad_low
        total("downb", grad)
        grad_up = mm_bt(grad_low, down_w[...]).astype(BF16).astype(F32)
        grad_pre = (grad_up * pre_s[span]).astype(BF16)
        gpre_s[span] = grad_pre
        total("upb", grad_pre.astype(F32))

    def mlp_norm_back(i):
        span = spans[i]
        grad_norm2 = mm_bt(gpre_s[span], up_w[...]).astype(BF16).astype(F32)
        hat = hat2_s[span]
        total("mgain", grad_norm2 * hat)
        total("mbias", grad_norm2)
        grad_mid = norm_grad(grad_norm2, mgain_row, hat, rstd2_s[span]) + glow_s[span].astype(F32)
        gn2_s[span] = grad_mid
        grad_mid_low = grad_mid.astype(BF16)
        gmid_s[span] = grad_mid_low
        gatt_s[span] = mm_bt(grad_mid_low, aproj[...]).astype(BF16)

    def mlp_out(i):
        span = spans[i]
        result = (mid_s[span] + mm(up_s[span], down_w[...]) + downb_row) * live_rows(i)
        blk_s[group * i : group * (i + 1)] = result.astype(BF16).reshape(group, steps, half_tok, width)

    staged(len(spans), mlp_in, mlp_gelu, mlp_back, mlp_norm_back, mlp_out)

    def trunk_back_probs(s):
        _, _, value = trunk_rows(s)
        grad_spread = spread(gatt_s[pl.ds(s * ctx, ctx)], tmask_low)
        gprob_s[s] = mm_bt(value, grad_spread).astype(BF16)
        gqkv_s[pl.ds(s * ctx, ctx), 2 * width :] = mm(tlow_s[s], grad_spread).astype(BF16)

    def trunk_back_softmax(s):
        grad_prob = gprob_s[s].astype(F32)
        tlow_s[s] = softmax_rows_grad(tprob_s[s], grad_prob).astype(BF16)

    def trunk_back_rows(s):
        query, key, _ = trunk_rows(s)
        mine = pl.ds(s * ctx, ctx)
        gqkv_s[mine, :width] = (fold(mm_at(tlow_s[s], key), tmask) * scale).astype(BF16)
        gqkv_s[mine, width : 2 * width] = (mm(tlow_s[s], spread(query, tmask_low)) * scale).astype(BF16)

    staged(n, trunk_back_probs, trunk_back_softmax, trunk_back_rows)

    again_sum = jnp.zeros((1, width), F32)
    abias_sum = jnp.zeros((1, width), F32)
    for i, span in enumerate(spans):
        grad_norm1 = mm_bt(gqkv_s[span], qkv_w[...]).astype(BF16).astype(F32)
        hat = hat1_s[span]
        again_sum += jnp.sum(grad_norm1 * hat, axis=0, keepdims=True)
        abias_sum += jnp.sum(grad_norm1, axis=0, keepdims=True)
        grad_tok = norm_grad(grad_norm1, again_row, hat, rstd1_s[span]) + gn2_s[span]
        gtok_s[group * i : group * (i + 1)] = grad_tok.astype(BF16).reshape(group, steps, half_tok, width)
    qkv = mm_at(norm1_s[...], gqkv_s[...])
    for j in range(3):
        put("qkv", width * j, qkv[:, width * j : width * (j + 1)])
    vectors = [again_sum, abias_sum, sums["mgain"], sums["mbias"], sums["downb"]]
    vectors += [sums["upb"][:, width * j : width * (j + 1)] for j in range(ffw // width)]
    vectors += [jnp.zeros((16 - len(vectors), width), F32)]
    put("vectors", 0, jnp.concatenate(vectors, axis=0))

    put("aproj", 0, mm_at(att_s[...], gmid_s[...]))
    down = mm_at(glow_s[...], up_s[...]).astype(BF16)
    up = mm_at(norm2_s[...], gpre_s[...])
    for j in range(ffw // width):
        cols = slice(width * j, width * (j + 1))
        put("down", width * j, down[:, cols].T)
        put("up", width * j, up[:, cols])

    grad_prop = spread_columns(gtok_s[:, :, qry:].reshape(n * steps * ptok, width).astype(F32))
    mixer = mm_at(act_s[...], grad_prop)
    grad_act = mm_bt(grad_prop, mix_cat).astype(BF16).astype(F32)
    grad_lift = spread_columns((grad_act * dact_s[...]).astype(BF16).astype(F32))
    lift = mm_at(prop_rows, grad_lift)
    for e in range(emb):
        put("mixer", width * e, mixer[:, width * e : width * (e + 1)])
        put("lift", lift.shape[0] * e, lift[:, width * e : width * (e + 1)])
    prp_s[...] = mm_bt(grad_lift, lift_cat).astype(BF16).reshape(n, steps, ptok, -1)

    grad_img = gtok_s[:, :, :qry].reshape(n * steps * qry, width)
    put("stem", 0, mm_at(satt_s[...].reshape(n * steps * qry, width), grad_img))
    gsatt_s[...] = mm_bt(grad_img, stem_proj[...]).astype(BF16).reshape(n, steps, qry, width)

    def stem_back_values(s):
        spreads = [spread(gsatt_s[s, t], smask_low) for t in range(steps)]
        grad_spread = jnp.concatenate(spreads, axis=0)
        ab_s[s, :, : 2 * width] = mm_bt(value_w[embs[s]], grad_spread).astype(BF16)
        ab_s[s, :, 2 * width :] = a_s[embs[s]]
        vacc_s[embs[s]] += mm(ut_s[s], grad_spread)

    def stem_back_probs(s):
        both = mm(x_s[s], ab_s[s, :, : 2 * width])
        sgrad_s[s] = jnp.where(first_step, both[:, :width], both[:, width:]).astype(BF16)

    def stem_back_softmax(s):
        grad_prob = sgrad_s[s].astype(F32)
        mix_s[s, :, 2 * width :] = softmax_lines_grad(prob_s[s], grad_prob).astype(BF16)

    def stem_back_moments(s):
        macc_s[embs[s]] += mm(xt_s[s], mix_s[s, :, 2 * width :])

    def image_gradient(s):
        img_s[pl.ds(s, tall, stride=n)] = mm_bt(mix_s[s], ab_s[s])

    staged(n, stem_back_values, stem_back_probs, stem_back_softmax, stem_back_moments, image_gradient)

    for e in range(emb):
        moment = (macc_s[e] * scale).astype(BF16)
        put("keyw", width * e, mm(moment, qs_s[e]))
        put("queries", qry * e, fold(mm_at(moment, key_w[e]), smask))
        put("valuew", width * e, vacc_s[e])
    other = 1 - sec
    half = own_half()
    image = img_s.reshape(tall // steps, steps, n, width)
    first, second = keys * n, keys * n + n * half_tok
    for ref, at in ((extra_keep, sec), (extra_send, other)):
        ref[:first] = image[:keys, at].reshape(first, width).astype(BF16)
        ref[first:second] = blk_s[:, at].reshape(second - first, width)
        ref[second:, : prp_s.shape[3]] = prp_s[:, at].reshape(n * ptok, -1)
        ref[second:, prp_s.shape[3] :] = jnp.zeros((n * ptok, width - prp_s.shape[3]), BF16)
    for ref, at, chain in ((keep0, half, 0), (keep1, half, 1), (send0, 1 - half, 0), (send1, 1 - half, 1)):
        ref[...] = pack_s[at, 2 * chain : 2 * chain + 2]


def rows_of(images):
    return images.transpose(0, 2, 1, 3).reshape(-1, images.shape[-1])


def compute(args, table, total):
    images, proprio, view_mask, embodiment, ctx_steps = args[:5]
    weights, out_grad = args[5:21], args[21]
    samples, steps, keys, width = images.shape
    ptok, feats = proprio.shape[2:]
    emb, qry = weights[0].shape[:2]
    ffw = weights[12].shape[1]
    n = samples // CORES
    half_tok = qry + ptok
    ctx = steps * half_tok
    rows = n * ctx
    piece = total // (CORES * PIECES)
    lines = steps * keys
    tall = (lines + 31) // 32 * 32
    dims = (n, steps, keys, width, qry, ptok, emb, ffw, table, view_mask.shape[1])

    def low(*shape):
        return pltpu.VMEM(shape, BF16)

    def full(*shape):
        return pltpu.VMEM(shape, F32)

    small = (embodiment, ctx_steps, view_mask.T)
    scratch = [pltpu.SMEM(v.shape, v.dtype) for v in small]
    scratch += [low(*w.shape) for w in weights]
    scratch += [
        low(((n - 1) * lines + tall + 15) // 16 * 16, width),
        low(n, tall, width),
        low(n, steps, ptok, feats),
        low(n, ctx, width),
        low(emb, HEADS * qry, width),
        low(emb, width, HEADS * qry),
        low(emb, width, HEADS * qry),
        low(n, tall, width),
        low(n, steps, half_tok, width),
        low(n, width, tall),
        full(n, tall, HEADS * qry),
        low(n, tall, HEADS * qry),
        low(n, tall, (steps + 1) * width),
        low(n, width, (steps + 1) * width),
        low(n, width, steps * width),
        low(n, steps, qry, width),
        low(n * steps * ptok, width),
        full(n * steps * ptok, width),
        full(rows, width),
        full(rows, width),
        low(rows, width),
        low(rows, 3 * width),
        full(n, ctx, HEADS * ctx),
        low(n, ctx, HEADS * ctx),
        low(n, ctx, HEADS * ctx),
        low(rows, width),
        full(rows, width),
        full(rows, ffw),
        full(rows, width),
        full(rows, width),
        low(rows, width),
        low(rows, ffw),
        low(rows, width),
        low(rows, ffw),
        full(rows, width),
        low(rows, width),
        low(rows, width),
        low(rows, 3 * width),
        low(n, steps, half_tok, width),
        low(n, steps, qry, width),
        low(n, steps, half_tok, width),
        full(tall * n, width),
        low(n, steps, ptok, feats),
        full(emb, width, HEADS * qry),
        full(emb, width, width),
        low(CORES, PIECES, piece, width),
        pltpu.SemaphoreType.DMA((22,)),
    ]
    inputs = (*small, rows_of(images), proprio, out_grad, *weights)
    return pl.pallas_call(
        functools.partial(compute_kernel, dims),
        out_shape=(
            low(2, piece, width),
            low(2, piece, width),
            low(2, piece, width),
            low(2, piece, width),
            low(keys * n + n * half_tok + n * ptok, width),
            low(keys * n + n * half_tok + n * ptok, width),
        ),
        in_specs=[ANY] * 22,
        out_specs=(VMEM,) * 6,
        scratch_shapes=scratch,
        compiler_params=pltpu.CompilerParams(vmem_limit_bytes=40 * 2**20),
        name="stem_trunk",
    )(*(pltpu.with_memory_space_constraint(v, pltpu.HBM) for v in inputs))


def parity(index, levels):
    total = index & 1
    for level in range(1, levels):
        total = total ^ ((index >> level) & 1)
    return total


def own_half():
    levels = lax.axis_size("dp").bit_length() - 1
    return lax.axis_index("section") ^ parity(lax.axis_index("dp"), levels)


def own_bits(half):
    dp = lax.axis_index("dp")
    low, high = dp & 1, (dp >> 1) & 1
    return jnp.where(half == 0, low, high), jnp.where(half == 0, high, low)


def select(bit, low, high):
    return jnp.where(bit == 0, low, high)


def add(held, came):
    return (held.astype(F32) + came.astype(F32)).astype(BF16)


def swap_cores(value):
    return lax.ppermute(value, "section", [(0, 1), (1, 0)])


def swap_chips(value, bits):
    count = lax.axis_size("dp")
    levels = count.bit_length() - 1
    pairs = []
    for core in range(CORES):
        for i in range(count):
            bit = bits[core ^ parity(i, levels)]
            pairs.append((core * count + i, (1 - core) * count + (i ^ (1 << bit))))
    return lax.ppermute(value, ("section", "dp"), pairs)


def send_kernel(count, *refs):
    sem = refs[-1]
    copies = [pltpu.make_async_copy(refs[i], refs[count + i], sem.at[i]) for i in range(count)]
    for copy in copies:
        copy.start()
    for copy in copies:
        copy.wait()


def send_out(*values):
    return pl.pallas_call(
        functools.partial(send_kernel, len(values)),
        out_shape=tuple(jax.ShapeDtypeStruct(v.shape, v.dtype) for v in values),
        in_specs=[VMEM] * len(values),
        out_specs=(ANY,) * len(values),
        scratch_shapes=[pltpu.SemaphoreType.DMA((len(values),))],
        compiler_params=pltpu.CompilerParams(vmem_limit_bytes=8 * 2**20),
        name="send_out",
    )(*(pltpu.with_memory_space_constraint(v, pltpu.VMEM) for v in values))


def finish_kernel(table, *refs):
    pieces, refs = refs[: CORES * PIECES], refs[CORES * PIECES :]
    count = len(refs) // 2 - 1
    outs, held, (pack, sem) = refs[:count], refs[count : 2 * count], refs[2 * count :]
    size, width = pieces[0].shape
    own = own_half()
    for i, ref in enumerate(pieces):
        half = own if i < PIECES else 1 - own
        chain, far = i % CHAINS, i // CHAINS % 2
        at = half * PIECES + chain * 2 + (own_bits(half)[0] ^ far)
        pack[pl.ds(pl.multiple_of(at * size, size), size)] = ref[...]
    names = ("queries", "keyw", "valuew", "stem", "lift", "mixer", "again", "abias", "qkv", "aproj")
    names += ("mgain", "mbias", "up", "upb", "down", "downb")
    vectors = pack[pl.ds(table["vectors"][0], 16)].astype(F32)
    rows = {"again": 0, "abias": 1, "mgain": 2, "mbias": 3, "downb": 4}
    copies = []
    for i, (name, out, ref) in enumerate(zip(names, outs, held)):
        if name in rows:
            ref[...] = vectors[rows[name]]
        elif name == "upb":
            for j in range(ref.shape[0] // width):
                ref[width * j : width * (j + 1)] = vectors[5 + j]
        else:
            first, total = table[name]
            wide = ref.shape[-1] // width
            for j in range(wide):
                part = pack[first + total // wide * j : first + total // wide * (j + 1)].astype(F32)
                if ref.ndim == 3:
                    ref[...] = part.reshape(ref.shape)
                else:
                    ref[:, width * j : width * (j + 1)] = part
        copies.append(pltpu.make_async_copy(ref, out, sem.at[i]))
        copies[-1].start()
    for copy in copies:
        copy.wait()


def finish(table, pieces, shapes):
    total = len(pieces) * pieces[0].shape[0]
    return pl.pallas_call(
        functools.partial(finish_kernel, table),
        out_shape=tuple(jax.ShapeDtypeStruct(v, F32) for v in shapes),
        in_specs=[VMEM] * len(pieces),
        out_specs=(ANY,) * len(shapes),
        scratch_shapes=[pltpu.VMEM(v, F32) for v in shapes]
        + [pltpu.VMEM((total, pieces[0].shape[1]), BF16), pltpu.SemaphoreType.DMA((len(shapes),))],
        compiler_params=pltpu.CompilerParams(vmem_limit_bytes=24 * 2**20),
        name="finish",
    )(*(pltpu.with_memory_space_constraint(v, pltpu.VMEM) for v in pieces))


def sum_chips(held, came, extra):
    levels = lax.axis_size("dp").bit_length() - 1
    first, second = (0, 1), (1, 0)
    half = own_half()
    one, two = own_bits(half)
    totals = [add(a, b) for a, b in zip(held, came)]
    *totals[1:], extra = lax.optimization_barrier((*totals[1:], extra))
    for bit, bits in ((one, first), (two, second)):
        split = [t.reshape((2, -1, t.shape[-1])) for t in totals]
        sent = [swap_chips(select(bit, t[1], t[0]), bits) for t in split]
        totals = [add(select(bit, t[0], t[1]), c) for t, c in zip(split, sent)]
    extra = swap_cores(extra)
    for bits in zip(range(2, levels), reversed(range(2, levels))):
        sent = [swap_chips(t, bits) for t in totals]
        totals = [add(t, c) for t, c in zip(totals, sent)]
    sent = [swap_chips(t, second) for t in totals]
    near = [either(two, t, c) for t, c in zip(totals, sent)]
    far = [swap_chips(t, first) for t in near]
    return near + far + [swap_cores(t) for t in near + far], extra


def either(bit, mine, came, axis=0):
    return select(bit, jnp.concatenate([mine, came], axis), jnp.concatenate([came, mine], axis))


def per_device(*args):
    images, proprio, weights = args[0], args[1], args[5:21]
    emb, qry, width = weights[0].shape
    n, keys = images.shape[0] // CORES, images.shape[2]
    ptok, feats = proprio.shape[2:]
    table, total = layout(width, weights[12].shape[1], emb, qry, weights[4].shape[1])
    *packed, extra, extra_sent = compute(args, table, total)
    keep, send = packed[:CHAINS], packed[CHAINS:]
    pieces, came = sum_chips(keep, [swap_cores(v) for v in send], extra_sent)
    sec = lax.axis_index("section")
    first, second = keys * n, keys * n + n * (qry + ptok)
    img = either(sec, *(v[:first].reshape(keys, n, width) for v in (extra, came)), 1)
    blk = either(sec, *(v[first:second].reshape(n, -1, width) for v in (extra, came)))
    prp = either(sec, *(v[second:, :feats].reshape(n, ptok, feats) for v in (extra, came)))
    blk, img, prp = send_out(blk, img, prp)
    grads = finish(table, pieces, [w.shape for w in weights])
    return (blk, img.transpose(1, 0, 2)[:, None], prp[:, None]) + tuple(grads)


def solution(mesh):
    sample = [P("dp")] * 5
    return jax.shard_map(
        per_device,
        mesh=mesh,
        in_specs=tuple(sample + [P()] * 16 + [P("dp")]),
        out_specs=(P("dp", "section"),) * 3 + (P(),) * 16,
        check_vma=False,
    )
```

```python
import functools
import math

import jax
import jax.numpy as jnp
from jax import lax
from jax.experimental import pallas as pl
from jax.experimental.pallas import tpu as pltpu
from jax.sharding import PartitionSpec as P

HEADS = 8
F32 = jnp.float32
BF16 = jnp.bfloat16
CORES = 2
CHAINS = 2
PIECES = 2 * CHAINS
EPS = 1e-05
LAG = 8
INV_SQRT2 = 1.0 / math.sqrt(2.0)
INV_SQRT2PI = 1.0 / math.sqrt(2.0 * math.pi)
ANY = pl.BlockSpec(memory_space=pl.ANY)
VMEM = pl.BlockSpec(memory_space=pltpu.VMEM)
SMEM = pl.BlockSpec(memory_space=pltpu.SMEM)


def mm(left, right):
    return lax.dot_general(left, right, (((1,), (0,)), ((), ())), preferred_element_type=F32)


def mm_bt(left, right):
    return lax.dot_general(left, right, (((1,), (1,)), ((), ())), preferred_element_type=F32)


def mm_at(left, right):
    return lax.dot_general(left, right, (((0,), (0,)), ((), ())), preferred_element_type=F32)


def layout(width, ffw, emb, queries, feats):
    counts = (
        ("keyw", emb * width),
        ("valuew", emb * width),
        ("mixer", emb * width),
        ("stem", width),
        ("lift", emb * feats),
        ("queries", emb * queries),
        ("qkv", 3 * width),
        ("aproj", width),
        ("up", ffw),
        ("down", ffw),
        ("vectors", 16),
    )
    table, first = {}, 0
    for name, rows in counts:
        table[name] = (first, rows)
        first += rows
    step = CORES * PIECES * 32
    return table, (first + step - 1) // step * step


def cuts(first, rows, piece):
    done = 0
    while done < rows:
        at = first + done
        count = min(rows - done, piece - at % piece)
        yield at // piece, at % piece, done, count
        done += count


def head_mask(rows, per_head, width):
    row = lax.broadcasted_iota(jnp.int32, (rows, width), 0) // per_head
    col = lax.broadcasted_iota(jnp.int32, (rows, width), 1) // (width // HEADS)
    return (row == col).astype(F32)


def spread(rows, mask):
    return jnp.concatenate([rows] * HEADS, axis=0) * mask


def fold(full, mask):
    per = full.shape[0] // HEADS
    return jnp.sum((full * mask).reshape(HEADS, per, full.shape[1]), axis=0)


def gelu_parts(values):
    cdf = 0.5 * (1.0 + lax.erf(values * INV_SQRT2))
    pdf = INV_SQRT2PI * jnp.exp(-0.5 * values * values)
    return values * cdf, cdf + values * pdf


def staged(count, *stages):
    for step in range(count + LAG * (len(stages) - 1)):
        for lag, stage in enumerate(stages):
            if 0 <= step - LAG * lag < count:
                stage(step - LAG * lag)


def softmax_rows(scores):
    expo = jnp.exp(scores - jnp.max(scores, axis=0, keepdims=True))
    return expo * (1.0 / jnp.sum(expo, axis=0, keepdims=True))


def per_step(row, reduce):
    part = reduce(row.reshape(-1, 8, row.shape[1]), axis=0)
    pair = jnp.maximum if reduce is jnp.max else jnp.add
    part = pair(part, pltpu.roll(part, 4, 0))
    return pair(part, pltpu.roll(part, 2, 0))


def softmax_lines(scores):
    expo = jnp.exp(scores.reshape(-1, 8, scores.shape[1]) - per_step(scores, jnp.max))
    return (expo * (1.0 / per_step(expo.reshape(scores.shape), jnp.sum))).reshape(scores.shape)


def softmax_lines_grad(probs, grad):
    terms = probs * grad
    total = per_step(terms, jnp.sum)
    tiles = (-1, 8, probs.shape[1])
    return (terms.reshape(tiles) - probs.reshape(tiles) * total).reshape(probs.shape)


def softmax_rows_grad(probs, grad):
    terms = probs * grad
    return terms - probs * jnp.sum(terms, axis=0, keepdims=True)


def row_mean(values):
    width = values.shape[1]
    high = values.astype(BF16)
    low = (values - high.astype(F32)).astype(BF16)
    ones = jnp.full((2 * width, width), 1.0 / width, BF16)
    return mm(jnp.concatenate([high, low], axis=1), ones)


def norm_parts(values):
    center = values - row_mean(values)
    rstd = lax.rsqrt(row_mean(center * center) + EPS)
    return center * rstd, rstd


def norm_grad(grad, gain, hat, rstd):
    scaled = grad * gain
    first = row_mean(scaled)
    second = row_mean(scaled * hat)
    return rstd * (scaled - first - hat * second)


def compute_kernel(
    dims,
    emb_h,
    steps_h,
    views_h,
    images,
    proprio,
    out_grad,
    queries_h,
    key_h,
    value_h,
    stem_h,
    lift_h,
    mix_h,
    again_h,
    abias_h,
    qkv_h,
    aproj_h,
    mgain_h,
    mbias_h,
    up_h,
    up_bh,
    down_h,
    down_bh,
    keep0,
    keep1,
    send0,
    send1,
    extra_keep,
    extra_send,
    emb_ref,
    steps_ref,
    views_ref,
    queries,
    key_w,
    value_w,
    stem_proj,
    lift_w,
    mix_w,
    again,
    abias,
    qkv_w,
    aproj,
    mgain,
    mbias,
    up_w,
    up_b,
    down_w,
    down_b,
    xin_s,
    x_s,
    p_s,
    g_s,
    qs_s,
    qst_s,
    a_s,
    keys_s,
    vals_s,
    tok_s,
    xt_s,
    prob_s,
    sgrad_s,
    mix_s,
    ab_s,
    ut_s,
    satt_s,
    act_s,
    dact_s,
    hat1_s,
    rstd1_s,
    norm1_s,
    qkv_s,
    tprob_s,
    tlow_s,
    gprob_s,
    att_s,
    mid_s,
    pre_s,
    hat2_s,
    rstd2_s,
    norm2_s,
    up_s,
    glow_s,
    gpre_s,
    gn2_s,
    gmid_s,
    gatt_s,
    gqkv_s,
    gtok_s,
    gsatt_s,
    blk_s,
    img_s,
    prp_s,
    macc_s,
    vacc_s,
    pack_s,
    in_sem,
):
    n, steps, keys, width, qry, ptok, emb, ffw, table, views = dims
    half_tok = qry + ptok
    ctx = steps * half_tok
    rows = n * ctx
    scale = 1.0 / math.sqrt(width // HEADS)
    piece = pack_s.shape[2]
    scale_low = jnp.asarray(scale, BF16)
    sec = lax.axis_index("section")
    base = sec * n
    lines = steps * keys
    tall = x_s.shape[1]
    def put(name, row, value):
        first = table[name][0] + row
        for at, lo, done, count in cuts(first, value.shape[0], piece):
            pack_s[at // PIECES, at % PIECES, lo : lo + count] = value[done : done + count].astype(BF16)

    sources = (
        (emb_h, emb_ref),
        (queries_h, queries),
        (key_h, key_w),
        (images.at[pl.ds(pl.multiple_of(sec * n * lines, 16), n * lines)], xin_s.at[pl.ds(0, n * lines)]),
        (views_h, views_ref),
        (value_h, value_w),
        (proprio.at[pl.ds(base, n)], p_s),
        (lift_h, lift_w),
        (mix_h, mix_w),
        (stem_h, stem_proj),
        (again_h, again),
        (abias_h, abias),
        (qkv_h, qkv_w),
        (steps_h, steps_ref),
        (aproj_h, aproj),
        (mgain_h, mgain),
        (mbias_h, mbias),
        (up_h, up_w),
        (up_bh, up_b),
        (down_h, down_w),
        (down_bh, down_b),
        (out_grad.at[pl.ds(base, n)], g_s),
    )
    loads = [pltpu.make_async_copy(a, b, in_sem.at[i]) for i, (a, b) in enumerate(sources)]
    for copy in loads:
        copy.start()
    waited = [0]

    def ready(count):
        for copy in loads[waited[0] : count]:
            copy.wait()
        waited[0] = max(waited[0], count)

    smask = head_mask(HEADS * qry, qry, width)
    smask_low = smask.astype(BF16)
    tmask = head_mask(HEADS * ctx, ctx, width)
    tmask_low = tmask.astype(BF16)
    for e in range(emb):
        macc_s[e] = jnp.zeros((width, width), F32)
        vacc_s[e] = jnp.zeros((width, width), F32)
    used = max(first + count for first, count in table.values())
    for at, lo, _, count in cuts(used, CORES * PIECES * piece - used, piece):
        pack_s[at // PIECES, at % PIECES, lo : lo + count] = jnp.zeros((count, width), BF16)
    xin_s[n * lines :] = jnp.zeros((xin_s.shape[0] - n * lines, width), BF16)
    ready(3)
    embs = [emb_ref[base + s] for s in range(n)]
    for e in range(emb):
        qs = spread(queries[e], smask_low)
        qs_s[e] = qs
        qst_s[e] = (qs * scale_low).T
        a_s[e] = (mm_bt(key_w[e], qs) * scale).astype(BF16)

    ready(4)
    edge = lines // 16 * 16
    inside = lax.broadcasted_iota(jnp.int32, (tall - edge, width), 0) < lines - edge
    for s in range(n):
        x_s[s] = xin_s[lines * s : lines * s + tall]
        last = x_s[s, edge:].astype(F32)
        x_s[s, edge:] = jnp.where(inside, last, 0.0).astype(BF16)

    ready(9)
    emb_rows = jnp.concatenate([jnp.full((steps * ptok, width), e) for e in embs], axis=0)
    lift_cat = jnp.concatenate([lift_w[e] for e in range(emb)], axis=1)
    mix_cat = jnp.concatenate([mix_w[e] for e in range(emb)], axis=1)

    def own_columns(values):
        result = values[:, :width]
        for e in range(1, emb):
            result = jnp.where(emb_rows == e, values[:, width * e : width * (e + 1)], result)
        return result

    def spread_columns(values):
        parts = [jnp.where(emb_rows == e, values, 0.0).astype(BF16) for e in range(emb)]
        return jnp.concatenate(parts, axis=1)

    prop_rows = p_s[...].reshape(n * steps * ptok, -1)
    act, dact = gelu_parts(own_columns(mm(prop_rows, lift_cat)))
    act_s[...] = act.astype(BF16)
    dact_s[...] = dact
    prop_tok = own_columns(mm(act_s[...], mix_cat)).astype(BF16)
    tok_s[:, :, qry:] = prop_tok.reshape(n, steps, ptok, width)

    first_step = lax.broadcasted_iota(jnp.int32, (tall, width), 0) % steps == 0

    first_low = jnp.where(first_step, 1.0, 0.0).astype(BF16)

    def view_bias(s):
        lost = [jnp.where(views_ref[v, base + s] > 0, 0.0, -1e30).astype(F32) for v in range(views)]
        lost.append(jnp.float32(-1e30))
        ends = [lines // views * (v + 1) for v in range(views)]
        tiles, at = [], 0
        while at < tall:
            view = sum(at >= end for end in ends)
            stop = min([end // 8 * 8 for end in ends if end // 8 * 8 > at] + [tall])
            if view < views and ends[view] < at + 8:
                row = lax.broadcasted_iota(jnp.int32, (8, width), 0)
                tiles.append(jnp.where(row < ends[view] - at, lost[view], lost[view + 1]))
                at += 8
            else:
                tiles.append(jnp.full((stop - at, width), lost[view], F32))
                at = stop
        return jnp.concatenate(tiles, axis=0)

    def stem_keys(s):
        keys_s[s] = mm(x_s[s], key_w[embs[s]]).astype(BF16)

    def stem_scores(s):
        prob_s[s] = mm(keys_s[s], qst_s[embs[s]]) + view_bias(s)

    def stem_softmax(s):
        prob = softmax_lines(prob_s[s])
        prob_s[s] = prob
        prob_low = prob.astype(BF16)
        even = prob_low * first_low
        mix_s[s, :, :width] = even
        mix_s[s, :, width : 2 * width] = prob_low - even

    def stem_moments(s):
        turned = x_s[s].T
        xt_s[s] = turned
        ut_s[s] = mm(turned, mix_s[s, :, : 2 * width]).astype(BF16)

    def stem_turned(s):
        vals_s[s] = mm(x_s[s], value_w[embs[s]]).astype(BF16).T

    def stem_values(s):
        mixed = mm(vals_s[s], mix_s[s, :, : 2 * width]).astype(BF16).T.astype(F32)
        for t in range(steps):
            satt_s[s, t] = fold(mixed[width * t : width * (t + 1)], smask).astype(BF16)

    ready(6)
    staged(n, stem_keys, stem_scores, stem_turned, stem_softmax, stem_values, stem_moments)
    ready(10)
    image_tok = mm(satt_s[...].reshape(n * steps * qry, width), stem_proj[...])
    tok_s[:, :, :qry] = image_tok.astype(BF16).reshape(n, steps, qry, width)

    ready(len(loads))
    group = n
    chunk = group * ctx
    spans = [pl.ds(i * chunk, chunk) for i in range(rows // chunk)]
    again_row = again[...].astype(F32).reshape(1, width)
    abias_row = abias[...].astype(F32).reshape(1, width)
    mgain_row = mgain[...].astype(F32).reshape(1, width)
    mbias_row = mbias[...].astype(F32).reshape(1, width)
    upb_row = up_b[...].astype(F32).reshape(1, ffw)
    downb_row = down_b[...].astype(F32).reshape(1, width)

    def tokens_of(i):
        return tok_s[group * i : group * (i + 1)].reshape(chunk, width).astype(F32)

    for i, span in enumerate(spans):
        hat, rstd = norm_parts(tokens_of(i))
        hat1_s[span] = hat
        rstd1_s[span] = jnp.broadcast_to(rstd, hat.shape)
        norm1 = (hat * again_row + abias_row).astype(BF16)
        norm1_s[span] = norm1
        qkv_s[span] = mm(norm1, qkv_w[...]).astype(BF16)

    key_step = lax.broadcasted_iota(jnp.int32, (ctx, 1), 0) // half_tok
    def trunk_rows(s):
        mine = pl.ds(s * ctx, ctx)
        return (qkv_s[mine, width * j : width * (j + 1)] for j in range(3))

    def trunk_scores(s):
        query, key, _ = trunk_rows(s)
        dead = jnp.where(key_step < steps_ref[base + s], 0.0, -1e30).astype(F32)
        tprob_s[s] = mm_bt(key, spread(query * scale_low, tmask_low)) + dead

    def trunk_softmax(s):
        prob = softmax_rows(tprob_s[s])
        tprob_s[s] = prob
        tlow_s[s] = prob.astype(BF16)

    def trunk_values(s):
        _, _, value = trunk_rows(s)
        att_s[pl.ds(s * ctx, ctx)] = fold(mm_at(tlow_s[s], value), tmask).astype(BF16)

    staged(n, trunk_scores, trunk_softmax, trunk_values)

    row_step = lax.broadcasted_iota(jnp.int32, (ctx, 1), 0) // half_tok
    sums = {name: jnp.zeros((1, width), F32) for name in ("mgain", "mbias", "downb")}
    sums["upb"] = jnp.zeros((1, ffw), F32)

    def total(name, values):
        sums[name] += jnp.sum(values, axis=0, keepdims=True)

    def live_rows(i):
        parts = [row_step < steps_ref[base + group * i + j] for j in range(group)]
        return jnp.concatenate([jnp.where(part, 1.0, 0.0).astype(F32) for part in parts], axis=0)

    def mlp_in(i):
        span = spans[i]
        middle = tokens_of(i) + mm(att_s[span], aproj[...])
        mid_s[span] = middle
        hat, rstd = norm_parts(middle)
        hat2_s[span] = hat
        rstd2_s[span] = jnp.broadcast_to(rstd, hat.shape)
        norm2 = (hat * mgain_row + mbias_row).astype(BF16)
        norm2_s[span] = norm2
        pre_s[span] = mm(norm2, up_w[...]) + upb_row

    def mlp_gelu(i):
        span = spans[i]
        act, dact = gelu_parts(pre_s[span])
        up_s[span] = act.astype(BF16)
        pre_s[span] = dact

    def mlp_back(i):
        span = spans[i]
        grad = g_s[group * i : group * (i + 1)].reshape(chunk, width).astype(F32) * live_rows(i)
        grad_low = grad.astype(BF16)
        glow_s[span] = grad_low
        total("downb", grad)
        grad_up = mm_bt(grad_low, down_w[...]).astype(BF16).astype(F32)
        grad_pre = (grad_up * pre_s[span]).astype(BF16)
        gpre_s[span] = grad_pre
        total("upb", grad_pre.astype(F32))

    def mlp_norm_back(i):
        span = spans[i]
        grad_norm2 = mm_bt(gpre_s[span], up_w[...]).astype(BF16).astype(F32)
        hat = hat2_s[span]
        total("mgain", grad_norm2 * hat)
        total("mbias", grad_norm2)
        grad_mid = norm_grad(grad_norm2, mgain_row, hat, rstd2_s[span]) + glow_s[span].astype(F32)
        gn2_s[span] = grad_mid
        grad_mid_low = grad_mid.astype(BF16)
        gmid_s[span] = grad_mid_low
        gatt_s[span] = mm_bt(grad_mid_low, aproj[...]).astype(BF16)

    def mlp_out(i):
        span = spans[i]
        result = (mid_s[span] + mm(up_s[span], down_w[...]) + downb_row) * live_rows(i)
        blk_s[group * i : group * (i + 1)] = result.astype(BF16).reshape(group, steps, half_tok, width)

    staged(len(spans), mlp_in, mlp_gelu, mlp_back, mlp_norm_back, mlp_out)

    def trunk_back_probs(s):
        _, _, value = trunk_rows(s)
        grad_spread = spread(gatt_s[pl.ds(s * ctx, ctx)], tmask_low)
        gprob_s[s] = mm_bt(value, grad_spread).astype(BF16)
        gqkv_s[pl.ds(s * ctx, ctx), 2 * width :] = mm(tlow_s[s], grad_spread).astype(BF16)

    def trunk_back_softmax(s):
        grad_prob = gprob_s[s].astype(F32)
        tlow_s[s] = softmax_rows_grad(tprob_s[s], grad_prob).astype(BF16)

    def trunk_back_rows(s):
        query, key, _ = trunk_rows(s)
        mine = pl.ds(s * ctx, ctx)
        gqkv_s[mine, :width] = (fold(mm_at(tlow_s[s], key), tmask) * scale).astype(BF16)
        gqkv_s[mine, width : 2 * width] = (mm(tlow_s[s], spread(query, tmask_low)) * scale).astype(BF16)

    staged(n, trunk_back_probs, trunk_back_softmax, trunk_back_rows)

    again_sum = jnp.zeros((1, width), F32)
    abias_sum = jnp.zeros((1, width), F32)
    for i, span in enumerate(spans):
        grad_norm1 = mm_bt(gqkv_s[span], qkv_w[...]).astype(BF16).astype(F32)
        hat = hat1_s[span]
        again_sum += jnp.sum(grad_norm1 * hat, axis=0, keepdims=True)
        abias_sum += jnp.sum(grad_norm1, axis=0, keepdims=True)
        grad_tok = norm_grad(grad_norm1, again_row, hat, rstd1_s[span]) + gn2_s[span]
        gtok_s[group * i : group * (i + 1)] = grad_tok.astype(BF16).reshape(group, steps, half_tok, width)
    qkv = mm_at(norm1_s[...], gqkv_s[...])
    for j in range(3):
        put("qkv", width * j, qkv[:, width * j : width * (j + 1)])
    vectors = [again_sum, abias_sum, sums["mgain"], sums["mbias"], sums["downb"]]
    vectors += [sums["upb"][:, width * j : width * (j + 1)] for j in range(ffw // width)]
    vectors += [jnp.zeros((16 - len(vectors), width), F32)]
    put("vectors", 0, jnp.concatenate(vectors, axis=0))

    put("aproj", 0, mm_at(att_s[...], gmid_s[...]))
    down = mm_at(glow_s[...], up_s[...]).astype(BF16)
    up = mm_at(norm2_s[...], gpre_s[...])
    for j in range(ffw // width):
        cols = slice(width * j, width * (j + 1))
        put("down", width * j, down[:, cols].T)
        put("up", width * j, up[:, cols])

    grad_prop = spread_columns(gtok_s[:, :, qry:].reshape(n * steps * ptok, width).astype(F32))
    mixer = mm_at(act_s[...], grad_prop)
    grad_act = mm_bt(grad_prop, mix_cat).astype(BF16).astype(F32)
    grad_lift = spread_columns((grad_act * dact_s[...]).astype(BF16).astype(F32))
    lift = mm_at(prop_rows, grad_lift)
    for e in range(emb):
        put("mixer", width * e, mixer[:, width * e : width * (e + 1)])
        put("lift", lift.shape[0] * e, lift[:, width * e : width * (e + 1)])
    prp_s[...] = mm_bt(grad_lift, lift_cat).astype(BF16).reshape(n, steps, ptok, -1)

    grad_img = gtok_s[:, :, :qry].reshape(n * steps * qry, width)
    put("stem", 0, mm_at(satt_s[...].reshape(n * steps * qry, width), grad_img))
    gsatt_s[...] = mm_bt(grad_img, stem_proj[...]).astype(BF16).reshape(n, steps, qry, width)

    def stem_back_values(s):
        spreads = [spread(gsatt_s[s, t], smask_low) for t in range(steps)]
        grad_spread = jnp.concatenate(spreads, axis=0)
        ab_s[s, :, : 2 * width] = mm_bt(value_w[embs[s]], grad_spread).astype(BF16)
        ab_s[s, :, 2 * width :] = a_s[embs[s]]
        vacc_s[embs[s]] += mm(ut_s[s], grad_spread)

    def stem_back_probs(s):
        both = mm(x_s[s], ab_s[s, :, : 2 * width])
        sgrad_s[s] = jnp.where(first_step, both[:, :width], both[:, width:]).astype(BF16)

    def stem_back_softmax(s):
        grad_prob = sgrad_s[s].astype(F32)
        mix_s[s, :, 2 * width :] = softmax_lines_grad(prob_s[s], grad_prob).astype(BF16)

    def stem_back_moments(s):
        macc_s[embs[s]] += mm(xt_s[s], mix_s[s, :, 2 * width :])

    def image_gradient(s):
        img_s[pl.ds(s, tall, stride=n)] = mm_bt(mix_s[s], ab_s[s])

    staged(n, stem_back_values, stem_back_probs, stem_back_softmax, stem_back_moments, image_gradient)

    for e in range(emb):
        moment = (macc_s[e] * scale).astype(BF16)
        put("keyw", width * e, mm(moment, qs_s[e]))
        put("queries", qry * e, fold(mm_at(moment, key_w[e]), smask))
        put("valuew", width * e, vacc_s[e])
    other = 1 - sec
    half = own_half()
    image = img_s.reshape(tall // steps, steps, n, width)
    first, second = keys * n, keys * n + n * half_tok
    for ref, at in ((extra_keep, sec), (extra_send, other)):
        ref[:first] = image[:keys, at].reshape(first, width).astype(BF16)
        ref[first:second] = blk_s[:, at].reshape(second - first, width)
        ref[second:, : prp_s.shape[3]] = prp_s[:, at].reshape(n * ptok, -1)
        ref[second:, prp_s.shape[3] :] = jnp.zeros((n * ptok, width - prp_s.shape[3]), BF16)
    for ref, at, chain in ((keep0, half, 0), (keep1, half, 1), (send0, 1 - half, 0), (send1, 1 - half, 1)):
        ref[...] = pack_s[at, 2 * chain : 2 * chain + 2]


def rows_of(images):
    return images.transpose(0, 2, 1, 3).reshape(-1, images.shape[-1])


def compute(args, table, total):
    images, proprio, view_mask, embodiment, ctx_steps = args[:5]
    weights, out_grad = args[5:21], args[21]
    samples, steps, keys, width = images.shape
    ptok, feats = proprio.shape[2:]
    emb, qry = weights[0].shape[:2]
    ffw = weights[12].shape[1]
    n = samples // CORES
    half_tok = qry + ptok
    ctx = steps * half_tok
    rows = n * ctx
    piece = total // (CORES * PIECES)
    lines = steps * keys
    tall = (lines + 31) // 32 * 32
    dims = (n, steps, keys, width, qry, ptok, emb, ffw, table, view_mask.shape[1])

    def low(*shape):
        return pltpu.VMEM(shape, BF16)

    def full(*shape):
        return pltpu.VMEM(shape, F32)

    small = (embodiment, ctx_steps, view_mask.T)
    scratch = [pltpu.SMEM(v.shape, v.dtype) for v in small]
    scratch += [low(*w.shape) for w in weights]
    scratch += [
        low(((n - 1) * lines + tall + 15) // 16 * 16, width),
        low(n, tall, width),
        low(n, steps, ptok, feats),
        low(n, ctx, width),
        low(emb, HEADS * qry, width),
        low(emb, width, HEADS * qry),
        low(emb, width, HEADS * qry),
        low(n, tall, width),
        low(n, width, tall),
        low(n, steps, half_tok, width),
        low(n, width, tall),
        full(n, tall, HEADS * qry),
        low(n, tall, HEADS * qry),
        low(n, tall, (steps + 1) * width),
        low(n, width, (steps + 1) * width),
        low(n, width, steps * width),
        low(n, steps, qry, width),
        low(n * steps * ptok, width),
        full(n * steps * ptok, width),
        full(rows, width),
        full(rows, width),
        low(rows, width),
        low(rows, 3 * width),
        full(n, ctx, HEADS * ctx),
        low(n, ctx, HEADS * ctx),
        low(n, ctx, HEADS * ctx),
        low(rows, width),
        full(rows, width),
        full(rows, ffw),
        full(rows, width),
        full(rows, width),
        low(rows, width),
        low(rows, ffw),
        low(rows, width),
        low(rows, ffw),
        full(rows, width),
        low(rows, width),
        low(rows, width),
        low(rows, 3 * width),
        low(n, steps, half_tok, width),
        low(n, steps, qry, width),
        low(n, steps, half_tok, width),
        full(tall * n, width),
        low(n, steps, ptok, feats),
        full(emb, width, HEADS * qry),
        full(emb, width, width),
        low(CORES, PIECES, piece, width),
        pltpu.SemaphoreType.DMA((22,)),
    ]
    inputs = (*small, rows_of(images), proprio, out_grad, *weights)
    return pl.pallas_call(
        functools.partial(compute_kernel, dims),
        out_shape=(
            low(2, piece, width),
            low(2, piece, width),
            low(2, piece, width),
            low(2, piece, width),
            low(keys * n + n * half_tok + n * ptok, width),
            low(keys * n + n * half_tok + n * ptok, width),
        ),
        in_specs=[ANY] * 22,
        out_specs=(VMEM,) * 6,
        scratch_shapes=scratch,
        compiler_params=pltpu.CompilerParams(vmem_limit_bytes=40 * 2**20),
        name="stem_trunk",
    )(*(pltpu.with_memory_space_constraint(v, pltpu.HBM) for v in inputs))


def parity(index, levels):
    total = index & 1
    for level in range(1, levels):
        total = total ^ ((index >> level) & 1)
    return total


def own_half():
    levels = lax.axis_size("dp").bit_length() - 1
    return lax.axis_index("section") ^ parity(lax.axis_index("dp"), levels)


def own_bits(half):
    dp = lax.axis_index("dp")
    low, high = dp & 1, (dp >> 1) & 1
    return jnp.where(half == 0, low, high), jnp.where(half == 0, high, low)


def select(bit, low, high):
    return jnp.where(bit == 0, low, high)


def add(held, came):
    return (held.astype(F32) + came.astype(F32)).astype(BF16)


def swap_cores(value):
    return lax.ppermute(value, "section", [(0, 1), (1, 0)])


def swap_chips(value, bits):
    count = lax.axis_size("dp")
    levels = count.bit_length() - 1
    pairs = []
    for core in range(CORES):
        for i in range(count):
            bit = bits[core ^ parity(i, levels)]
            pairs.append((core * count + i, (1 - core) * count + (i ^ (1 << bit))))
    return lax.ppermute(value, ("section", "dp"), pairs)


def send_kernel(count, *refs):
    sem = refs[-1]
    copies = [pltpu.make_async_copy(refs[i], refs[count + i], sem.at[i]) for i in range(count)]
    for copy in copies:
        copy.start()
    for copy in copies:
        copy.wait()


def send_out(*values):
    return pl.pallas_call(
        functools.partial(send_kernel, len(values)),
        out_shape=tuple(jax.ShapeDtypeStruct(v.shape, v.dtype) for v in values),
        in_specs=[VMEM] * len(values),
        out_specs=(ANY,) * len(values),
        scratch_shapes=[pltpu.SemaphoreType.DMA((len(values),))],
        compiler_params=pltpu.CompilerParams(vmem_limit_bytes=8 * 2**20),
        name="send_out",
    )(*(pltpu.with_memory_space_constraint(v, pltpu.VMEM) for v in values))


def finish_kernel(table, *refs):
    pieces, refs = refs[: CORES * PIECES], refs[CORES * PIECES :]
    count = len(refs) // 2 - 1
    outs, held, (pack, sem) = refs[:count], refs[count : 2 * count], refs[2 * count :]
    size, width = pieces[0].shape
    own = own_half()
    for i, ref in enumerate(pieces):
        half = own if i < PIECES else 1 - own
        chain, far = i % CHAINS, i // CHAINS % 2
        at = half * PIECES + chain * 2 + (own_bits(half)[0] ^ far)
        pack[pl.ds(pl.multiple_of(at * size, size), size)] = ref[...]
    names = ("queries", "keyw", "valuew", "stem", "lift", "mixer", "again", "abias", "qkv", "aproj")
    names += ("mgain", "mbias", "up", "upb", "down", "downb")
    vectors = pack[pl.ds(table["vectors"][0], 16)].astype(F32)
    rows = {"again": 0, "abias": 1, "mgain": 2, "mbias": 3, "downb": 4}
    copies = []
    for i, (name, out, ref) in enumerate(zip(names, outs, held)):
        if name in rows:
            ref[...] = vectors[rows[name]]
        elif name == "upb":
            for j in range(ref.shape[0] // width):
                ref[width * j : width * (j + 1)] = vectors[5 + j]
        else:
            first, total = table[name]
            wide = ref.shape[-1] // width
            for j in range(wide):
                part = pack[first + total // wide * j : first + total // wide * (j + 1)].astype(F32)
                if ref.ndim == 3:
                    ref[...] = part.reshape(ref.shape)
                else:
                    ref[:, width * j : width * (j + 1)] = part
        copies.append(pltpu.make_async_copy(ref, out, sem.at[i]))
        copies[-1].start()
    for copy in copies:
        copy.wait()


def finish(table, pieces, shapes):
    total = len(pieces) * pieces[0].shape[0]
    return pl.pallas_call(
        functools.partial(finish_kernel, table),
        out_shape=tuple(jax.ShapeDtypeStruct(v, F32) for v in shapes),
        in_specs=[VMEM] * len(pieces),
        out_specs=(ANY,) * len(shapes),
        scratch_shapes=[pltpu.VMEM(v, F32) for v in shapes]
        + [pltpu.VMEM((total, pieces[0].shape[1]), BF16), pltpu.SemaphoreType.DMA((len(shapes),))],
        compiler_params=pltpu.CompilerParams(vmem_limit_bytes=24 * 2**20),
        name="finish",
    )(*(pltpu.with_memory_space_constraint(v, pltpu.VMEM) for v in pieces))


def sum_chips(held, came, extra):
    levels = lax.axis_size("dp").bit_length() - 1
    first, second = (0, 1), (1, 0)
    half = own_half()
    one, two = own_bits(half)
    totals = [add(a, b) for a, b in zip(held, came)]
    *totals[1:], extra = lax.optimization_barrier((*totals[1:], extra))
    for bit, bits in ((one, first), (two, second)):
        split = [t.reshape((2, -1, t.shape[-1])) for t in totals]
        sent = [swap_chips(select(bit, t[1], t[0]), bits) for t in split]
        totals = [add(select(bit, t[0], t[1]), c) for t, c in zip(split, sent)]
    extra = swap_cores(extra)
    for bits in zip(range(2, levels), reversed(range(2, levels))):
        sent = [swap_chips(t, bits) for t in totals]
        totals = [add(t, c) for t, c in zip(totals, sent)]
    sent = [swap_chips(t, second) for t in totals]
    near = [either(two, t, c) for t, c in zip(totals, sent)]
    far = [swap_chips(t, first) for t in near]
    return near + far + [swap_cores(t) for t in near + far], extra


def either(bit, mine, came, axis=0):
    return select(bit, jnp.concatenate([mine, came], axis), jnp.concatenate([came, mine], axis))


def per_device(*args):
    images, proprio, weights = args[0], args[1], args[5:21]
    emb, qry, width = weights[0].shape
    n, keys = images.shape[0] // CORES, images.shape[2]
    ptok, feats = proprio.shape[2:]
    table, total = layout(width, weights[12].shape[1], emb, qry, weights[4].shape[1])
    *packed, extra, extra_sent = compute(args, table, total)
    keep, send = packed[:CHAINS], packed[CHAINS:]
    pieces, came = sum_chips(keep, [swap_cores(v) for v in send], extra_sent)
    sec = lax.axis_index("section")
    first, second = keys * n, keys * n + n * (qry + ptok)
    img = either(sec, *(v[:first].reshape(keys, n, width) for v in (extra, came)), 1)
    blk = either(sec, *(v[first:second].reshape(n, -1, width) for v in (extra, came)))
    prp = either(sec, *(v[second:, :feats].reshape(n, ptok, feats) for v in (extra, came)))
    blk, img, prp = send_out(blk, img, prp)
    grads = finish(table, pieces, [w.shape for w in weights])
    return (blk, img.transpose(1, 0, 2)[:, None], prp[:, None]) + tuple(grads)


def solution(mesh):
    sample = [P("dp")] * 5
    return jax.shard_map(
        per_device,
        mesh=mesh,
        in_specs=tuple(sample + [P()] * 16 + [P("dp")]),
        out_specs=(P("dp", "section"),) * 3 + (P(),) * 16,
        check_vma=False,
    )
```
